128 devices in a mesh: gx: 16 (over x, z), gy: 8 (over y, core).
Axes of the slice: x: 4, y: 4, z: 4, core: 2. Of those that a mesh axis runs over, the one named last changes fastest.
Arguments:
- density: bfloat16 [393216, 128], P(('gx', 'gy')), may hold values from -6 to 6
- send_order: int32 [128, 3072], P(('gx', 'gy')), may hold values from 0 to 3071, each once within a row
- recv_order: int32 [128, 3072], P(('gx', 'gy')), may hold values from 0 to 3071, each once within a row
- geometry: float32 [4, 393216], P(None, ('gx', 'gy')), may hold values from -8 to 8, as said below
- pair_leaf: int32 [128, 3072], P(('gx', 'gy')), may hold values from 0 to 31, as said below
- near_list: int32 [4096, 12], P(('gx', 'gy')), may hold values from 0 to 95
- far_list: int32 [4096, 16], P(('gx', 'gy')), may hold values from 0 to 4095, as said below
- far_offset: int32 [4096, 16], P(('gx', 'gy')), may hold values from 0 to 15
- moment_table: bfloat16 [128, 121], replicated, may hold values from -0.25 to 0.25
- coulomb_block: bfloat16 [128, 128], replicated, may hold values from -0.5 to 0.5
- translation: float32 [16, 121, 121], replicated, may hold values from -0.125 to 0.125
Outputs:
- coulomb: float32 [393216, 128], P(('gx', 'gy'))
The draws below stay inside these ranges and needn't reach their ends.
Inputs may be any that keep to these rules, and one draw needn't show every extreme that they name: `send_order`: each row is a permutation of 0 .. 3071. `recv_order`: each row is a permutation of 0 .. 3071. `pair_leaf`: each row never falls and names every leaf 0 .. 31 at least once. `geometry`: row 3 lies between 0.5 and 2. `far_list`: the entries of a leaf of device d name leaves of devices d - 1, d and d + 1 (those that exist).
All inputs are finite; a program needn't handle non-finite values.
Results may differ from the reference program's by a relative error of at most 0.0038.
Values may be sent and summed in bfloat16 or wider, within the bound.
A program may use at most 64 MiB of HBM per device.

```python
import math
import jax
import jax.numpy as jnp
from jax import lax

PB = 128
NM = 121
NOFF = 16
NEAR = 12
NFAR = 16
PAIR_DEV = 3072
LEAF_DEV = 32
PAIRS = 393216
LEAVES = 4096
N_GX = 16
N_GY = 8
DEVICES = 128


def draw_geometry(key, part):
    key = jax.random.fold_in(key, 5)
    key_center, key_extent = jax.random.split(key)
    centers = 3.0 * jnp.clip(jax.random.normal(key_center, (3, PAIRS), jnp.float32), -2.6, 2.6)
    extent = jnp.exp(jax.random.uniform(key_extent, (1, PAIRS), jnp.float32, math.log(0.5), math.log(2.0)))
    return jnp.concatenate([centers, extent], axis=0)


def draw_pair_leaf(key, part):
    key = jax.random.fold_in(key, 11)
    keys = jax.random.split(key, DEVICES)
    slots = jnp.arange(PAIR_DEV, dtype=jnp.int32)

    def one_row(row_key):
        cuts = jax.random.permutation(row_key, PAIR_DEV - 1)[:LEAF_DEV - 1] + 1
        return jnp.sum((slots[:, None] >= cuts[None, :]).astype(jnp.int32), axis=1).astype(jnp.int32)
    return jax.vmap(one_row)(keys)


def draw_far_list(key, part):
    key = jax.random.fold_in(key, 17)
    owner = jnp.arange(LEAVES, dtype=jnp.int32) // LEAF_DEV
    lowest = jnp.maximum(owner - 1, 0) * LEAF_DEV
    highest = (jnp.minimum(owner + 1, DEVICES - 1) + 1) * LEAF_DEV
    return jax.random.randint(key, (LEAVES, NFAR), lowest[:, None], highest[:, None], dtype=jnp.int32)


def plant(array, key, low, largest):
    dims = array.shape
    place = [jax.random.randint(jax.random.fold_in(key, axis), (), 0, dims[axis]) for axis in range(len(dims))]
    array = array.at[tuple(place)].set(low)
    longest = dims.index(max(dims))
    place[longest] = (place[longest] + 1) % dims[longest]
    return array.at[tuple(place)].set(largest)


def shard_levels(own_key, dims, cuts, least, high):
    gain, own = 1.0, jax.random.fold_in(own_key, 6)
    for axis_at, parts in cuts:
        heights = jnp.exp(jax.random.uniform(jax.random.fold_in(own, axis_at), (parts,), jnp.float32, least / len(cuts), high / len(cuts)))
        gain = gain * jnp.repeat(heights, dims[axis_at] // parts).reshape([-1 if axis == axis_at else 1 for axis in range(len(dims))])
    return gain


def scatter_about(rng, shape, scale, most, cuts=(), kind=jnp.bfloat16):
    factor_of = shard_levels(rng, shape, cuts, -0.22, 0.18) if cuts else 1.0
    entries = jax.random.normal(rng, shape, jnp.float32) * scale * factor_of
    return jnp.minimum(jnp.maximum(entries, -most), most).astype(kind)


def setup_inputs(seed: int = 0) -> dict:
    splits = jax.random.split(jax.random.key(seed), 12)
    return {
        "density": scatter_about(splits[0], (PAIRS, PB), 1.0, 6.0, ((0, 128),)),
        "send_order": jax.vmap(lambda own: jax.random.permutation(own, PAIR_DEV))(jax.random.split(splits[1], (N_GX * N_GY))).reshape((N_GX * N_GY, PAIR_DEV)).astype(jnp.int32),
        "recv_order": jax.vmap(lambda own: jax.random.permutation(own, PAIR_DEV))(jax.random.split(splits[2], (N_GX * N_GY))).reshape((N_GX * N_GY, PAIR_DEV)).astype(jnp.int32),
        "geometry": draw_geometry(jax.random.fold_in(splits[11], 71), 0),
        "pair_leaf": draw_pair_leaf(jax.random.fold_in(splits[11], 71), 0),
        "near_list": plant(jax.random.randint(splits[5], (LEAVES, NEAR), 0, 3 * LEAF_DEV), jax.random.fold_in(splits[5], 1), 0, (3 * LEAF_DEV) - 1).astype(jnp.int32),
        "far_list": draw_far_list(jax.random.fold_in(splits[11], 71), 0),
        "far_offset": plant(jax.random.randint(splits[7], (LEAVES, NFAR), 0, NOFF), jax.random.fold_in(splits[7], 1), 0, NOFF - 1).astype(jnp.int32),
        "moment_table": scatter_about(splits[8], (PB, NM), (4 * PB) ** -0.5, 0.25),
        "coulomb_block": scatter_about(splits[9], (PB, PB), PB ** -0.5, 0.5),
        "translation": scatter_about(splits[10], (NOFF, NM, NM), (NM * NFAR) ** -0.5, 0.125, (), jnp.float32),
    }


def near_block(own, row_mask, window_geo, window_leaf, window_dens):
    mask = jnp.take(row_mask, window_leaf, axis=1)
    dist = (own[0][:, None] - window_geo[0][None, :]) ** 2
    dist = dist + (own[1][:, None] - window_geo[1][None, :]) ** 2
    dist = dist + (own[2][:, None] - window_geo[2][None, :]) ** 2
    kernel = mask * lax.rsqrt(dist + own[3][:, None] + window_geo[3][None, :])
    weights = kernel.astype(jnp.bfloat16)
    return jnp.dot(weights, window_dens, preferred_element_type=jnp.float32).astype(jnp.bfloat16)

def reference(density, send_order, recv_order, geometry, pair_leaf, near_list, far_list, far_offset, moment_table, coulomb_block, translation):
    devices = N_GX * N_GY
    quota = PAIR_DEV // devices
    highest = lax.Precision.HIGHEST
    blocks = density.reshape(devices, PAIR_DEV, PB)
    outgoing = jnp.take_along_axis(blocks, send_order[:, :, None], axis=1)
    moved = outgoing.reshape(devices, devices, quota, PB).transpose(1, 0, 2, 3).reshape(devices, PAIR_DEV, PB)
    leaf_density = jnp.take_along_axis(moved, recv_order[:, :, None], axis=1)
    leaf_hot = (pair_leaf[:, None, :] == jnp.arange(LEAF_DEV, dtype=jnp.int32)[None, :, None]).astype(jnp.float32)
    moments = moment_table.astype(jnp.float32)
    pair_multipoles = jnp.einsum('dpk,km->dpm', leaf_density.astype(jnp.float32), moments, precision=highest)
    multipoles = jnp.einsum('dlp,dpm->dlm', leaf_hot, pair_multipoles, precision=highest).reshape(LEAVES, NM)
    sources = jnp.take(multipoles, far_list.reshape(-1), axis=0).reshape(LEAVES, NFAR, NM)
    offset_hot = (far_offset[:, :, None] == jnp.arange(NOFF, dtype=jnp.int32)[None, None, :]).astype(jnp.float32)
    grouped = jnp.einsum('ljo,ljm->olm', offset_hot, sources, precision=highest)
    local_expansions = jnp.einsum('olm,onm->ln', grouped, translation, precision=highest).reshape(devices, LEAF_DEV, NM)
    pair_expansions = jnp.einsum('dlp,dlm->dpm', leaf_hot, local_expansions, precision=highest)
    far_coulomb = jnp.einsum('dpm,km->dpk', pair_expansions, moments, precision=highest)
    zero_dens = jnp.zeros((1, PAIR_DEV, PB), leaf_density.dtype)
    dens_pad = jnp.concatenate([zero_dens, leaf_density, zero_dens], axis=0)
    geo = geometry.reshape(4, devices, PAIR_DEV).transpose(1, 0, 2)
    stacked = jnp.concatenate([geo, pair_leaf[:, None, :].astype(jnp.float32)], axis=1)
    zero_geo = jnp.zeros((1, 5, PAIR_DEV), jnp.float32)
    geo_pad = jnp.concatenate([zero_geo, stacked, zero_geo], axis=0)
    window_ids = jnp.arange(3 * LEAF_DEV, dtype=jnp.int32)
    adjacency = lax.optimization_barrier(jnp.max((near_list.reshape(devices, LEAF_DEV, NEAR)[:, :, :, None] == window_ids).astype(jnp.float32), axis=2))
    rows = min(512, PAIR_DEV)
    count = PAIR_DEV // rows
    shard_of = jnp.arange(3 * PAIR_DEV, dtype=jnp.int32) // PAIR_DEV

    def near_one(index):
        window_dens = lax.dynamic_slice_in_dim(dens_pad, index, 3, 0).reshape(3 * PAIR_DEV, PB)
        window_geo = lax.dynamic_slice_in_dim(geo_pad, index, 3, 0).transpose(1, 0, 2).reshape(5, 3 * PAIR_DEV)
        window_leaf = window_geo[4].astype(jnp.int32) + LEAF_DEV * shard_of
        own = stacked[index]
        row_mask = jnp.take(adjacency[index], pair_leaf[index], axis=0)
        own_blocks = own.reshape(5, count, rows).transpose(1, 0, 2)
        mask_blocks = row_mask.reshape(count, rows, 3 * LEAF_DEV)
        potential = lax.map(lambda item: near_block(item[0], item[1], window_geo, window_leaf, window_dens), (own_blocks, mask_blocks))
        return jnp.dot(potential.reshape(PAIR_DEV, PB), coulomb_block, preferred_element_type=jnp.float32)
    near_coulomb = lax.map(near_one, jnp.arange(devices, dtype=jnp.int32))
    total = near_coulomb + far_coulomb
    device_ids = jnp.arange(devices, dtype=jnp.int32)[:, None]
    back = jnp.zeros_like(total).at[device_ids, recv_order].set(total)
    returned = back.reshape(devices, devices, quota, PB).transpose(1, 0, 2, 3).reshape(devices, PAIR_DEV, PB)
    coulomb = jnp.zeros_like(returned).at[device_ids, send_order].set(returned)
    return coulomb.reshape(PAIRS, PB)
```

```python
import functools

import jax
import jax.numpy as jnp
import numpy as np
from jax import lax
from jax.experimental import pallas as pl
from jax.experimental.pallas import tpu as pltpu
from jax.sharding import PartitionSpec as P

MESH = pl.DeviceIdType.MESH
F32, BF16 = jnp.float32, jnp.bfloat16
FAR_AWAY = 1e30
ROWS = 3072
WIDTH = 128
HALF = ROWS // 2
DEVS, CHIPS = 128, 64
QUOTA = 24
PACK = 2 * QUOTA
LEAVES = 32
HOT = 24
OWN = HOT + LEAVES
CHUNK = 32
CHUNKS = 3 * ROWS // CHUNK
BLOCK = 128
BLOCKS = ROWS // BLOCK
STEP = 32
LIST = 384
WINDOW = 3 * ROWS + CHUNK
VMEM = 56 * 1024 * 1024


def selections():
    own, other = np.zeros((128, 128), np.float32), np.zeros((128, 128), np.float32)
    for axis in range(3):
        for at, (a, b) in enumerate(((0, 0), (0, 8), (8, 0), (0, 16), (16, 0), (8, 8))):
            own[a + axis, 6 * axis + at] = 1.0
            other[b + axis, 6 * axis + at] = -2.0
    for at in range(3):
        own[8 * at + 3, 18 + at] = 1.0
        other[4, 18 + at] = 1.0
        own[4, 21 + at] = 1.0
        other[8 * at + 3, 21 + at] = 1.0
    own[4, 120] = FAR_AWAY
    for at in range(HOT, HOT + 3 * LEAVES):
        other[at, at] = 1.0
    return own, other


def iota(shape, axis):
    return lax.broadcasted_iota(jnp.int32, shape, axis)


def fiota(shape, axis):
    return iota(shape, axis).astype(F32)


def hot(condition):
    return jnp.where(condition, 1.0, 0.0).astype(BF16)


def times(a, b, dims=((1,), (0,))):
    return lax.dot_general(a, b, (dims, ((), ())), preferred_element_type=F32)


def parts(x):
    high = x.astype(BF16)
    rest = x - high.astype(F32)
    middle = rest.astype(BF16)
    low = (rest - middle.astype(F32)).astype(BF16)
    return high, middle, low


def remote(src, dst, send, recv, device):
    return pltpu.make_async_remote_copy(
        src_ref=src,
        dst_ref=dst,
        send_sem=send,
        recv_sem=recv,
        device_id=device,
        device_id_type=MESH,
    )


def place():
    gx, gy = lax.axis_index("gx"), lax.axis_index("gy")
    me = gx * 8 + gy
    return me, me // 2, gy % 2


def device_of(d):
    return (d // 8, d % 8)


def of_chip(chip, core):
    return (chip // 4, (chip % 4) * 2 + core)


def rows_at(start, count, step):
    return pl.ds(pl.multiple_of(start, step), count)


def to_columns(row_of, col_ref):
    def block(b, carry):
        at = rows_at(b * 128, 128, 128)
        col_ref[at, :] = jnp.broadcast_to(row_of(at), (128, 128)).T
        return carry

    lax.fori_loop(0, ROWS // 128, block, 0)


def side_by_side(x_ref, x2_ref):
    x2_ref[:, :WIDTH] = x_ref[:HALF]
    x2_ref[:, WIDTH:] = x_ref[HALF:]


def taken(idx, x2_ref):
    upper = idx >= HALF
    low = jnp.where(upper, idx - HALF, idx)
    lane = fiota(idx.shape, 1)
    pick = jnp.concatenate([hot(low == lane + 128.0 * b) for b in range(HALF // 128)], axis=1)
    both = times(pick, x2_ref[...])
    return jnp.where(upper, both[:, WIDTH:], both[:, :WIDTH])


def split_by_target(x_ref, col_ref, x2_ref):
    def block(b, carry):
        at = rows_at(b * 256, 256, 256)
        x = x_ref[at, :].astype(F32)
        upper = col_ref[at, :] >= HALF
        x2_ref[at, :WIDTH] = jnp.where(upper, 0.0, x).astype(BF16)
        x2_ref[at, WIDTH:] = jnp.where(upper, x, 0.0).astype(BF16)
        return carry

    lax.fori_loop(0, ROWS // 256, block, 0)


def wait_all(my, send_ref, land_ref, send_sem, recv_sem, device):
    got = pl.ds(0, PACK * (CHIPS - 1))
    copy = remote(send_ref.at[got], land_ref.at[got], send_sem, recv_sem, device)
    copy.wait_recv()
    copy.wait_send()


def send_packs(group, my, core, send_ref, land_ref, send_sem, recv_sem):
    for j in range(8):
        chip = 8 * group + (my + j) % 8

        @pl.when(chip != my)
        def _():
            remote(
                send_ref.at[rows_at(PACK * chip, PACK, 16)],
                land_ref.at[rows_at(PACK * my, PACK, 16)],
                send_sem,
                recv_sem,
                of_chip(chip, core),
            ).start()


def greet(my, core, others):
    barrier = pltpu.get_barrier_semaphore()

    def one(o, carry):
        pl.semaphore_signal(
            barrier, inc=1, device_id=of_chip((my + o) % CHIPS, core), device_id_type=MESH
        )
        return carry

    lax.fori_loop(1, CHIPS, one, 0)
    for other in others:
        pl.semaphore_signal(barrier, inc=1, device_id=device_of(other), device_id_type=MESH)
    pl.semaphore_wait(barrier, CHIPS - 1 + len(others))


def features(slot, info_ref, own_sel, other_sel, member, own_ref, other_ref, chunk_ref):
    def two_blocks(at_two, carry):
        got = []
        for half in range(2):
            at = rows_at(at_two * 256 + half * 128, 128, 128)
            geo = info_ref[slot, :, at]
            sub = iota((8, 128), 0)
            norm = geo[0:1] ** 2 + geo[1:2] ** 2 + geo[2:3] ** 2 + geo[3:4]
            base = jnp.where(
                sub < 3, geo, jnp.where(sub == 3, norm, jnp.where(sub == 4, 1.0, 0.0))
            )
            high, middle, low = (p.astype(F32) for p in parts(base))
            leaf = geo[4:5] + float(LEAVES * slot)
            named = jnp.where(fiota((104, 128), 0) == leaf, 1.0, 0.0)
            got.append(jnp.concatenate([high, middle, low, named], axis=0).T.astype(BF16))
        table = jnp.concatenate(got, axis=0)
        at = rows_at(slot * ROWS + at_two * 256, 256, 256)
        other_ref[at, :] = times(table, other_sel).astype(BF16)
        chunk_ref[rows_at(slot * (ROWS // CHUNK) + at_two * 8, 8, 8), :] = times(member, table)
        if slot == 1:
            own_ref[rows_at(at_two * 256, 256, 256), :] = times(table, own_sel).astype(BF16)
        return carry

    lax.fori_loop(0, ROWS // 256, two_blocks, 0)


def chunk_lists(chunk_ref, adjacent, list_ref):
    named = hot(chunk_ref[...] > 0.5)
    per = BLOCK // CHUNK
    own = ROWS // CHUNK
    member = hot(iota((32, own), 1) // per == iota((32, own), 0))
    of_block = hot(times(member, named[own : 2 * own]) > 0.5)
    wanted = hot(times(of_block, adjacent) > 0.5)
    needed = hot(times(named, wanted, ((1,), (1,))) > 0.5)
    below = hot(iota((CHUNKS, CHUNKS), 1) <= iota((CHUNKS, CHUNKS), 0))
    upto = times(below, needed)
    spot = fiota((CHUNKS, LIST), 1)
    last = iota((1, LIST), 1) == LIST - 1
    for b in range(BLOCKS):
        column = upto[:, b : b + 1]
        found = jnp.sum(jnp.where(column <= spot, 1.0, 0.0), axis=0, keepdims=True)
        total = column[CHUNKS - 1 : CHUNKS]
        list_ref[b : b + 1, :] = jnp.where(last, total, found).astype(jnp.int32)


def arrive_kernel(
    dens_ref,
    info_ref,
    near_ref,
    far_ref,
    offset_ref,
    table_ref,
    trans_ref,
    own_sel_ref,
    other_sel_ref,
    win_ref,
    other_ref,
    own_ref,
    local_ref,
    list_ref,
    infos_ref,
    mate_ref,
    x2_ref,
    col_ref,
    wide_ref,
    send_ref,
    land_ref,
    moment_ref,
    sel_ref,
    adj_ref,
    chunk_ref,
    multi_ref,
    padded_ref,
    info_send,
    info_recv,
    mate_send,
    mate_recv,
    pack_send,
    pack_recv,
    halo_send,
    halo_recv,
    multi_send,
    multi_recv,
):
    me, my, core = place()
    left, right = (me + DEVS - 1) % DEVS, (me + 1) % DEVS
    mate = me + 1 - 2 * core
    greet(my, core, (left, right))

    to_mate = remote(dens_ref, mate_ref, mate_send, mate_recv, device_of(mate))
    to_mate.start()
    info_copies = []
    for at, (device, slot) in enumerate(((right, 0), (left, 2))):
        copy = remote(
            info_ref, infos_ref.at[slot], info_send.at[at], info_recv.at[at], device_of(device)
        )
        copy.start()
        info_copies.append(copy)
    infos_ref[1] = info_ref[...]

    def gather_half(x_ref, slot, side, after):
        to_columns(lambda at: infos_ref[slot, 5:6, at], col_ref)
        side_by_side(x_ref, x2_ref)

        def one(step, carry):
            group = (step + my // 8) % 8
            idx = jnp.concatenate(
                [
                    col_ref[rows_at(PACK * (8 * group + j) + QUOTA * core, QUOTA, 8), :]
                    for j in range(8)
                ],
                axis=0,
            )
            got = taken(idx, x2_ref)
            for j in range(8):
                wide_ref[rows_at(PACK * (8 * group + j) + QUOTA * side, QUOTA, 8), :] = got[
                    QUOTA * j : QUOTA * (j + 1)
                ]
            after(group)
            return carry

        lax.fori_loop(0, 8, one, 0)

    def ship(group):
        at = rows_at(8 * PACK * group, 8 * PACK, 128)
        send_ref[at, :] = wide_ref[at, :].astype(BF16)
        send_packs(group, my, core, send_ref, land_ref, pack_send, pack_recv)

    gather_half(dens_ref, 1, core, lambda group: None)
    for copy in info_copies:
        copy.wait_recv()
    to_mate.wait_recv()
    gather_half(mate_ref, 2 - 2 * core, 1 - core, ship)
    mine = rows_at(PACK * my, PACK, 16)
    land_ref[mine, :] = send_ref[mine, :]

    lane = iota((LEAVES, 128), 1)
    adjacent = jnp.zeros((LEAVES, 128), F32)
    for j in range(near_ref.shape[1]):
        adjacent = jnp.maximum(
            adjacent, jnp.where(near_ref[:, j : j + 1] + HOT == lane, 1.0, 0.0)
        )
    first = jnp.where(me == 0, OWN, HOT)
    end = jnp.where(me == DEVS - 1, OWN + LEAVES, HOT + 3 * LEAVES)
    adjacent = jnp.where((lane >= first) & (lane < end), adjacent, 0.0)
    adj_ref[...] = jnp.zeros((128, 128), F32)
    adj_ref[OWN : OWN + LEAVES, :] = adjacent
    sel_ref[...] = own_sel_ref[...]
    sel_ref[OWN : OWN + LEAVES, :] = jnp.where(
        (lane >= HOT) & (lane < HOT + 3 * LEAVES), (1.0 - adjacent) * FAR_AWAY, 0.0
    )
    own_sel, other_sel = sel_ref[...].astype(BF16), other_sel_ref[...].astype(BF16)
    member = hot(iota((8, 256), 1) // CHUNK == iota((8, 256), 0))
    for slot in range(3):
        features(
            slot, infos_ref, own_sel, other_sel, member, own_ref, other_ref, chunk_ref
        )
    spare = pl.ds(3 * ROWS, CHUNK)
    other_ref[spare, :] = hot(iota((CHUNK, 128), 1) == 120)
    win_ref[spare, :] = jnp.zeros((CHUNK, WIDTH), BF16)
    chunk_lists(chunk_ref, adj_ref[...].astype(BF16), list_ref)
    moment_ref[...] = jnp.zeros((128, 128), F32)
    moment_ref[:, : table_ref.shape[1]] = table_ref[...].astype(F32)
    moment = moment_ref[...].astype(BF16)
    to_columns(lambda at: infos_ref[1, 6:7, at], col_ref)

    wait_all(my, send_ref, land_ref, pack_send, pack_recv, device_of(right))
    side_by_side(land_ref, x2_ref)

    def halo(start, count):
        src = win_ref.at[rows_at(ROWS + start, count, 256)]
        return [
            remote(
                src,
                win_ref.at[rows_at(base + start, count, 256)],
                halo_send.at[at],
                halo_recv.at[at],
                device_of(device),
            )
            for at, (device, base) in enumerate(((right, 0), (left, 2 * ROWS)))
        ]

    def leaf_rows(b, carry):
        at = rows_at(b * 256, 256, 256)
        win_ref[rows_at(ROWS + b * 256, 256, 256), :] = taken(col_ref[at, :], x2_ref).astype(BF16)
        for copy in halo(b * 256, 256):
            copy.start()
        return carry

    lax.fori_loop(0, ROWS // 256, leaf_rows, 0)

    in_leaf = jnp.concatenate(
        [
            hot(fiota((LEAVES, 128), 0) == infos_ref[1, 4:5, 128 * b : 128 * (b + 1)])
            for b in range(ROWS // 128)
        ],
        axis=1,
    )
    leaf_sum = times(in_leaf, win_ref[ROWS : 2 * ROWS, :])
    multi = sum(times(p, moment) for p in parts(leaf_sum))
    multi_ref[1] = multi
    multi_ref[3] = jnp.zeros((LEAVES, 128), F32)
    multi_copies = []
    for at, (device, slot) in enumerate(((right, 0), (left, 2))):
        copy = remote(
            multi_ref.at[1],
            multi_ref.at[slot],
            multi_send.at[at],
            multi_recv.at[at],
            device_of(device),
        )
        copy.start()
        multi_copies.append(copy)

    code = offset_ref[...] * 128 + far_ref[...] - (me - 1) * LEAVES
    offsets = trans_ref.shape[0]
    counted = []
    for o in range(offsets):
        count = jnp.zeros((LEAVES, 128), F32)
        for j in range(far_ref.shape[1]):
            count = count + jnp.where(code[:, j : j + 1] == lane + o * 128, 1.0, 0.0)
        counted.append(count.astype(BF16))
    counted = jnp.concatenate(counted, axis=0)
    for copy in multi_copies:
        copy.wait_recv()
    nearby = multi_ref[...].reshape(128, 128)
    grouped = sum(times(counted, p) for p in parts(nearby))
    local = jnp.zeros((LEAVES, 128), F32)
    nm = trans_ref.shape[1]
    padded_ref[...] = jnp.zeros((128, 128), F32)
    for o in range(offsets):
        padded_ref[:nm, :nm] = trans_ref[o]
        local = local + lax.dot_general(
            grouped[LEAVES * o : LEAVES * (o + 1)],
            padded_ref[...],
            (((1,), (1,)), ((), ())),
            precision=lax.Precision.HIGHEST,
            preferred_element_type=F32,
        )
    far = sum(times(p, moment, ((1,), (1,))) for p in parts(local))
    for at, part in enumerate(parts(far)):
        padded_ref[...] = jnp.zeros((128, 128), F32)
        padded_ref[OWN : OWN + LEAVES, :] = part.astype(F32)
        local_ref[at] = padded_ref[...].astype(BF16)

    for copy in halo(0, ROWS):
        copy.wait()
    for copy in multi_copies + info_copies + [to_mate]:
        copy.wait_send()


def near_kernel(
    list_ref, own_ref, other_ref, win_ref, local_ref, block_ref, out_ref, sum_ref
):
    def block(b, carry):
        at = rows_at(b * BLOCK, BLOCK, BLOCK)
        own = own_ref[at, :]
        sum_ref[...] = jnp.zeros((BLOCK, WIDTH), F32)

        def step(s, inner):
            total = sum_ref[...]
            for t in range(STEP // 8):
                starts = [
                    rows_at(list_ref[b, s * STEP + t * 8 + j] * CHUNK, CHUNK, CHUNK)
                    for j in range(8)
                ]
                other = jnp.concatenate([other_ref[start, :] for start in starts], axis=0)
                dist = times(own, other, ((1,), (1,)))
                weight = jnp.where(dist < 1e29, lax.rsqrt(dist), 0.0).astype(BF16)
                dens = jnp.concatenate([win_ref[start, :] for start in starts], axis=0)
                total = total + times(weight, dens)
            sum_ref[...] = total
            return inner

        steps = (list_ref[b, LIST - 1] + STEP - 1) // STEP
        lax.fori_loop(0, steps, step, 0)
        near = times(sum_ref[...].astype(BF16), block_ref[...])
        leaf = other_ref[rows_at(ROWS + b * BLOCK, BLOCK, BLOCK), :]
        far = times(leaf, local_ref[0]) + times(leaf, local_ref[1]) + times(leaf, local_ref[2])
        out_ref[at, :] = (near + far).astype(BF16)
        return carry

    lax.fori_loop(0, BLOCKS, block, 0)


def return_kernel(
    total_ref,
    infos_ref,
    land_ref,
    mate_ref,
    x2_ref,
    col_ref,
    wide_ref,
    send_ref,
    mate_send,
    mate_recv,
    pack_send,
    pack_recv,
):
    me, my, core = place()
    mate = me + 1 - 2 * core
    greet(my, core, (mate,))
    to_mate = remote(total_ref, mate_ref, mate_send, mate_recv, device_of(mate))
    to_mate.start()
    groups = CHIPS // 16
    sub = jnp.concatenate([iota((QUOTA, 128), 0) + PACK * j for j in range(8)], axis=0)

    def scatter_half(x_ref, slot, side, after):
        to_columns(lambda at: infos_ref[slot, 6:7, at], col_ref)
        split_by_target(x_ref, col_ref, x2_ref)

        def one(step, carry):
            group = (step + my // 8) % groups
            row = (sub + (8 * PACK * group + QUOTA * core)).astype(F32)
            pieces = []
            for b in range(ROWS // 128):
                order = infos_ref[slot, 6:7, 128 * b : 128 * (b + 1)]
                order = jnp.where(order >= HALF, order - HALF, order)
                pieces.append(hot(row == order))
            both = times(jnp.concatenate(pieces, axis=1), x2_ref[...])
            for upper in range(2):
                for j in range(8):
                    chip = CHIPS // 2 * upper + 8 * group + j
                    wide_ref[rows_at(PACK * chip + QUOTA * side, QUOTA, 8), :] = both[
                        QUOTA * j : QUOTA * (j + 1), WIDTH * upper : WIDTH * (upper + 1)
                    ]
            after(group)
            return carry

        lax.fori_loop(0, groups, one, 0)

    def ship(group):
        for upper in range(2):
            pack = group + groups * upper
            at = rows_at(8 * PACK * pack, 8 * PACK, 128)
            send_ref[at, :] = wide_ref[at, :].astype(BF16)
            send_packs(pack, my, core, send_ref, land_ref, pack_send, pack_recv)

    scatter_half(total_ref, 1, core, lambda group: None)
    to_mate.wait_recv()
    scatter_half(mate_ref, 2 - 2 * core, 1 - core, ship)
    mine = rows_at(PACK * my, PACK, 16)
    land_ref[mine, :] = send_ref[mine, :]
    wait_all(my, send_ref, land_ref, pack_send, pack_recv, device_of(mate))
    to_mate.wait_send()


def order_kernel(x_ref, info_ref, out_ref, x2_ref, col_ref):
    to_columns(lambda at: info_ref[5:6, at], col_ref)
    split_by_target(x_ref, col_ref, x2_ref)

    def one(b, carry):
        row = fiota((256, 128), 0) + (b * 256).astype(F32)
        pieces = []
        for c in range(ROWS // 128):
            order = info_ref[5:6, 128 * c : 128 * (c + 1)]
            order = jnp.where(order >= HALF, order - HALF, order)
            pieces.append(hot(row == order))
        both = times(jnp.concatenate(pieces, axis=1), x2_ref[...])
        out_ref[rows_at(b * 256, 256, 256), :] = both[:, :WIDTH]
        out_ref[rows_at(HALF + b * 256, 256, 256), :] = both[:, WIDTH:]
        return carry

    lax.fori_loop(0, HALF // 256, one, 0)


def call(kernel, outs, scratch, inputs, smem=0, collective=None):
    spec = lambda count: [pl.BlockSpec(memory_space=pltpu.VMEM)] * count
    params = dict(vmem_limit_bytes=VMEM)
    if collective is not None:
        params.update(collective_id=collective, has_side_effects=True)
    return pl.pallas_call(
        kernel,
        out_shape=outs,
        in_specs=[pl.BlockSpec(memory_space=pltpu.SMEM)] * smem + spec(len(inputs) - smem),
        out_specs=jax.tree.map(lambda _: pl.BlockSpec(memory_space=pltpu.VMEM), outs),
        scratch_shapes=scratch,
        compiler_params=pltpu.CompilerParams(**params),
    )(*inputs)


def shaped(*shape, dtype=BF16):
    return jax.ShapeDtypeStruct(shape, dtype)


def on_device(
    density,
    send_order,
    recv_order,
    geometry,
    pair_leaf,
    near_list,
    far_list,
    far_offset,
    moment_table,
    coulomb_block,
    translation,
):
    dma = pltpu.SemaphoreType.DMA
    vmem = lambda *shape, dtype=BF16: pltpu.VMEM(shape, dtype)
    small = [a.astype(F32) for a in (pair_leaf, send_order, recv_order)]
    info = jnp.concatenate([geometry, *small, jnp.zeros((1, ROWS), F32)], axis=0)
    own_sel, other_sel = (jnp.asarray(s) for s in selections())
    win, other, own, local, lists, infos = call(
        arrive_kernel,
        (
            shaped(WINDOW, WIDTH),
            shaped(WINDOW, 128),
            shaped(ROWS, 128),
            shaped(3, 128, 128),
            shaped(32, LIST, dtype=jnp.int32),
            shaped(3, 8, ROWS, dtype=F32),
        ),
        [
            vmem(ROWS, WIDTH),
            vmem(HALF, 2 * WIDTH),
            vmem(ROWS, 128, dtype=F32),
            vmem(ROWS, WIDTH, dtype=F32),
            vmem(ROWS, WIDTH),
            vmem(ROWS, WIDTH),
            vmem(128, 128, dtype=F32),
            vmem(128, 128, dtype=F32),
            vmem(128, 128, dtype=F32),
            vmem(CHUNKS, 128, dtype=F32),
            vmem(4, LEAVES, 128, dtype=F32),
            vmem(128, 128, dtype=F32),
            dma((2,)),
            dma((2,)),
            dma,
            dma,
            dma,
            dma,
            dma((2,)),
            dma((2,)),
            dma((2,)),
            dma((2,)),
        ],
        (
            density,
            info,
            near_list,
            far_list,
            far_offset,
            moment_table,
            translation,
            own_sel,
            other_sel,
        ),
        collective=0,
    )
    total = call(
        near_kernel,
        shaped(ROWS, WIDTH),
        [vmem(BLOCK, WIDTH, dtype=F32)],
        (lists, own, other, win, local, coulomb_block),
        smem=1,
    )
    returned = call(
        return_kernel,
        shaped(ROWS, WIDTH),
        [
            vmem(ROWS, WIDTH),
            vmem(ROWS, 2 * WIDTH),
            vmem(ROWS, 128, dtype=F32),
            vmem(ROWS, WIDTH, dtype=F32),
            vmem(ROWS, WIDTH),
            dma,
            dma,
            dma,
            dma,
        ],
        (total, infos),
        collective=1,
    )
    return call(
        order_kernel,
        shaped(ROWS, WIDTH, dtype=F32),
        [vmem(ROWS, 2 * WIDTH), vmem(ROWS, 128, dtype=F32)],
        (returned, info),
    )


def solution(mesh):
    rows = P(("gx", "gy"), None)
    placed = (rows, rows, rows, P(None, ("gx", "gy")), rows, rows, rows, rows, P(), P(), P())
    return jax.shard_map(
        on_device, mesh=mesh, in_specs=placed, out_specs=rows, check_vma=False
    )
```

```python
import functools

import jax
import jax.numpy as jnp
import numpy as np
from jax import lax
from jax.experimental import pallas as pl
from jax.experimental.pallas import tpu as pltpu
from jax.sharding import PartitionSpec as P

MESH = pl.DeviceIdType.MESH
F32, BF16 = jnp.float32, jnp.bfloat16
FAR_AWAY = 3e38
NAMED = 4.0
ROWS = 3072
WIDTH = 128
HALF = ROWS // 2
DEVS, CHIPS = 128, 64
QUOTA = 24
PACK = 2 * QUOTA
LEAVES = 32
HOT = 24
OWN = HOT + LEAVES
CHUNK = 32
CHUNKS = 3 * ROWS // CHUNK
BLOCK = 128
BLOCKS = ROWS // BLOCK
STEP = 64
PART = 8
ABREAST = 4
LIST = 384
PLAN = BLOCKS + 8
WINDOW = 3 * ROWS + CHUNK
VMEM = 56 * 1024 * 1024


def selections():
    own, other = np.zeros((128, 128), np.float32), np.zeros((128, 128), np.float32)
    for axis in range(3):
        for at, (a, b) in enumerate(((0, 0), (0, 8), (8, 0), (0, 16), (16, 0), (8, 8))):
            own[a + axis, 6 * axis + at] = 1.0
            other[b + axis, 6 * axis + at] = -2.0
    for at in range(3):
        own[8 * at + 3, 18 + at] = 1.0
        other[4, 18 + at] = 1.0
        own[4, 21 + at] = 1.0
        other[8 * at + 3, 21 + at] = 1.0
    own[4, 120] = FAR_AWAY
    for at in range(HOT, HOT + 3 * LEAVES):
        other[at, at] = NAMED
    return own, other


def iota(shape, axis):
    return lax.broadcasted_iota(jnp.int32, shape, axis)


def fiota(shape, axis):
    return iota(shape, axis).astype(F32)


def hot(condition):
    return jnp.where(condition, 1.0, 0.0).astype(BF16)


def times(a, b, dims=((1,), (0,))):
    return lax.dot_general(a, b, (dims, ((), ())), preferred_element_type=F32)


def parts(x):
    high = x.astype(BF16)
    rest = x - high.astype(F32)
    middle = rest.astype(BF16)
    low = (rest - middle.astype(F32)).astype(BF16)
    return high, middle, low


def remote(src, dst, send, recv, device):
    return pltpu.make_async_remote_copy(
        src_ref=src,
        dst_ref=dst,
        send_sem=send,
        recv_sem=recv,
        device_id=device,
        device_id_type=MESH,
    )


def place():
    gx, gy = lax.axis_index("gx"), lax.axis_index("gy")
    me = gx * 8 + gy
    return me, me // 2, gy % 2


def device_of(d):
    return (d // 8, d % 8)


def of_chip(chip, core):
    return (chip // 4, (chip % 4) * 2 + core)


def rows_at(start, count, step):
    return pl.ds(pl.multiple_of(start, step), count)


def to_columns(row_of, col_ref):
    def block(b, carry):
        at = rows_at(b * 128, 128, 128)
        col_ref[at, :] = jnp.broadcast_to(row_of(at), (128, 128)).T
        return carry

    lax.fori_loop(0, ROWS // 128, block, 0)


def side_by_side(x_ref, x2_ref):
    x2_ref[:, :WIDTH] = x_ref[:HALF]
    x2_ref[:, WIDTH:] = x_ref[HALF:]


def taken(idx, x2_ref):
    upper = idx >= HALF
    low = jnp.where(upper, idx - HALF, idx)
    lane = fiota(idx.shape, 1)
    pick = jnp.concatenate([hot(low == lane + 128.0 * b) for b in range(HALF // 128)], axis=1)
    both = times(pick, x2_ref[...])
    return jnp.where(upper, both[:, WIDTH:], both[:, :WIDTH])


def split_by_target(x_ref, col_ref, x2_ref):
    def block(b, carry):
        at = rows_at(b * 256, 256, 256)
        x = x_ref[at, :].astype(F32)
        upper = col_ref[at, :] >= HALF
        x2_ref[at, :WIDTH] = jnp.where(upper, 0.0, x).astype(BF16)
        x2_ref[at, WIDTH:] = jnp.where(upper, x, 0.0).astype(BF16)
        return carry

    lax.fori_loop(0, ROWS // 256, block, 0)


def wait_all(my, send_ref, land_ref, send_sem, recv_sem, device):
    got = pl.ds(0, PACK * (CHIPS - 1))
    copy = remote(send_ref.at[got], land_ref.at[got], send_sem, recv_sem, device)
    copy.wait_recv()
    copy.wait_send()


def send_packs(group, my, core, send_ref, land_ref, send_sem, recv_sem):
    for j in range(8):
        chip = 8 * group + (my + j) % 8

        @pl.when(chip != my)
        def _():
            remote(
                send_ref.at[rows_at(PACK * chip, PACK, 16)],
                land_ref.at[rows_at(PACK * my, PACK, 16)],
                send_sem,
                recv_sem,
                of_chip(chip, core),
            ).start()


def greet(my, core, others):
    barrier = pltpu.get_barrier_semaphore()

    def one(o, carry):
        pl.semaphore_signal(
            barrier, inc=1, device_id=of_chip((my + o) % CHIPS, core), device_id_type=MESH
        )
        return carry

    lax.fori_loop(1, CHIPS, one, 0)
    for other in others:
        pl.semaphore_signal(barrier, inc=1, device_id=device_of(other), device_id_type=MESH)
    pl.semaphore_wait(barrier, CHIPS - 1 + len(others))


def features(slot, info_ref, own_sel, other_sel, member, own_ref, other_ref, chunk_ref):
    def two_blocks(at_two, carry):
        got = []
        for half in range(2):
            at = rows_at(at_two * 256 + half * 128, 128, 128)
            geo = info_ref[slot, :, at]
            sub = iota((8, 128), 0)
            norm = geo[0:1] ** 2 + geo[1:2] ** 2 + geo[2:3] ** 2 + geo[3:4]
            base = jnp.where(
                sub < 3, geo, jnp.where(sub == 3, norm, jnp.where(sub == 4, 1.0, 0.0))
            )
            high, middle, low = (p.astype(F32) for p in parts(base))
            leaf = geo[4:5] + float(LEAVES * slot)
            named = jnp.where(fiota((104, 128), 0) == leaf, 1.0, 0.0)
            got.append(jnp.concatenate([high, middle, low, named], axis=0).T.astype(BF16))
        table = jnp.concatenate(got, axis=0)
        at = rows_at(slot * ROWS + at_two * 256, 256, 256)
        other_ref[at, :] = times(table, other_sel).astype(BF16)
        chunk_ref[rows_at(slot * (ROWS // CHUNK) + at_two * 8, 8, 8), :] = times(member, table)
        if slot == 1:
            own_ref[rows_at(at_two * 256, 256, 256), :] = times(table, own_sel).astype(BF16)
        return carry

    lax.fori_loop(0, ROWS // 256, two_blocks, 0)


def chunk_lists(chunk_ref, adjacent, list_ref):
    named = hot(chunk_ref[...] > 0.5)
    per = BLOCK // CHUNK
    own = ROWS // CHUNK
    member = hot(iota((32, own), 1) // per == iota((32, own), 0))
    of_block = hot(times(member, named[own : 2 * own]) > 0.5)
    wanted = hot(times(of_block, adjacent) > 0.5)
    needed = hot(times(named, wanted, ((1,), (1,))) > 0.5)
    below = hot(iota((CHUNKS, CHUNKS), 1) <= iota((CHUNKS, CHUNKS), 0))
    upto = times(below, needed)
    spot = fiota((CHUNKS, LIST), 1)
    for b in range(BLOCKS):
        column = upto[:, b : b + 1]
        found = jnp.sum(jnp.where(column <= spot, 1.0, 0.0), axis=0, keepdims=True)
        list_ref[b : b + 1, :] = (found * CHUNK).astype(jnp.int32)
    list_ref[BLOCKS : BLOCKS + 8, :] = jnp.full((8, LIST), CHUNKS * CHUNK, jnp.int32)
    spot = fiota((1, LIST), 1)
    block, begun, end = (jnp.zeros((1, LIST), F32) for _ in range(3))
    for b in range(BLOCKS):
        count = upto[CHUNKS - 1 : CHUNKS, b : b + 1]
        steps = jnp.zeros((1, 1), F32)
        for n in range(0, CHUNKS, STEP):
            steps = steps + jnp.where(count > n, 1.0, 0.0)
        end = end + steps
        passed = end <= spot
        block = block + jnp.where(passed, 1.0, 0.0)
        begun = begun + jnp.where(passed, steps, 0.0)
    within = jnp.where(block < BLOCKS, (spot - begun) * STEP, 0.0)
    list_ref[PLAN : PLAN + 1, :] = block.astype(jnp.int32)
    last = iota((1, LIST), 1) == LIST - 1
    list_ref[PLAN + 1 : PLAN + 2, :] = jnp.where(last, end, within).astype(jnp.int32)


def arrive_kernel(
    dens_ref,
    geometry_ref,
    leaf_ref,
    from_ref,
    to_ref,
    near_ref,
    far_ref,
    offset_ref,
    table_ref,
    translation_ref,
    own_sel_ref,
    other_sel_ref,
    win_ref,
    other_ref,
    own_ref,
    local_ref,
    list_ref,
    infos_ref,
    mate_ref,
    x2_ref,
    col_ref,
    wide_ref,
    send_ref,
    land_ref,
    moment_ref,
    sel_ref,
    adj_ref,
    chunk_ref,
    multi_ref,
    padded_ref,
    info_ref,
    trans_ref,
    trans_sem,
    info_send,
    info_recv,
    mate_send,
    mate_recv,
    pack_send,
    pack_recv,
    halo_send,
    halo_recv,
    multi_send,
    multi_recv,
):
    me, my, core = place()
    left, right = (me + DEVS - 1) % DEVS, (me + 1) % DEVS
    mate = me + 1 - 2 * core
    offsets = trans_ref.shape[0]
    fetched = [
        pltpu.make_async_copy(translation_ref.at[:, o], trans_ref.at[o], trans_sem.at[o])
        for o in range(offsets)
    ]
    for copy in fetched:
        copy.start()
    info_ref[...] = jnp.zeros(info_ref.shape, F32)
    info_ref[0:4, :] = geometry_ref[...]
    info_ref[4:5, :] = leaf_ref[...].astype(F32)
    info_ref[5:6, :] = from_ref[...].astype(F32)
    info_ref[6:7, :] = to_ref[...].astype(F32)
    greet(my, core, (left, right))

    to_mate = remote(dens_ref, mate_ref, mate_send, mate_recv, device_of(mate))
    to_mate.start()
    info_copies = []
    for at, (device, slot) in enumerate(((right, 0), (left, 2))):
        copy = remote(
            info_ref, infos_ref.at[slot], info_send.at[at], info_recv.at[at], device_of(device)
        )
        copy.start()
        info_copies.append(copy)
    infos_ref[1] = info_ref[...]

    def gather_half(x_ref, slot, side, after):
        to_columns(lambda at: infos_ref[slot, 5:6, at], col_ref)
        side_by_side(x_ref, x2_ref)

        def one(step, carry):
            group = (step + my // 8) % 8
            idx = jnp.concatenate(
                [
                    col_ref[rows_at(PACK * (8 * group + j) + QUOTA * core, QUOTA, 8), :]
                    for j in range(8)
                ],
                axis=0,
            )
            got = taken(idx, x2_ref)
            for j in range(8):
                wide_ref[rows_at(PACK * (8 * group + j) + QUOTA * side, QUOTA, 8), :] = got[
                    QUOTA * j : QUOTA * (j + 1)
                ]
            after(group)
            return carry

        lax.fori_loop(0, 8, one, 0)

    def ship(group):
        at = rows_at(8 * PACK * group, 8 * PACK, 128)
        send_ref[at, :] = wide_ref[at, :].astype(BF16)
        send_packs(group, my, core, send_ref, land_ref, pack_send, pack_recv)

    gather_half(dens_ref, 1, core, lambda group: None)
    for copy in info_copies:
        copy.wait_recv()
    to_mate.wait_recv()
    gather_half(mate_ref, 2 - 2 * core, 1 - core, ship)
    mine = rows_at(PACK * my, PACK, 16)
    land_ref[mine, :] = send_ref[mine, :]

    lane = iota((LEAVES, 128), 1)
    nears, fars = near_ref.shape[0], far_ref.shape[0]
    padded_ref[...] = jnp.zeros((128, 128), F32)
    padded_ref[0:nears, 0:LEAVES] = near_ref[...].astype(F32)
    base = ((me - 1) * LEAVES).astype(F32)
    code = offset_ref[...].astype(F32) * 128.0 + far_ref[...].astype(F32) - base
    padded_ref[16 : 16 + fars, 0:LEAVES] = code
    listed = padded_ref[...].T[:LEAVES].astype(jnp.int32)
    adjacent = jnp.zeros((LEAVES, 128), F32)
    for j in range(nears):
        adjacent = jnp.maximum(
            adjacent, jnp.where(listed[:, j : j + 1] + HOT == lane, 1.0, 0.0)
        )
    first = jnp.where(me == 0, OWN, HOT)
    end = jnp.where(me == DEVS - 1, OWN + LEAVES, HOT + 3 * LEAVES)
    adjacent = jnp.where((lane >= first) & (lane < end), adjacent, 0.0)
    adj_ref[...] = jnp.zeros((128, 128), F32)
    adj_ref[OWN : OWN + LEAVES, :] = adjacent
    sel_ref[...] = own_sel_ref[...]
    sel_ref[OWN : OWN + LEAVES, :] = jnp.where(
        (lane >= HOT) & (lane < HOT + 3 * LEAVES), (1.0 - adjacent) * FAR_AWAY, 0.0
    )
    own_sel, other_sel = sel_ref[...].astype(BF16), other_sel_ref[...].astype(BF16)
    member = hot(iota((8, 256), 1) // CHUNK == iota((8, 256), 0))
    for slot in range(3):
        features(
            slot, infos_ref, own_sel, other_sel, member, own_ref, other_ref, chunk_ref
        )
    spare = pl.ds(3 * ROWS, CHUNK)
    other_ref[spare, :] = hot(iota((CHUNK, 128), 1) == 120)
    win_ref[spare, :] = jnp.zeros((CHUNK, WIDTH), BF16)
    chunk_lists(chunk_ref, adj_ref[...].astype(BF16), list_ref)
    moment_ref[...] = jnp.zeros((128, 128), F32)
    moment_ref[:, : table_ref.shape[1]] = table_ref[...].astype(F32)
    moment = moment_ref[...].astype(BF16)
    to_columns(lambda at: infos_ref[1, 6:7, at], col_ref)

    wait_all(my, send_ref, land_ref, pack_send, pack_recv, device_of(right))
    side_by_side(land_ref, x2_ref)

    def halo(start, count):
        src = win_ref.at[rows_at(ROWS + start, count, 256)]
        return [
            remote(
                src,
                win_ref.at[rows_at(base + start, count, 256)],
                halo_send.at[at],
                halo_recv.at[at],
                device_of(device),
            )
            for at, (device, base) in enumerate(((right, 0), (left, 2 * ROWS)))
        ]

    def leaf_rows(b, carry):
        at = rows_at(b * 256, 256, 256)
        win_ref[rows_at(ROWS + b * 256, 256, 256), :] = taken(col_ref[at, :], x2_ref).astype(BF16)
        for copy in halo(b * 256, 256):
            copy.start()
        return carry

    lax.fori_loop(0, ROWS // 256, leaf_rows, 0)

    in_leaf = jnp.concatenate(
        [
            hot(fiota((LEAVES, 128), 0) == infos_ref[1, 4:5, 128 * b : 128 * (b + 1)])
            for b in range(ROWS // 128)
        ],
        axis=1,
    )
    leaf_sum = times(in_leaf, win_ref[ROWS : 2 * ROWS, :])
    multi = sum(times(p, moment) for p in parts(leaf_sum))
    multi_ref[1] = multi
    multi_ref[3] = jnp.zeros((LEAVES, 128), F32)
    multi_copies = []
    for at, (device, slot) in enumerate(((right, 0), (left, 2))):
        copy = remote(
            multi_ref.at[1],
            multi_ref.at[slot],
            multi_send.at[at],
            multi_recv.at[at],
            device_of(device),
        )
        copy.start()
        multi_copies.append(copy)

    counted = []
    for o in range(offsets):
        count = jnp.zeros((LEAVES, 128), F32)
        for j in range(16, 16 + fars):
            count = count + jnp.where(listed[:, j : j + 1] == lane + o * 128, 1.0, 0.0)
        counted.append(count.astype(BF16))
    counted = jnp.concatenate(counted, axis=0)
    for copy in multi_copies:
        copy.wait_recv()
    nearby = multi_ref[...].reshape(128, 128)
    grouped = sum(times(counted, p) for p in parts(nearby))
    local = jnp.zeros((LEAVES, 128), F32)
    nm = trans_ref.shape[1]
    padded_ref[...] = jnp.zeros((128, 128), F32)
    for o in range(offsets):
        fetched[o].wait()
        padded_ref[:nm, :nm] = trans_ref[o]
        local = local + lax.dot_general(
            grouped[LEAVES * o : LEAVES * (o + 1)],
            padded_ref[...],
            (((1,), (1,)), ((), ())),
            precision=lax.Precision.HIGHEST,
            preferred_element_type=F32,
        )
    far = sum(times(p, moment, ((1,), (1,))) for p in parts(local))
    for at, part in enumerate(parts(far / NAMED)):
        padded_ref[...] = jnp.zeros((128, 128), F32)
        padded_ref[OWN : OWN + LEAVES, :] = part.astype(F32)
        local_ref[at] = padded_ref[...].astype(BF16)

    for copy in halo(0, ROWS):
        copy.wait()
    for copy in multi_copies + info_copies + [to_mate]:
        copy.wait_send()


def near_kernel(
    list_ref, own_ref, other_ref, win_ref, local_ref, block_ref, out_ref, sum_ref
):
    sum_ref[...] = jnp.zeros((ROWS, WIDTH), F32)

    def rows_of(at):
        return rows_at(jnp.minimum(list_ref[PLAN, at], BLOCKS - 1) * BLOCK, BLOCK, BLOCK)

    def potential(at):
        own = own_ref[rows_of(at), :]
        row, first = list_ref[PLAN, at], list_ref[PLAN + 1, at]
        total = None
        for part in range(0, STEP, PART):
            starts = [
                rows_at(list_ref[row, first + part + j], CHUNK, CHUNK) for j in range(PART)
            ]
            other = jnp.concatenate([other_ref[start, :] for start in starts], axis=0)
            weight = lax.rsqrt(times(own, other, ((1,), (1,)))).astype(BF16)
            dens = jnp.concatenate([win_ref[start, :] for start in starts], axis=0)
            got = times(weight, dens)
            total = got if total is None else total + got
        return total

    def together(i, carry):
        found = [potential(i * ABREAST + j) for j in range(ABREAST)]
        for j in range(ABREAST):
            at = rows_of(i * ABREAST + j)
            sum_ref[at, :] = sum_ref[at, :] + found[j]
        return carry

    steps = list_ref[PLAN + 1, LIST - 1]
    lax.fori_loop(0, (steps + ABREAST - 1) // ABREAST, together, 0)

    def finish(b, carry):
        at = rows_at(b * 512, 512, 512)
        near = times(sum_ref[at, :].astype(BF16), block_ref[...])
        leaf = other_ref[rows_at(ROWS + b * 512, 512, 512), :]
        far = times(leaf, local_ref[0]) + times(leaf, local_ref[1]) + times(leaf, local_ref[2])
        out_ref[at, :] = (near + far).astype(BF16)
        return carry

    lax.fori_loop(0, ROWS // 512, finish, 0)


def return_kernel(
    total_ref,
    infos_ref,
    land_ref,
    mate_ref,
    x2_ref,
    col_ref,
    wide_ref,
    send_ref,
    mate_send,
    mate_recv,
    pack_send,
    pack_recv,
):
    me, my, core = place()
    mate = me + 1 - 2 * core
    greet(my, core, (mate,))
    to_mate = remote(total_ref, mate_ref, mate_send, mate_recv, device_of(mate))
    to_mate.start()
    groups = CHIPS // 16
    sub = jnp.concatenate([iota((QUOTA, 128), 0) + PACK * j for j in range(8)], axis=0)

    def scatter_half(x_ref, slot, side, after):
        to_columns(lambda at: infos_ref[slot, 6:7, at], col_ref)
        split_by_target(x_ref, col_ref, x2_ref)

        def one(step, carry):
            group = (step + my // 8) % groups
            row = (sub + (8 * PACK * group + QUOTA * core)).astype(F32)
            pieces = []
            for b in range(ROWS // 128):
                order = infos_ref[slot, 6:7, 128 * b : 128 * (b + 1)]
                order = jnp.where(order >= HALF, order - HALF, order)
                pieces.append(hot(row == order))
            both = times(jnp.concatenate(pieces, axis=1), x2_ref[...])
            for upper in range(2):
                for j in range(8):
                    chip = CHIPS // 2 * upper + 8 * group + j
                    wide_ref[rows_at(PACK * chip + QUOTA * side, QUOTA, 8), :] = both[
                        QUOTA * j : QUOTA * (j + 1), WIDTH * upper : WIDTH * (upper + 1)
                    ]
            after(group)
            return carry

        lax.fori_loop(0, groups, one, 0)

    def ship(group):
        for upper in range(2):
            pack = group + groups * upper
            at = rows_at(8 * PACK * pack, 8 * PACK, 128)
            send_ref[at, :] = wide_ref[at, :].astype(BF16)
            send_packs(pack, my, core, send_ref, land_ref, pack_send, pack_recv)

    scatter_half(total_ref, 1, core, lambda group: None)
    to_mate.wait_recv()
    scatter_half(mate_ref, 2 - 2 * core, 1 - core, ship)
    mine = rows_at(PACK * my, PACK, 16)
    land_ref[mine, :] = send_ref[mine, :]
    wait_all(my, send_ref, land_ref, pack_send, pack_recv, device_of(mate))
    to_mate.wait_send()


def order_kernel(x_ref, from_ref, out_ref, x2_ref, col_ref):
    to_columns(lambda at: from_ref[0:1, at].astype(F32), col_ref)
    split_by_target(x_ref, col_ref, x2_ref)

    def one(b, carry):
        row = fiota((256, 128), 0) + (b * 256).astype(F32)
        pieces = []
        for c in range(ROWS // 128):
            order = from_ref[0:1, 128 * c : 128 * (c + 1)].astype(F32)
            order = jnp.where(order >= HALF, order - HALF, order)
            pieces.append(hot(row == order))
        both = times(jnp.concatenate(pieces, axis=1), x2_ref[...])
        out_ref[rows_at(b * 256, 256, 256), :] = both[:, :WIDTH]
        out_ref[rows_at(HALF + b * 256, 256, 256), :] = both[:, WIDTH:]
        return carry

    lax.fori_loop(0, HALF // 256, one, 0)


def call(kernel, outs, scratch, inputs, smem=(), hbm=(), collective=None):
    spaces = [
        pltpu.SMEM if at in smem else pl.ANY if at in hbm else pltpu.VMEM
        for at in range(len(inputs))
    ]
    params = dict(vmem_limit_bytes=VMEM)
    if collective is not None:
        params.update(collective_id=collective, has_side_effects=True)
    return pl.pallas_call(
        kernel,
        out_shape=outs,
        in_specs=[pl.BlockSpec(memory_space=space) for space in spaces],
        out_specs=jax.tree.map(lambda _: pl.BlockSpec(memory_space=pltpu.VMEM), outs),
        scratch_shapes=scratch,
        compiler_params=pltpu.CompilerParams(**params),
    )(*inputs)


def shaped(*shape, dtype=BF16):
    return jax.ShapeDtypeStruct(shape, dtype)


def on_device(
    density,
    send_order,
    recv_order,
    geometry,
    pair_leaf,
    near_list,
    far_list,
    far_offset,
    moment_table,
    coulomb_block,
    translation,
):
    dma = pltpu.SemaphoreType.DMA
    vmem = lambda *shape, dtype=BF16: pltpu.VMEM(shape, dtype)
    offsets, nm = translation.shape[:2]
    own_sel, other_sel = (jnp.asarray(s) for s in selections())
    win, other, own, local, lists, infos = call(
        arrive_kernel,
        (
            shaped(WINDOW, WIDTH),
            shaped(WINDOW, 128),
            shaped(ROWS, 128),
            shaped(3, 128, 128),
            shaped(PLAN + 8, LIST, dtype=jnp.int32),
            shaped(3, 8, ROWS, dtype=F32),
        ),
        [
            vmem(ROWS, WIDTH),
            vmem(HALF, 2 * WIDTH),
            vmem(ROWS, 128, dtype=F32),
            vmem(ROWS, WIDTH, dtype=F32),
            vmem(ROWS, WIDTH),
            vmem(ROWS, WIDTH),
            vmem(128, 128, dtype=F32),
            vmem(128, 128, dtype=F32),
            vmem(128, 128, dtype=F32),
            vmem(CHUNKS, 128, dtype=F32),
            vmem(4, LEAVES, 128, dtype=F32),
            vmem(128, 128, dtype=F32),
            vmem(8, ROWS, dtype=F32),
            vmem(offsets, nm, nm, dtype=F32),
            dma((offsets,)),
            dma((2,)),
            dma((2,)),
            dma,
            dma,
            dma,
            dma,
            dma((2,)),
            dma((2,)),
            dma((2,)),
            dma((2,)),
        ],
        (
            density,
            geometry,
            pair_leaf,
            send_order,
            recv_order,
            near_list.T,
            far_list.T,
            far_offset.T,
            moment_table,
            translation.transpose(1, 0, 2),
            own_sel,
            other_sel,
        ),
        hbm=(9,),
        collective=0,
    )
    total = call(
        near_kernel,
        shaped(ROWS, WIDTH),
        [vmem(ROWS, WIDTH, dtype=F32)],
        (lists, own, other, win, local, coulomb_block),
        smem=(0,),
    )
    returned = call(
        return_kernel,
        shaped(ROWS, WIDTH),
        [
            vmem(ROWS, WIDTH),
            vmem(ROWS, 2 * WIDTH),
            vmem(ROWS, 128, dtype=F32),
            vmem(ROWS, WIDTH, dtype=F32),
            vmem(ROWS, WIDTH),
            dma,
            dma,
            dma,
            dma,
        ],
        (total, infos),
        collective=1,
    )
    return call(
        order_kernel,
        shaped(ROWS, WIDTH, dtype=F32),
        [vmem(ROWS, 2 * WIDTH), vmem(ROWS, 128, dtype=F32)],
        (returned, send_order),
    )


def solution(mesh):
    rows = P(("gx", "gy"), None)
    placed = (rows, rows, rows, P(None, ("gx", "gy")), rows, rows, rows, rows, P(), P(), P())
    return jax.shard_map(
        on_device, mesh=mesh, in_specs=placed, out_specs=rows, check_vma=False
    )
```

```python
import functools

import jax
import jax.numpy as jnp
import numpy as np
from jax import lax
from jax.experimental import pallas as pl
from jax.experimental.pallas import tpu as pltpu
from jax.sharding import PartitionSpec as P

MESH = pl.DeviceIdType.MESH
F32, BF16 = jnp.float32, jnp.bfloat16
FAR_AWAY = 3e38
NAMED = 4.0
ROWS = 3072
WIDTH = 128
HALF = ROWS // 2
DEVS, CHIPS = 128, 64
QUOTA = 24
PAIRS = 4
PACK = 2 * QUOTA
LEAVES = 32
HOT = 24
OWN = HOT + LEAVES
CHUNK = 32
CHUNKS = 3 * ROWS // CHUNK
BLOCK = 128
BLOCKS = ROWS // BLOCK
STEP = 64
PART = 8
ABREAST = 4
LIST = 384
PLAN = BLOCKS + 8
WINDOW = 3 * ROWS + CHUNK
VMEM = 56 * 1024 * 1024


def selections():
    own, other = np.zeros((128, 128), np.float32), np.zeros((128, 128), np.float32)
    for axis in range(3):
        for at, (a, b) in enumerate(((0, 0), (0, 8), (8, 0), (0, 16), (16, 0), (8, 8))):
            own[a + axis, 6 * axis + at] = 1.0
            other[b + axis, 6 * axis + at] = -2.0
    for at in range(3):
        own[8 * at + 3, 18 + at] = 1.0
        other[4, 18 + at] = 1.0
        own[4, 21 + at] = 1.0
        other[8 * at + 3, 21 + at] = 1.0
    own[4, 120] = FAR_AWAY
    for at in range(HOT, HOT + 3 * LEAVES):
        other[at, at] = NAMED
    return own, other


def iota(shape, axis):
    return lax.broadcasted_iota(jnp.int32, shape, axis)


def fiota(shape, axis):
    return iota(shape, axis).astype(F32)


def hot(condition):
    return jnp.where(condition, 1.0, 0.0).astype(BF16)


def times(a, b, dims=((1,), (0,))):
    return lax.dot_general(a, b, (dims, ((), ())), preferred_element_type=F32)


def parts(x):
    high = x.astype(BF16)
    rest = x - high.astype(F32)
    middle = rest.astype(BF16)
    low = (rest - middle.astype(F32)).astype(BF16)
    return high, middle, low


def remote(src, dst, send, recv, device):
    return pltpu.make_async_remote_copy(
        src_ref=src,
        dst_ref=dst,
        send_sem=send,
        recv_sem=recv,
        device_id=device,
        device_id_type=MESH,
    )


def place():
    gx, gy = lax.axis_index("gx"), lax.axis_index("gy")
    me = gx * 8 + gy
    return me, me // 2, gy % 2


def device_of(d):
    return (d // 8, d % 8)


def of_chip(chip, core):
    return (chip // 4, (chip % 4) * 2 + core)


def rows_at(start, count, step):
    return pl.ds(pl.multiple_of(start, step), count)


def to_columns(row_of, col_ref):
    def block(b, carry):
        at = rows_at(b * 128, 128, 128)
        col_ref[at, :] = jnp.broadcast_to(row_of(at), (128, 128)).T
        return carry

    lax.fori_loop(0, ROWS // 128, block, 0, unroll=8)


def side_by_side(x_ref, x2_ref):
    x2_ref[:, :WIDTH] = x_ref[:HALF]
    x2_ref[:, WIDTH:] = x_ref[HALF:]


def taken(idx, x2_ref):
    upper = idx >= HALF
    low = jnp.where(upper, idx - HALF, idx)
    lane = fiota(idx.shape, 1)
    pick = jnp.concatenate([hot(low == lane + 128.0 * b) for b in range(HALF // 128)], axis=1)
    both = times(pick, x2_ref[...])
    return jnp.where(upper, both[:, WIDTH:], both[:, :WIDTH])


def split_by_target(x_ref, col_ref, x2_ref):
    def block(b, carry):
        at = rows_at(b * 256, 256, 256)
        x = x_ref[at, :].astype(F32)
        upper = col_ref[at, :] >= HALF
        x2_ref[at, :WIDTH] = jnp.where(upper, 0.0, x).astype(BF16)
        x2_ref[at, WIDTH:] = jnp.where(upper, x, 0.0).astype(BF16)
        return carry

    lax.fori_loop(0, ROWS // 256, block, 0)


def send_packs(step, pair, my, core, send_ref, land_ref, send_sem, recv_sem):
    for upper in range(2):
        for j in range(8):
            chip = CHIPS // 2 * upper + 8 * pair + (my + j) % 8

            @pl.when(chip != my)
            def _():
                remote(
                    send_ref.at[rows_at(PACK * chip, PACK, 16)],
                    land_ref.at[rows_at(PACK * my, PACK, 16)],
                    send_sem,
                    recv_sem.at[step],
                    of_chip(chip, core),
                ).start()


def received(packs, land_ref, recv_sem, send_sem, device):
    got = pl.ds(0, PACK * packs)
    remote(land_ref.at[got], land_ref.at[got], send_sem, recv_sem, device).wait_recv()


def all_received(land_ref, recv_sem, send_sem, device):
    for step in range(PAIRS):
        packs = 15 if step == 0 else 16
        received(packs, land_ref, recv_sem.at[step], send_sem, device)


def all_sent(send_ref, land_ref, send_sem, recv_sem, device):
    got = pl.ds(0, PACK * (CHIPS - 1))
    remote(send_ref.at[got], land_ref.at[got], send_sem, recv_sem.at[0], device).wait_send()


def greet(my, core, others):
    barrier = pltpu.get_barrier_semaphore()

    def one(o, carry):
        pl.semaphore_signal(
            barrier, inc=1, device_id=of_chip((my + o) % CHIPS, core), device_id_type=MESH
        )
        return carry

    lax.fori_loop(1, CHIPS, one, 0)
    for other in others:
        pl.semaphore_signal(barrier, inc=1, device_id=device_of(other), device_id_type=MESH)
    return lambda: pl.semaphore_wait(barrier, CHIPS - 1 + len(others))


def features(slot, info_ref, own_sel, other_sel, member, own_ref, other_ref, chunk_ref):
    def blocks(at_four, carry):
        got = []
        for part in range(4):
            at = rows_at(at_four * 512 + part * 128, 128, 128)
            geo = info_ref[slot, :, at]
            sub = iota((8, 128), 0)
            norm = geo[0:1] ** 2 + geo[1:2] ** 2 + geo[2:3] ** 2 + geo[3:4]
            base = jnp.where(
                sub < 3, geo, jnp.where(sub == 3, norm, jnp.where(sub == 4, 1.0, 0.0))
            )
            high, middle, low = (p.astype(F32) for p in parts(base))
            leaf = geo[4:5] + float(LEAVES * slot)
            named = jnp.where(fiota((104, 128), 0) == leaf, 1.0, 0.0)
            got.append(jnp.concatenate([high, middle, low, named], axis=0).T.astype(BF16))
        table = jnp.concatenate(got, axis=0)
        at = rows_at(slot * ROWS + at_four * 512, 512, 512)
        other_ref[at, :] = times(table, other_sel).astype(BF16)
        chunk_ref[rows_at(slot * (ROWS // CHUNK) + at_four * 16, 16, 16), :] = times(member, table)
        if slot == 1:
            own_ref[rows_at(at_four * 512, 512, 512), :] = times(table, own_sel).astype(BF16)
        return carry

    lax.fori_loop(0, ROWS // 512, blocks, 0)


def chunk_lists(chunk_ref, adjacent, list_ref):
    named = hot(chunk_ref[...] > 0.5)
    per = BLOCK // CHUNK
    own = ROWS // CHUNK
    member = hot(iota((32, own), 1) // per == iota((32, own), 0))
    of_block = hot(times(member, named[own : 2 * own]) > 0.5)
    wanted = hot(times(of_block, adjacent) > 0.5)
    needed = hot(times(named, wanted, ((1,), (1,))) > 0.5)
    below = hot(iota((CHUNKS, CHUNKS), 1) <= iota((CHUNKS, CHUNKS), 0))
    upto = times(below, needed)
    spot = fiota((CHUNKS, LIST), 1)
    for b in range(BLOCKS):
        column = upto[:, b : b + 1]
        found = jnp.sum(jnp.where(column <= spot, 1.0, 0.0), axis=0, keepdims=True)
        list_ref[b : b + 1, :] = (found * CHUNK).astype(jnp.int32)
    list_ref[BLOCKS : BLOCKS + 8, :] = jnp.full((8, LIST), CHUNKS * CHUNK, jnp.int32)
    spot = fiota((1, LIST), 1)
    block, begun, end = (jnp.zeros((1, LIST), F32) for _ in range(3))
    for b in range(BLOCKS):
        count = upto[CHUNKS - 1 : CHUNKS, b : b + 1]
        steps = jnp.zeros((1, 1), F32)
        for n in range(0, CHUNKS, STEP):
            steps = steps + jnp.where(count > n, 1.0, 0.0)
        end = end + steps
        passed = end <= spot
        block = block + jnp.where(passed, 1.0, 0.0)
        begun = begun + jnp.where(passed, steps, 0.0)
    within = jnp.where(block < BLOCKS, (spot - begun) * STEP, 0.0)
    list_ref[PLAN : PLAN + 1, :] = block.astype(jnp.int32)
    last = iota((1, LIST), 1) == LIST - 1
    list_ref[PLAN + 1 : PLAN + 2, :] = jnp.where(last, end, within).astype(jnp.int32)


def arrive_kernel(
    dens_ref,
    geometry_ref,
    leaf_ref,
    from_ref,
    to_ref,
    near_ref,
    far_ref,
    offset_ref,
    table_ref,
    translation_ref,
    own_sel_ref,
    other_sel_ref,
    win_out,
    other_out,
    own_out,
    local_ref,
    list_ref,
    mate_to_ref,
    mate_ref,
    x2_ref,
    col_ref,
    wide_ref,
    send_ref,
    land_ref,
    moment_ref,
    sel_ref,
    adj_ref,
    chunk_ref,
    multi_ref,
    padded_ref,
    info_ref,
    infos_ref,
    mid_ref,
    spare_ref,
    other_ref,
    own_ref,
    trans_ref,
    trans_sem,
    out_sem,
    info_send,
    info_recv,
    mate_send,
    mate_recv,
    pack_send,
    pack_recv,
    halo_send,
    halo_recv,
    multi_send,
    multi_recv,
):
    me, my, core = place()
    left, right = (me + DEVS - 1) % DEVS, (me + 1) % DEVS
    mate = me + 1 - 2 * core
    all_here = greet(my, core, (left, right))

    info_ref[...] = jnp.zeros(info_ref.shape, F32)
    info_ref[0:4, :] = geometry_ref[...]
    info_ref[4:5, :] = leaf_ref[...].astype(F32)
    info_ref[5:6, :] = from_ref[...].astype(F32)
    info_ref[6:7, :] = to_ref[...].astype(F32)
    infos_ref[1] = info_ref[...]
    to_columns(lambda at: info_ref[5:6, at], col_ref)
    side_by_side(dens_ref, x2_ref)

    all_here()
    to_mate = remote(dens_ref, mate_ref, mate_send, mate_recv, device_of(mate))
    to_mate.start()
    info_copies = []
    for at, (device, slot) in enumerate(((right, 0), (left, 2))):
        copy = remote(
            info_ref, infos_ref.at[slot], info_send.at[at], info_recv.at[at], device_of(device)
        )
        copy.start()
        info_copies.append(copy)

    def gather_half(side, after):
        def one(step, carry):
            pair = (step + my // 8) % PAIRS
            chips = [CHIPS // 2 * upper + 8 * pair + j for upper in range(2) for j in range(8)]
            idx = jnp.concatenate(
                [col_ref[rows_at(PACK * chip + QUOTA * core, QUOTA, 8), :] for chip in chips],
                axis=0,
            )
            got = taken(idx, x2_ref)
            for at, chip in enumerate(chips):
                wide_ref[rows_at(PACK * chip + QUOTA * side, QUOTA, 8), :] = got[
                    QUOTA * at : QUOTA * (at + 1)
                ]
            after(step, pair)
            return carry

        lax.fori_loop(0, PAIRS, one, 0)

    def ship(step, pair):
        for upper in range(2):
            at = rows_at(8 * PACK * pair + HALF * upper, 8 * PACK, 128)
            send_ref[at, :] = wide_ref[at, :].astype(BF16)
        send_packs(step, pair, my, core, send_ref, land_ref, pack_send, pack_recv)

    gather_half(core, lambda step, pair: None)
    for copy in info_copies:
        copy.wait_recv()
    to_columns(lambda at: infos_ref[2 - 2 * core, 5:6, at], col_ref)
    to_mate.wait_recv()
    side_by_side(mate_ref, x2_ref)
    gather_half(1 - core, ship)
    mine = rows_at(PACK * my, PACK, 16)
    land_ref[mine, :] = send_ref[mine, :]

    offsets = trans_ref.shape[0]
    fetched = [
        pltpu.make_async_copy(translation_ref.at[:, o], trans_ref.at[o], trans_sem.at[o])
        for o in range(offsets)
    ]
    for copy in fetched:
        copy.start()
    mate_to_ref[...] = infos_ref[2 - 2 * core, 6:7, :]
    lane = iota((LEAVES, 128), 1)
    nears, fars = near_ref.shape[0], far_ref.shape[0]
    padded_ref[...] = jnp.zeros((128, 128), F32)
    padded_ref[0:nears, 0:LEAVES] = near_ref[...].astype(F32)
    base = ((me - 1) * LEAVES).astype(F32)
    code = offset_ref[...].astype(F32) * 128.0 + far_ref[...].astype(F32) - base
    padded_ref[16 : 16 + fars, 0:LEAVES] = code
    listed = padded_ref[...].T[:LEAVES].astype(jnp.int32)
    adjacent = jnp.zeros((LEAVES, 128), F32)
    for j in range(nears):
        adjacent = jnp.maximum(
            adjacent, jnp.where(listed[:, j : j + 1] + HOT == lane, 1.0, 0.0)
        )
    first = jnp.where(me == 0, OWN, HOT)
    end = jnp.where(me == DEVS - 1, OWN + LEAVES, HOT + 3 * LEAVES)
    adjacent = jnp.where((lane >= first) & (lane < end), adjacent, 0.0)
    adj_ref[...] = jnp.zeros((128, 128), F32)
    adj_ref[OWN : OWN + LEAVES, :] = adjacent
    sel_ref[...] = own_sel_ref[...]
    sel_ref[OWN : OWN + LEAVES, :] = jnp.where(
        (lane >= HOT) & (lane < HOT + 3 * LEAVES), (1.0 - adjacent) * FAR_AWAY, 0.0
    )
    own_sel, other_sel = sel_ref[...].astype(BF16), other_sel_ref[...].astype(BF16)
    member = hot(iota((16, 512), 1) // CHUNK == iota((16, 512), 0))
    for slot in range(3):
        features(
            slot, infos_ref, own_sel, other_sel, member, own_ref, other_ref, chunk_ref
        )
    spare = pl.ds(3 * ROWS, CHUNK)
    other_ref[spare, :] = hot(iota((CHUNK, 128), 1) == 120)
    spare_ref[...] = jnp.zeros((CHUNK, WIDTH), BF16)
    stored = [
        pltpu.make_async_copy(src, dst, out_sem.at[at])
        for at, (src, dst) in enumerate(
            ((other_ref, other_out), (own_ref, own_out), (spare_ref, win_out.at[spare]))
        )
    ]
    for copy in stored:
        copy.start()
    chunk_lists(chunk_ref, adj_ref[...].astype(BF16), list_ref)
    moment_ref[...] = jnp.zeros((128, 128), F32)
    moment_ref[:, : table_ref.shape[1]] = table_ref[...].astype(F32)
    moment = moment_ref[...].astype(BF16)
    to_columns(lambda at: info_ref[6:7, at], col_ref)
    in_leaf = jnp.concatenate(
        [
            hot(fiota((LEAVES, 128), 0) == info_ref[4:5, 128 * b : 128 * (b + 1)])
            for b in range(ROWS // 128)
        ],
        axis=1,
    )
    counted = []
    for o in range(offsets):
        count = jnp.zeros((LEAVES, 128), F32)
        for j in range(16, 16 + fars):
            count = count + jnp.where(listed[:, j : j + 1] == lane + o * 128, 1.0, 0.0)
        counted.append(count.astype(BF16))
    counted = jnp.concatenate(counted, axis=0)

    all_received(land_ref, pack_recv, pack_send, device_of(right))
    side_by_side(land_ref, x2_ref)

    def halo(start, count):
        src = mid_ref.at[rows_at(start, count, 512)]
        return [
            remote(
                src,
                win_out.at[rows_at(base + start, count, 512)],
                halo_send.at[at],
                halo_recv.at[at],
                device_of(device),
            )
            for at, (device, base) in enumerate(((right, 0), (left, 2 * ROWS)))
        ]

    def leaf_rows(b, carry):
        at = rows_at(b * 512, 512, 512)
        mid_ref[at, :] = taken(col_ref[at, :], x2_ref).astype(BF16)
        for copy in halo(b * 512, 512):
            copy.start()
        return carry

    lax.fori_loop(0, ROWS // 512, leaf_rows, 0)
    kept = pltpu.make_async_copy(mid_ref, win_out.at[pl.ds(ROWS, ROWS)], out_sem.at[3])
    kept.start()

    leaf_sum = times(in_leaf, mid_ref[...])
    multi = sum(times(p, moment) for p in parts(leaf_sum))
    multi_ref[1] = multi
    multi_ref[3] = jnp.zeros((LEAVES, 128), F32)
    multi_copies = []
    for at, (device, slot) in enumerate(((right, 0), (left, 2))):
        copy = remote(
            multi_ref.at[1],
            multi_ref.at[slot],
            multi_send.at[at],
            multi_recv.at[at],
            device_of(device),
        )
        copy.start()
        multi_copies.append(copy)
    for copy in multi_copies:
        copy.wait_recv()
    nearby = multi_ref[...].reshape(128, 128)
    grouped = sum(times(counted, p) for p in parts(nearby))
    local = jnp.zeros((LEAVES, 128), F32)
    nm = trans_ref.shape[1]
    padded_ref[...] = jnp.zeros((128, 128), F32)
    for o in range(offsets):
        fetched[o].wait()
        padded_ref[:nm, :nm] = trans_ref[o]
        local = local + lax.dot_general(
            grouped[LEAVES * o : LEAVES * (o + 1)],
            padded_ref[...],
            (((1,), (1,)), ((), ())),
            precision=lax.Precision.HIGHEST,
            preferred_element_type=F32,
        )
    far = sum(times(p, moment, ((1,), (1,))) for p in parts(local))
    for at, part in enumerate(parts(far / NAMED)):
        padded_ref[...] = jnp.zeros((128, 128), F32)
        padded_ref[OWN : OWN + LEAVES, :] = part.astype(F32)
        local_ref[at] = padded_ref[...].astype(BF16)

    all_sent(send_ref, land_ref, pack_send, pack_recv, device_of(right))
    for copy in halo(0, ROWS):
        copy.wait()
    for copy in multi_copies + info_copies + [to_mate]:
        copy.wait_send()
    for copy in stored + [kept]:
        copy.wait()


def near_kernel(
    list_ref, own_ref, other_ref, win_ref, local_ref, block_ref, out_ref, sum_ref
):
    sum_ref[...] = jnp.zeros((ROWS, WIDTH), F32)

    def rows_of(at):
        return rows_at(jnp.minimum(list_ref[PLAN, at], BLOCKS - 1) * BLOCK, BLOCK, BLOCK)

    def potential(at):
        own = own_ref[rows_of(at), :]
        row, first = list_ref[PLAN, at], list_ref[PLAN + 1, at]
        total = None
        for part in range(0, STEP, PART):
            starts = [
                rows_at(list_ref[row, first + part + j], CHUNK, CHUNK) for j in range(PART)
            ]
            other = jnp.concatenate([other_ref[start, :] for start in starts], axis=0)
            weight = lax.rsqrt(times(own, other, ((1,), (1,)))).astype(BF16)
            dens = jnp.concatenate([win_ref[start, :] for start in starts], axis=0)
            got = times(weight, dens)
            total = got if total is None else total + got
        return total

    def together(i, carry):
        found = [potential(i * ABREAST + j) for j in range(ABREAST)]
        for j in range(ABREAST):
            at = rows_of(i * ABREAST + j)
            sum_ref[at, :] = sum_ref[at, :] + found[j]
        return carry

    steps = list_ref[PLAN + 1, LIST - 1]
    lax.fori_loop(0, (steps + ABREAST - 1) // ABREAST, together, 0)

    def finish(b, carry):
        at = rows_at(b * 512, 512, 512)
        near = times(sum_ref[at, :].astype(BF16), block_ref[...])
        leaf = other_ref[rows_at(ROWS + b * 512, 512, 512), :]
        far = times(leaf, local_ref[0]) + times(leaf, local_ref[1]) + times(leaf, local_ref[2])
        out_ref[at, :] = (near + far).astype(BF16)
        return carry

    lax.fori_loop(0, ROWS // 512, finish, 0)


def return_kernel(
    total_ref,
    from_ref,
    to_ref,
    mate_to_ref,
    out_ref,
    mate_ref,
    x2_ref,
    col_ref,
    mate_col_ref,
    wide_ref,
    send_ref,
    land_ref,
    mate_send,
    mate_recv,
    pack_send,
    pack_recv,
):
    me, my, core = place()
    mate = me + 1 - 2 * core
    all_here = greet(my, core, (mate,))
    to_columns(lambda at: to_ref[0:1, at].astype(F32), col_ref)
    to_columns(lambda at: mate_to_ref[0:1, at], mate_col_ref)
    split_by_target(total_ref, col_ref, x2_ref)
    all_here()
    to_mate = remote(total_ref, mate_ref, mate_send, mate_recv, device_of(mate))
    to_mate.start()
    sub = jnp.concatenate([iota((QUOTA, 128), 0) + PACK * j for j in range(8)], axis=0)

    def scattered(row, order_of):
        pieces = []
        for b in range(ROWS // 128):
            order = order_of(pl.ds(128 * b, 128)).astype(F32)
            order = jnp.where(order >= HALF, order - HALF, order)
            pieces.append(hot(row == order))
        return times(jnp.concatenate(pieces, axis=1), x2_ref[...])

    def scatter_half(order_ref, side, after):
        def one(step, carry):
            pair = (step + my // 8) % PAIRS
            row = (sub + (8 * PACK * pair + QUOTA * core)).astype(F32)
            both = scattered(row, lambda at: order_ref[0:1, at])
            for upper in range(2):
                for j in range(8):
                    chip = CHIPS // 2 * upper + 8 * pair + j
                    wide_ref[rows_at(PACK * chip + QUOTA * side, QUOTA, 8), :] = both[
                        QUOTA * j : QUOTA * (j + 1), WIDTH * upper : WIDTH * (upper + 1)
                    ]
            after(step, pair)
            return carry

        lax.fori_loop(0, PAIRS, one, 0)

    def ship(step, pair):
        for upper in range(2):
            at = rows_at(8 * PACK * pair + HALF * upper, 8 * PACK, 128)
            send_ref[at, :] = wide_ref[at, :].astype(BF16)
        send_packs(step, pair, my, core, send_ref, land_ref, pack_send, pack_recv)

    scatter_half(to_ref, core, lambda step, pair: None)
    to_mate.wait_recv()
    split_by_target(mate_ref, mate_col_ref, x2_ref)
    scatter_half(mate_to_ref, 1 - core, ship)
    mine = rows_at(PACK * my, PACK, 16)
    land_ref[mine, :] = send_ref[mine, :]
    to_columns(lambda at: from_ref[0:1, at].astype(F32), col_ref)
    all_received(land_ref, pack_recv, pack_send, device_of(mate))
    split_by_target(land_ref, col_ref, x2_ref)

    def ordered(b, carry):
        row = fiota((256, 128), 0) + (b * 256).astype(F32)
        both = scattered(row, lambda at: from_ref[0:1, at])
        out_ref[rows_at(b * 256, 256, 256), :] = both[:, :WIDTH]
        out_ref[rows_at(HALF + b * 256, 256, 256), :] = both[:, WIDTH:]
        return carry

    lax.fori_loop(0, HALF // 256, ordered, 0)
    all_sent(send_ref, land_ref, pack_send, pack_recv, device_of(mate))
    to_mate.wait_send()


def call(kernel, outs, scratch, inputs, smem=(), hbm=(), hbm_outs=(), collective=None):
    spaces = [
        pltpu.SMEM if at in smem else pl.ANY if at in hbm else pltpu.VMEM
        for at in range(len(inputs))
    ]
    params = dict(vmem_limit_bytes=VMEM)
    if collective is not None:
        params.update(collective_id=collective, has_side_effects=True)
    return pl.pallas_call(
        kernel,
        out_shape=outs,
        in_specs=[pl.BlockSpec(memory_space=space) for space in spaces],
        out_specs=[
            pl.BlockSpec(memory_space=pl.ANY if at in hbm_outs else pltpu.VMEM)
            for at in range(len(outs))
        ],
        scratch_shapes=scratch,
        compiler_params=pltpu.CompilerParams(**params),
    )(*inputs)


def shaped(*shape, dtype=BF16):
    return jax.ShapeDtypeStruct(shape, dtype)


def on_device(
    density,
    send_order,
    recv_order,
    geometry,
    pair_leaf,
    near_list,
    far_list,
    far_offset,
    moment_table,
    coulomb_block,
    translation,
):
    dma = pltpu.SemaphoreType.DMA
    vmem = lambda *shape, dtype=BF16: pltpu.VMEM(shape, dtype)
    offsets, nm = translation.shape[:2]
    own_sel, other_sel = (jnp.asarray(s) for s in selections())
    win, other, own, local, lists, mate_to = call(
        arrive_kernel,
        (
            shaped(WINDOW, WIDTH),
            shaped(WINDOW, 128),
            shaped(ROWS, 128),
            shaped(3, 128, 128),
            shaped(PLAN + 8, LIST, dtype=jnp.int32),
            shaped(1, ROWS, dtype=F32),
        ),
        [
            vmem(ROWS, WIDTH),
            vmem(HALF, 2 * WIDTH),
            vmem(ROWS, 128, dtype=F32),
            vmem(ROWS, WIDTH, dtype=F32),
            vmem(ROWS, WIDTH),
            vmem(ROWS, WIDTH),
            vmem(128, 128, dtype=F32),
            vmem(128, 128, dtype=F32),
            vmem(128, 128, dtype=F32),
            vmem(CHUNKS, 128, dtype=F32),
            vmem(4, LEAVES, 128, dtype=F32),
            vmem(128, 128, dtype=F32),
            vmem(8, ROWS, dtype=F32),
            vmem(3, 8, ROWS, dtype=F32),
            vmem(ROWS, WIDTH),
            vmem(CHUNK, WIDTH),
            vmem(WINDOW, 128),
            vmem(ROWS, 128),
            vmem(offsets, nm, nm, dtype=F32),
            dma((offsets,)),
            dma((4,)),
            dma((2,)),
            dma((2,)),
            dma,
            dma,
            dma,
            dma((PAIRS,)),
            dma((2,)),
            dma((2,)),
            dma((2,)),
            dma((2,)),
        ],
        (
            density,
            geometry,
            pair_leaf,
            send_order,
            recv_order,
            near_list.T,
            far_list.T,
            far_offset.T,
            moment_table,
            translation.transpose(1, 0, 2),
            own_sel,
            other_sel,
        ),
        hbm=(9,),
        hbm_outs=(0, 1, 2),
        collective=0,
    )
    (total,) = call(
        near_kernel,
        (shaped(ROWS, WIDTH),),
        [vmem(ROWS, WIDTH, dtype=F32)],
        (lists, own, other, win, local, coulomb_block),
        smem=(0,),
    )
    (coulomb,) = call(
        return_kernel,
        (shaped(ROWS, WIDTH, dtype=F32),),
        [
            vmem(ROWS, WIDTH),
            vmem(ROWS, 2 * WIDTH),
            vmem(ROWS, 128, dtype=F32),
            vmem(ROWS, 128, dtype=F32),
            vmem(ROWS, WIDTH, dtype=F32),
            vmem(ROWS, WIDTH),
            vmem(ROWS, WIDTH),
            dma,
            dma,
            dma,
            dma((PAIRS,)),
        ],
        (total, send_order, recv_order, mate_to),
        collective=1,
    )
    return coulomb


def solution(mesh):
    rows = P(("gx", "gy"), None)
    placed = (rows, rows, rows, P(None, ("gx", "gy")), rows, rows, rows, rows, P(), P(), P())
    return jax.shard_map(
        on_device, mesh=mesh, in_specs=placed, out_specs=rows, check_vma=False
    )
```

```python
import functools

import jax
import jax.numpy as jnp
import numpy as np
from jax import lax
from jax.experimental import pallas as pl
from jax.experimental.pallas import tpu as pltpu
from jax.sharding import PartitionSpec as P

MESH = pl.DeviceIdType.MESH
F32, BF16 = jnp.float32, jnp.bfloat16
FAR_AWAY = 3e38
NAMED = 4.0
ROWS = 3072
WIDTH = 128
HALF = ROWS // 2
DEVS, CHIPS = 128, 64
QUOTA = 24
PAIRS = 4
PACK = 2 * QUOTA
LEAVES = 32
HOT = 24
OWN = HOT + LEAVES
CHUNK = 32
CHUNKS = 3 * ROWS // CHUNK
BLOCK = 128
BLOCKS = ROWS // BLOCK
STEP = 64
PART = 8
ABREAST = 4
LIST = 384
PLAN = BLOCKS + 8
WINDOW = 3 * ROWS + CHUNK
VMEM = 56 * 1024 * 1024


def selections():
    own, other = np.zeros((128, 128), np.float32), np.zeros((128, 128), np.float32)
    for axis in range(3):
        for at, (a, b) in enumerate(((0, 0), (0, 8), (8, 0), (0, 16), (16, 0), (8, 8))):
            own[a + axis, 6 * axis + at] = 1.0
            other[b + axis, 6 * axis + at] = -2.0
    for at in range(3):
        own[8 * at + 3, 18 + at] = 1.0
        other[4, 18 + at] = 1.0
        own[4, 21 + at] = 1.0
        other[8 * at + 3, 21 + at] = 1.0
    own[4, 120] = FAR_AWAY
    for at in range(HOT, HOT + 3 * LEAVES):
        other[at, at] = NAMED
    return own, other


def iota(shape, axis):
    return lax.broadcasted_iota(jnp.int32, shape, axis)


def fiota(shape, axis):
    return iota(shape, axis).astype(F32)


def hot(condition):
    return jnp.where(condition, 1.0, 0.0).astype(BF16)


def times(a, b, dims=((1,), (0,))):
    return lax.dot_general(a, b, (dims, ((), ())), preferred_element_type=F32)


def parts(x):
    high = x.astype(BF16)
    rest = x - high.astype(F32)
    middle = rest.astype(BF16)
    low = (rest - middle.astype(F32)).astype(BF16)
    return high, middle, low


def remote(src, dst, send, recv, device):
    return pltpu.make_async_remote_copy(
        src_ref=src,
        dst_ref=dst,
        send_sem=send,
        recv_sem=recv,
        device_id=device,
        device_id_type=MESH,
    )


def place():
    gx, gy = lax.axis_index("gx"), lax.axis_index("gy")
    me = gx * 8 + gy
    return me, me // 2, gy % 2


def device_of(d):
    return (d // 8, d % 8)


def of_chip(chip, core):
    return (chip // 4, (chip % 4) * 2 + core)


def rows_at(start, count, step):
    return pl.ds(pl.multiple_of(start, step), count)


def to_columns(row_of, col_ref):
    def block(b, carry):
        at = rows_at(b * 128, 128, 128)
        col_ref[at, :] = jnp.broadcast_to(row_of(at), (128, 128)).T
        return carry

    lax.fori_loop(0, ROWS // 128, block, 0, unroll=8)


def side_by_side(x_ref, x2_ref):
    x2_ref[:, :WIDTH] = x_ref[:HALF]
    x2_ref[:, WIDTH:] = x_ref[HALF:]


def taken(idx, x2_ref):
    upper = idx >= HALF
    low = jnp.where(upper, idx - HALF, idx)
    lane = fiota(idx.shape, 1)
    pick = jnp.concatenate([hot(low == lane + 128.0 * b) for b in range(HALF // 128)], axis=1)
    both = times(pick, x2_ref[...])
    return jnp.where(upper, both[:, WIDTH:], both[:, :WIDTH])


def split_by_target(x_ref, col_ref, x2_ref):
    def block(b, carry):
        at = rows_at(b * 256, 256, 256)
        x = x_ref[at, :].astype(F32)
        upper = col_ref[at, :] >= HALF
        x2_ref[at, :WIDTH] = jnp.where(upper, 0.0, x).astype(BF16)
        x2_ref[at, WIDTH:] = jnp.where(upper, x, 0.0).astype(BF16)
        return carry

    lax.fori_loop(0, ROWS // 256, block, 0)


def turns(my):
    order = [(my + j) % 8 for j in range(8)]
    return [(m, m // 4, (m % 4) * 2) for m in order]


def send_packs(step, pair, turn, my, core, send_ref, land_ref, send_sem, recv_sem):
    for upper in range(2):
        for m, along, across in turn:
            chip = CHIPS // 2 * upper + 8 * pair + m

            @pl.when(chip != my)
            def _():
                remote(
                    send_ref.at[rows_at(PACK * chip, PACK, 16)],
                    land_ref.at[rows_at(PACK * my, PACK, 16)],
                    send_sem,
                    recv_sem.at[step],
                    (8 * upper + 2 * pair + along, across + core),
                ).start()


def received(packs, land_ref, recv_sem, send_sem, device):
    got = pl.ds(0, PACK * packs)
    remote(land_ref.at[got], land_ref.at[got], send_sem, recv_sem, device).wait_recv()


def all_received(land_ref, recv_sem, send_sem, device):
    for step in range(PAIRS):
        packs = 15 if step == 0 else 16
        received(packs, land_ref, recv_sem.at[step], send_sem, device)


def all_sent(send_ref, land_ref, send_sem, recv_sem, device):
    got = pl.ds(0, PACK * (CHIPS - 1))
    remote(send_ref.at[got], land_ref.at[got], send_sem, recv_sem.at[0], device).wait_send()


def greet(my, core, others):
    barrier = pltpu.get_barrier_semaphore()

    for chip in range(CHIPS):

        @pl.when(chip != my)
        def _():
            pl.semaphore_signal(
                barrier, inc=1, device_id=of_chip(chip, core), device_id_type=MESH
            )

    for other in others:
        pl.semaphore_signal(barrier, inc=1, device_id=device_of(other), device_id_type=MESH)
    return lambda: pl.semaphore_wait(barrier, CHIPS - 1 + len(others))


def features(slot, info_ref, own_sel, other_sel, member, own_ref, other_ref, chunk_ref):
    def blocks(at_four, carry):
        got = []
        for part in range(4):
            at = rows_at(at_four * 512 + part * 128, 128, 128)
            geo = info_ref[slot, :, at]
            sub = iota((8, 128), 0)
            norm = geo[0:1] ** 2 + geo[1:2] ** 2 + geo[2:3] ** 2 + geo[3:4]
            base = jnp.where(
                sub < 3, geo, jnp.where(sub == 3, norm, jnp.where(sub == 4, 1.0, 0.0))
            )
            high, middle, low = (p.astype(F32) for p in parts(base))
            leaf = geo[4:5] + float(LEAVES * slot)
            named = jnp.where(fiota((104, 128), 0) == leaf, 1.0, 0.0)
            got.append(jnp.concatenate([high, middle, low, named], axis=0).T.astype(BF16))
        table = jnp.concatenate(got, axis=0)
        at = rows_at(slot * ROWS + at_four * 512, 512, 512)
        other_ref[at, :] = times(table, other_sel).astype(BF16)
        chunk_ref[rows_at(slot * (ROWS // CHUNK) + at_four * 16, 16, 16), :] = times(member, table)
        if slot == 1:
            own_ref[rows_at(at_four * 512, 512, 512), :] = times(table, own_sel).astype(BF16)
        return carry

    lax.fori_loop(0, ROWS // 512, blocks, 0)


def chunk_lists(chunk_ref, adjacent, list_ref):
    named = hot(chunk_ref[...] > 0.5)
    per = BLOCK // CHUNK
    own = ROWS // CHUNK
    member = hot(iota((32, own), 1) // per == iota((32, own), 0))
    of_block = hot(times(member, named[own : 2 * own]) > 0.5)
    wanted = hot(times(of_block, adjacent) > 0.5)
    needed = hot(times(named, wanted, ((1,), (1,))) > 0.5)
    below = hot(iota((CHUNKS, CHUNKS), 1) <= iota((CHUNKS, CHUNKS), 0))
    upto = times(below, needed)
    spot = fiota((CHUNKS, LIST), 1)
    for b in range(BLOCKS):
        column = upto[:, b : b + 1]
        found = jnp.sum(jnp.where(column <= spot, 1.0, 0.0), axis=0, keepdims=True)
        list_ref[b : b + 1, :] = (found * CHUNK).astype(jnp.int32)
    list_ref[BLOCKS : BLOCKS + 8, :] = jnp.full((8, LIST), CHUNKS * CHUNK, jnp.int32)
    spot = fiota((1, LIST), 1)
    block, begun, end = (jnp.zeros((1, LIST), F32) for _ in range(3))
    for b in range(BLOCKS):
        count = upto[CHUNKS - 1 : CHUNKS, b : b + 1]
        steps = jnp.zeros((1, 1), F32)
        for n in range(0, CHUNKS, STEP):
            steps = steps + jnp.where(count > n, 1.0, 0.0)
        end = end + steps
        passed = end <= spot
        block = block + jnp.where(passed, 1.0, 0.0)
        begun = begun + jnp.where(passed, steps, 0.0)
    within = jnp.where(block < BLOCKS, (spot - begun) * STEP, 0.0)
    list_ref[PLAN : PLAN + 1, :] = block.astype(jnp.int32)
    last = iota((1, LIST), 1) == LIST - 1
    list_ref[PLAN + 1 : PLAN + 2, :] = jnp.where(last, end, within).astype(jnp.int32)


def arrive_kernel(
    dens_ref,
    geometry_ref,
    leaf_ref,
    from_ref,
    to_ref,
    near_ref,
    far_ref,
    offset_ref,
    table_ref,
    translation_ref,
    own_sel_ref,
    other_sel_ref,
    win_out,
    other_out,
    own_out,
    local_ref,
    list_ref,
    mate_to_ref,
    mate_ref,
    x2_ref,
    col_ref,
    wide_ref,
    send_ref,
    land_ref,
    moment_ref,
    sel_ref,
    adj_ref,
    chunk_ref,
    multi_ref,
    padded_ref,
    info_ref,
    infos_ref,
    mid_ref,
    spare_ref,
    other_ref,
    own_ref,
    trans_ref,
    wide_trans_ref,
    trans_part_ref,
    trans_sem,
    out_sem,
    info_send,
    info_recv,
    mate_send,
    mate_recv,
    pack_send,
    pack_recv,
    halo_send,
    halo_recv,
    multi_send,
    multi_recv,
):
    me, my, core = place()
    left, right = (me + DEVS - 1) % DEVS, (me + 1) % DEVS
    mate = me + 1 - 2 * core
    turn = turns(my)
    all_here = greet(my, core, (left, right))

    info_ref[...] = jnp.zeros(info_ref.shape, F32)
    info_ref[0:4, :] = geometry_ref[...]
    info_ref[4:5, :] = leaf_ref[...].astype(F32)
    info_ref[5:6, :] = from_ref[...].astype(F32)
    info_ref[6:7, :] = to_ref[...].astype(F32)
    infos_ref[1] = info_ref[...]
    to_columns(lambda at: info_ref[5:6, at], col_ref)
    side_by_side(dens_ref, x2_ref)

    all_here()
    to_mate = remote(dens_ref, mate_ref, mate_send, mate_recv, device_of(mate))
    to_mate.start()
    info_copies = []
    for at, (device, slot) in enumerate(((right, 0), (left, 2))):
        copy = remote(
            info_ref, infos_ref.at[slot], info_send.at[at], info_recv.at[at], device_of(device)
        )
        copy.start()
        info_copies.append(copy)

    def gather_half(side, after):
        def one(step, carry):
            pair = (step + my // 8) % PAIRS
            chips = [CHIPS // 2 * upper + 8 * pair + j for upper in range(2) for j in range(8)]
            idx = jnp.concatenate(
                [col_ref[rows_at(PACK * chip + QUOTA * core, QUOTA, 8), :] for chip in chips],
                axis=0,
            )
            got = taken(idx, x2_ref)
            for at, chip in enumerate(chips):
                wide_ref[rows_at(PACK * chip + QUOTA * side, QUOTA, 8), :] = got[
                    QUOTA * at : QUOTA * (at + 1)
                ]
            after(step, pair)
            return carry

        lax.fori_loop(0, PAIRS, one, 0)

    def ship(step, pair):
        for upper in range(2):
            at = rows_at(8 * PACK * pair + HALF * upper, 8 * PACK, 128)
            send_ref[at, :] = wide_ref[at, :].astype(BF16)
        send_packs(step, pair, turn, my, core, send_ref, land_ref, pack_send, pack_recv)

    gather_half(core, lambda step, pair: None)
    for copy in info_copies:
        copy.wait_recv()
    to_columns(lambda at: infos_ref[2 - 2 * core, 5:6, at], col_ref)
    to_mate.wait_recv()
    side_by_side(mate_ref, x2_ref)
    gather_half(1 - core, ship)
    mine = rows_at(PACK * my, PACK, 16)
    land_ref[mine, :] = send_ref[mine, :]

    offsets = trans_ref.shape[0]
    fetched = [
        pltpu.make_async_copy(translation_ref.at[:, o], trans_ref.at[o], trans_sem.at[o])
        for o in range(offsets)
    ]
    for copy in fetched:
        copy.start()
    mate_to_ref[...] = infos_ref[2 - 2 * core, 6:7, :]
    lane = iota((LEAVES, 128), 1)
    nears, fars = near_ref.shape[0], far_ref.shape[0]
    padded_ref[...] = jnp.zeros((128, 128), F32)
    padded_ref[0:nears, 0:LEAVES] = near_ref[...].astype(F32)
    base = ((me - 1) * LEAVES).astype(F32)
    code = offset_ref[...].astype(F32) * 128.0 + far_ref[...].astype(F32) - base
    padded_ref[16 : 16 + fars, 0:LEAVES] = code
    listed = padded_ref[...].T[:LEAVES].astype(jnp.int32)
    adjacent = jnp.zeros((LEAVES, 128), F32)
    for j in range(nears):
        adjacent = jnp.maximum(
            adjacent, jnp.where(listed[:, j : j + 1] + HOT == lane, 1.0, 0.0)
        )
    first = jnp.where(me == 0, OWN, HOT)
    end = jnp.where(me == DEVS - 1, OWN + LEAVES, HOT + 3 * LEAVES)
    adjacent = jnp.where((lane >= first) & (lane < end), adjacent, 0.0)
    adj_ref[...] = jnp.zeros((128, 128), F32)
    adj_ref[OWN : OWN + LEAVES, :] = adjacent
    sel_ref[...] = own_sel_ref[...]
    sel_ref[OWN : OWN + LEAVES, :] = jnp.where(
        (lane >= HOT) & (lane < HOT + 3 * LEAVES), (1.0 - adjacent) * FAR_AWAY, 0.0
    )
    own_sel, other_sel = sel_ref[...].astype(BF16), other_sel_ref[...].astype(BF16)
    member = hot(iota((16, 512), 1) // CHUNK == iota((16, 512), 0))
    for slot in range(3):
        features(
            slot, infos_ref, own_sel, other_sel, member, own_ref, other_ref, chunk_ref
        )
    spare = pl.ds(3 * ROWS, CHUNK)
    other_ref[spare, :] = hot(iota((CHUNK, 128), 1) == 120)
    spare_ref[...] = jnp.zeros((CHUNK, WIDTH), BF16)
    stored = [
        pltpu.make_async_copy(src, dst, out_sem.at[at])
        for at, (src, dst) in enumerate(
            ((other_ref, other_out), (own_ref, own_out), (spare_ref, win_out.at[spare]))
        )
    ]
    for copy in stored:
        copy.start()
    chunk_lists(chunk_ref, adj_ref[...].astype(BF16), list_ref)
    moment_ref[...] = jnp.zeros((128, 128), F32)
    moment_ref[:, : table_ref.shape[1]] = table_ref[...].astype(F32)
    moment = moment_ref[...].astype(BF16)
    to_columns(lambda at: info_ref[6:7, at], col_ref)
    in_leaf = jnp.concatenate(
        [
            hot(fiota((LEAVES, 128), 0) == info_ref[4:5, 128 * b : 128 * (b + 1)])
            for b in range(ROWS // 128)
        ],
        axis=1,
    )
    counted = []
    for o in range(offsets):
        count = jnp.zeros((LEAVES, 128), F32)
        for j in range(16, 16 + fars):
            count = count + jnp.where(listed[:, j : j + 1] == lane + o * 128, 1.0, 0.0)
        counted.append(count.astype(BF16))
    counted = jnp.concatenate(counted, axis=0)
    nm = trans_ref.shape[1]
    wide_trans_ref[...] = jnp.zeros(wide_trans_ref.shape, F32)
    for o in range(offsets):
        fetched[o].wait()
        wide_trans_ref[:nm, 128 * o : 128 * o + nm] = trans_ref[o]
    for o in range(offsets):
        at = slice(128 * o, 128 * (o + 1))
        for p, part in enumerate(parts(wide_trans_ref[:, at])):
            trans_part_ref[p, :, at] = part

    all_received(land_ref, pack_recv, pack_send, device_of(right))
    side_by_side(land_ref, x2_ref)

    def halo(start, count):
        src = mid_ref.at[rows_at(start, count, 512)]
        return [
            remote(
                src,
                win_out.at[rows_at(base + start, count, 512)],
                halo_send.at[at],
                halo_recv.at[at],
                device_of(device),
            )
            for at, (device, base) in enumerate(((right, 0), (left, 2 * ROWS)))
        ]

    def leaf_rows(b, carry):
        at = rows_at(b * 512, 512, 512)
        mid_ref[at, :] = taken(col_ref[at, :], x2_ref).astype(BF16)
        for copy in halo(b * 512, 512):
            copy.start()
        return carry

    lax.fori_loop(0, ROWS // 512, leaf_rows, 0)
    kept = pltpu.make_async_copy(mid_ref, win_out.at[pl.ds(ROWS, ROWS)], out_sem.at[3])
    kept.start()

    leaf_sum = times(in_leaf, mid_ref[...])
    multi = sum(times(p, moment) for p in parts(leaf_sum))
    multi_ref[1] = multi
    multi_ref[3] = jnp.zeros((LEAVES, 128), F32)
    multi_copies = []
    for at, (device, slot) in enumerate(((right, 0), (left, 2))):
        copy = remote(
            multi_ref.at[1],
            multi_ref.at[slot],
            multi_send.at[at],
            multi_recv.at[at],
            device_of(device),
        )
        copy.start()
        multi_copies.append(copy)
    for copy in multi_copies:
        copy.wait_recv()
    nearby = multi_ref[...].reshape(128, 128)
    grouped = sum(times(counted, p) for p in parts(nearby))
    grouped = jnp.concatenate(
        [grouped[LEAVES * o : LEAVES * (o + 1)] for o in range(offsets)], axis=1
    )
    grouped = jnp.concatenate(parts(grouped), axis=0)
    local = jnp.zeros((LEAVES, 128), F32)
    for p in range(3):
        kept_parts = (3 - p) * LEAVES
        got = times(grouped[:kept_parts], trans_part_ref[p], ((1,), (1,)))
        for at in range(0, kept_parts, LEAVES):
            local = local + got[at : at + LEAVES]
    far = sum(times(p, moment, ((1,), (1,))) for p in parts(local))
    for at, part in enumerate(parts(far / NAMED)):
        padded_ref[...] = jnp.zeros((128, 128), F32)
        padded_ref[OWN : OWN + LEAVES, :] = part.astype(F32)
        local_ref[at] = padded_ref[...].astype(BF16)

    all_sent(send_ref, land_ref, pack_send, pack_recv, device_of(right))
    for copy in halo(0, ROWS):
        copy.wait()
    for copy in multi_copies + info_copies + [to_mate]:
        copy.wait_send()
    for copy in stored + [kept]:
        copy.wait()


def near_kernel(
    list_ref, own_ref, other_ref, win_ref, local_ref, block_ref, out_ref, sum_ref
):
    sum_ref[...] = jnp.zeros((ROWS, WIDTH), F32)

    def rows_of(at):
        return rows_at(jnp.minimum(list_ref[PLAN, at], BLOCKS - 1) * BLOCK, BLOCK, BLOCK)

    def potential(at):
        own = own_ref[rows_of(at), :]
        row, first = list_ref[PLAN, at], list_ref[PLAN + 1, at]
        total = None
        for part in range(0, STEP, PART):
            starts = [
                rows_at(list_ref[row, first + part + j], CHUNK, CHUNK) for j in range(PART)
            ]
            other = jnp.concatenate([other_ref[start, :] for start in starts], axis=0)
            weight = lax.rsqrt(times(own, other, ((1,), (1,)))).astype(BF16)
            dens = jnp.concatenate([win_ref[start, :] for start in starts], axis=0)
            got = times(weight, dens)
            total = got if total is None else total + got
        return total

    def together(i, carry):
        found = [potential(i * ABREAST + j) for j in range(ABREAST)]
        for j in range(ABREAST):
            at = rows_of(i * ABREAST + j)
            sum_ref[at, :] = sum_ref[at, :] + found[j]
        return carry

    steps = list_ref[PLAN + 1, LIST - 1]
    lax.fori_loop(0, (steps + ABREAST - 1) // ABREAST, together, 0)

    near_first = jnp.concatenate([block_ref[...], local_ref[0]], axis=0)
    rest = jnp.concatenate([local_ref[1], local_ref[2]], axis=0)

    def finish(b, carry):
        at = rows_at(b * 1024, 1024, 1024)
        near = sum_ref[at, :].astype(BF16)
        leaf = other_ref[rows_at(ROWS + b * 1024, 1024, 1024), :]
        total = times(jnp.concatenate([near, leaf], axis=1), near_first)
        total = total + times(jnp.concatenate([leaf, leaf], axis=1), rest)
        out_ref[at, :] = total.astype(BF16)
        return carry

    lax.fori_loop(0, ROWS // 1024, finish, 0)


def return_kernel(
    total_ref,
    from_ref,
    to_ref,
    mate_to_ref,
    out_ref,
    mate_ref,
    x2_ref,
    col_ref,
    mate_col_ref,
    wide_ref,
    send_ref,
    land_ref,
    mate_send,
    mate_recv,
    pack_send,
    pack_recv,
):
    me, my, core = place()
    mate = me + 1 - 2 * core
    turn = turns(my)
    all_here = greet(my, core, (mate,))
    to_columns(lambda at: to_ref[0:1, at].astype(F32), col_ref)
    to_columns(lambda at: mate_to_ref[0:1, at], mate_col_ref)
    split_by_target(total_ref, col_ref, x2_ref)
    all_here()
    to_mate = remote(total_ref, mate_ref, mate_send, mate_recv, device_of(mate))
    to_mate.start()
    sub = jnp.concatenate([iota((QUOTA, 128), 0) + PACK * j for j in range(8)], axis=0)

    def scattered(row, order_of):
        pieces = []
        for b in range(ROWS // 128):
            order = order_of(pl.ds(128 * b, 128)).astype(F32)
            order = jnp.where(order >= HALF, order - HALF, order)
            pieces.append(hot(row == order))
        return times(jnp.concatenate(pieces, axis=1), x2_ref[...])

    def scatter_half(order_ref, side, after):
        def one(step, carry):
            pair = (step + my // 8) % PAIRS
            row = (sub + (8 * PACK * pair + QUOTA * core)).astype(F32)
            both = scattered(row, lambda at: order_ref[0:1, at])
            for upper in range(2):
                for j in range(8):
                    chip = CHIPS // 2 * upper + 8 * pair + j
                    wide_ref[rows_at(PACK * chip + QUOTA * side, QUOTA, 8), :] = both[
                        QUOTA * j : QUOTA * (j + 1), WIDTH * upper : WIDTH * (upper + 1)
                    ]
            after(step, pair)
            return carry

        lax.fori_loop(0, PAIRS, one, 0)

    def ship(step, pair):
        for upper in range(2):
            at = rows_at(8 * PACK * pair + HALF * upper, 8 * PACK, 128)
            send_ref[at, :] = wide_ref[at, :].astype(BF16)
        send_packs(step, pair, turn, my, core, send_ref, land_ref, pack_send, pack_recv)

    scatter_half(to_ref, core, lambda step, pair: None)
    to_mate.wait_recv()
    split_by_target(mate_ref, mate_col_ref, x2_ref)
    scatter_half(mate_to_ref, 1 - core, ship)
    mine = rows_at(PACK * my, PACK, 16)
    land_ref[mine, :] = send_ref[mine, :]
    to_columns(lambda at: from_ref[0:1, at].astype(F32), col_ref)
    all_received(land_ref, pack_recv, pack_send, device_of(mate))
    split_by_target(land_ref, col_ref, x2_ref)

    def ordered(b, carry):
        row = fiota((256, 128), 0) + (b * 256).astype(F32)
        both = scattered(row, lambda at: from_ref[0:1, at])
        out_ref[rows_at(b * 256, 256, 256), :] = both[:, :WIDTH].astype(BF16)
        out_ref[rows_at(HALF + b * 256, 256, 256), :] = both[:, WIDTH:].astype(BF16)
        return carry

    lax.fori_loop(0, HALF // 256, ordered, 0)
    all_sent(send_ref, land_ref, pack_send, pack_recv, device_of(mate))
    to_mate.wait_send()


def call(kernel, outs, scratch, inputs, smem=(), hbm=(), hbm_outs=(), collective=None):
    spaces = [
        pltpu.SMEM if at in smem else pl.ANY if at in hbm else pltpu.VMEM
        for at in range(len(inputs))
    ]
    params = dict(vmem_limit_bytes=VMEM)
    if collective is not None:
        params.update(collective_id=collective, has_side_effects=True)
    return pl.pallas_call(
        kernel,
        out_shape=outs,
        in_specs=[pl.BlockSpec(memory_space=space) for space in spaces],
        out_specs=[
            pl.BlockSpec(memory_space=pl.ANY if at in hbm_outs else pltpu.VMEM)
            for at in range(len(outs))
        ],
        scratch_shapes=scratch,
        compiler_params=pltpu.CompilerParams(**params),
    )(*inputs)


def shaped(*shape, dtype=BF16):
    return jax.ShapeDtypeStruct(shape, dtype)


def on_device(
    density,
    send_order,
    recv_order,
    geometry,
    pair_leaf,
    near_list,
    far_list,
    far_offset,
    moment_table,
    coulomb_block,
    translation,
):
    dma = pltpu.SemaphoreType.DMA
    vmem = lambda *shape, dtype=BF16: pltpu.VMEM(shape, dtype)
    offsets, nm = translation.shape[:2]
    own_sel, other_sel = (jnp.asarray(s) for s in selections())
    win, other, own, local, lists, mate_to = call(
        arrive_kernel,
        (
            shaped(WINDOW, WIDTH),
            shaped(WINDOW, 128),
            shaped(ROWS, 128),
            shaped(3, 128, 128),
            shaped(PLAN + 8, LIST, dtype=jnp.int32),
            shaped(1, ROWS, dtype=F32),
        ),
        [
            vmem(ROWS, WIDTH),
            vmem(HALF, 2 * WIDTH),
            vmem(ROWS, 128, dtype=F32),
            vmem(ROWS, WIDTH, dtype=F32),
            vmem(ROWS, WIDTH),
            vmem(ROWS, WIDTH),
            vmem(128, 128, dtype=F32),
            vmem(128, 128, dtype=F32),
            vmem(128, 128, dtype=F32),
            vmem(CHUNKS, 128, dtype=F32),
            vmem(4, LEAVES, 128, dtype=F32),
            vmem(128, 128, dtype=F32),
            vmem(8, ROWS, dtype=F32),
            vmem(3, 8, ROWS, dtype=F32),
            vmem(ROWS, WIDTH),
            vmem(CHUNK, WIDTH),
            vmem(WINDOW, 128),
            vmem(ROWS, 128),
            vmem(offsets, nm, nm, dtype=F32),
            vmem(128, 128 * offsets, dtype=F32),
            vmem(3, 128, 128 * offsets),
            dma((offsets,)),
            dma((4,)),
            dma((2,)),
            dma((2,)),
            dma,
            dma,
            dma,
            dma((PAIRS,)),
            dma((2,)),
            dma((2,)),
            dma((2,)),
            dma((2,)),
        ],
        (
            density,
            geometry,
            pair_leaf,
            send_order,
            recv_order,
            near_list.T,
            far_list.T,
            far_offset.T,
            moment_table,
            translation.transpose(1, 0, 2),
            own_sel,
            other_sel,
        ),
        hbm=(9,),
        hbm_outs=(0, 1, 2),
        collective=0,
    )
    (total,) = call(
        near_kernel,
        (shaped(ROWS, WIDTH),),
        [vmem(ROWS, WIDTH, dtype=F32)],
        (lists, own, other, win, local, coulomb_block),
        smem=(0,),
    )
    (coulomb,) = call(
        return_kernel,
        (shaped(ROWS, WIDTH),),
        [
            vmem(ROWS, WIDTH),
            vmem(ROWS, 2 * WIDTH),
            vmem(ROWS, 128, dtype=F32),
            vmem(ROWS, 128, dtype=F32),
            vmem(ROWS, WIDTH, dtype=F32),
            vmem(ROWS, WIDTH),
            vmem(ROWS, WIDTH),
            dma,
            dma,
            dma,
            dma((PAIRS,)),
        ],
        (total, send_order, recv_order, mate_to),
        collective=1,
    )
    return coulomb.astype(F32)


def solution(mesh):
    rows = P(("gx", "gy"), None)
    placed = (rows, rows, rows, P(None, ("gx", "gy")), rows, rows, rows, rows, P(), P(), P())
    return jax.shard_map(
        on_device, mesh=mesh, in_specs=placed, out_specs=rows, check_vma=False
    )
```

```python
import functools

import jax
import jax.numpy as jnp
import numpy as np
from jax import lax
from jax.experimental import pallas as pl
from jax.experimental.pallas import tpu as pltpu
from jax.sharding import PartitionSpec as P

MESH = pl.DeviceIdType.MESH
F32, BF16 = jnp.float32, jnp.bfloat16
FAR_AWAY = 3e38
NAMED = 4.0
ROWS = 3072
WIDTH = 128
HALF = ROWS // 2
DEVS, CHIPS = 128, 64
QUOTA = 24
PAIRS = 4
PACK = 2 * QUOTA
LEAVES = 32
HOT = 24
OWN = HOT + LEAVES
CHUNK = 32
CHUNKS = 3 * ROWS // CHUNK
BLOCK = 128
BLOCKS = ROWS // BLOCK
STEP = 8
ABREAST = 32
LIST = 384
PLAN = 896
WINDOW = 3 * ROWS + CHUNK
VMEM = 56 * 1024 * 1024


def selections():
    own, other = np.zeros((128, 128), np.float32), np.zeros((128, 128), np.float32)
    for axis in range(3):
        for at, (a, b) in enumerate(((0, 0), (0, 8), (8, 0), (0, 16), (16, 0), (8, 8))):
            own[a + axis, 6 * axis + at] = 1.0
            other[b + axis, 6 * axis + at] = -2.0
    for at in range(3):
        own[8 * at + 3, 18 + at] = 1.0
        other[4, 18 + at] = 1.0
        own[4, 21 + at] = 1.0
        other[8 * at + 3, 21 + at] = 1.0
    own[4, 120] = FAR_AWAY
    for at in range(HOT, HOT + 3 * LEAVES):
        other[at, at] = NAMED
    return own, other


def iota(shape, axis):
    return lax.broadcasted_iota(jnp.int32, shape, axis)


def fiota(shape, axis):
    return iota(shape, axis).astype(F32)


def hot(condition):
    return jnp.where(condition, 1.0, 0.0).astype(BF16)


def times(a, b, dims=((1,), (0,))):
    return lax.dot_general(a, b, (dims, ((), ())), preferred_element_type=F32)


def parts(x):
    high = x.astype(BF16)
    rest = x - high.astype(F32)
    middle = rest.astype(BF16)
    low = (rest - middle.astype(F32)).astype(BF16)
    return high, middle, low


def remote(src, dst, send, recv, device):
    return pltpu.make_async_remote_copy(
        src_ref=src,
        dst_ref=dst,
        send_sem=send,
        recv_sem=recv,
        device_id=device,
        device_id_type=MESH,
    )


def place():
    gx, gy = lax.axis_index("gx"), lax.axis_index("gy")
    me = gx * 8 + gy
    return me, me // 2, gy % 2


def device_of(d):
    return (d // 8, d % 8)


def of_chip(chip, core):
    return (chip // 4, (chip % 4) * 2 + core)


def rows_at(start, count, step):
    return pl.ds(pl.multiple_of(start, step), count)


def to_columns(row_of, col_ref):
    def block(b, carry):
        at = rows_at(b * 128, 128, 128)
        col_ref[at, :] = jnp.broadcast_to(row_of(at), (128, 128)).T
        return carry

    lax.fori_loop(0, ROWS // 128, block, 0, unroll=8)


def side_by_side(x_ref, x2_ref):
    x2_ref[:, :WIDTH] = x_ref[:HALF]
    x2_ref[:, WIDTH:] = x_ref[HALF:]


def taken(idx, x2_ref):
    upper = idx >= HALF
    low = jnp.where(upper, idx - HALF, idx)
    lane = fiota(idx.shape, 1)
    pick = jnp.concatenate([hot(low == lane + 128.0 * b) for b in range(HALF // 128)], axis=1)
    both = times(pick, x2_ref[...])
    return jnp.where(upper, both[:, WIDTH:], both[:, :WIDTH])


def split_rows(x, target, x2_ref, at):
    x, upper = x.astype(F32), target >= HALF
    x2_ref[at, :WIDTH] = jnp.where(upper, 0.0, x).astype(BF16)
    x2_ref[at, WIDTH:] = jnp.where(upper, x, 0.0).astype(BF16)


def split_by_target(x_ref, col_ref, x2_ref):
    def block(b, carry):
        at = rows_at(b * 256, 256, 256)
        split_rows(x_ref[at, :], col_ref[at, :], x2_ref, at)
        return carry

    lax.fori_loop(0, ROWS // 256, block, 0)


def turns(my):
    order = [(my + j) % 8 for j in range(8)]
    return [(m, m // 4, (m % 4) * 2) for m in order]


def send_packs(step, pair, turn, my, core, send_ref, land_ref, send_sem, recv_sem):
    for upper in range(2):
        for m, along, across in turn:
            chip = CHIPS // 2 * upper + 8 * pair + m

            @pl.when(chip != my)
            def _():
                remote(
                    send_ref.at[rows_at(PACK * chip, PACK, 16)],
                    land_ref.at[rows_at(PACK * my, PACK, 16)],
                    send_sem,
                    recv_sem.at[step],
                    (8 * upper + 2 * pair + along, across + core),
                ).start()


def received(packs, land_ref, recv_sem, send_sem, device):
    got = pl.ds(0, PACK * packs)
    remote(land_ref.at[got], land_ref.at[got], send_sem, recv_sem, device).wait_recv()


def all_received(land_ref, recv_sem, send_sem, device):
    for step in range(PAIRS):
        packs = 15 if step == 0 else 16
        received(packs, land_ref, recv_sem.at[step], send_sem, device)


def all_sent(send_ref, land_ref, send_sem, recv_sem, device):
    got = pl.ds(0, PACK * (CHIPS - 1))
    remote(send_ref.at[got], land_ref.at[got], send_sem, recv_sem.at[0], device).wait_send()


def lines(axis, core):
    gx, gy = lax.axis_index("gx"), lax.axis_index("gy")
    x, z, y = gx // 4, gx % 4, gy // 2
    if axis == "x":
        return [(((x + o) % 4) * 4 + z, gy) for o in (1, 2, 3)]
    if axis == "z":
        return [(x * 4 + (z + o) % 4, gy) for o in (1, 2, 3)]
    return [(gx, ((y + o) % 4) * 2 + core) for o in (1, 2, 3)]


def greet(core, others):
    barrier = pltpu.get_barrier_semaphore()
    devices = lines("x", core) + lines("y", core) + lines("z", core)
    devices = [device_of(other) for other in others] + devices
    for device in devices:
        pl.semaphore_signal(barrier, inc=1, device_id=device, device_id_type=MESH)
    return lambda: pl.semaphore_wait(barrier, len(devices))


def spread(axis, core, sem):
    for device in lines(axis, core):
        pl.semaphore_signal(sem, inc=1, device_id=device, device_id_type=MESH)


def features(slot, info_ref, own_sel, other_sel, member, own_ref, other_ref, chunk_ref):
    def blocks(at_four, carry):
        got = []
        for part in range(4):
            at = rows_at(at_four * 512 + part * 128, 128, 128)
            geo = info_ref[slot, :, at]
            sub = iota((8, 128), 0)
            norm = geo[0:1] ** 2 + geo[1:2] ** 2 + geo[2:3] ** 2 + geo[3:4]
            base = jnp.where(
                sub < 3, geo, jnp.where(sub == 3, norm, jnp.where(sub == 4, 1.0, 0.0))
            )
            high, middle, low = (p.astype(F32) for p in parts(base))
            leaf = geo[4:5] + float(LEAVES * slot)
            named = jnp.where(fiota((104, 128), 0) == leaf, 1.0, 0.0)
            got.append(jnp.concatenate([high, middle, low, named], axis=0).T.astype(BF16))
        table = jnp.concatenate(got, axis=0)
        at = rows_at(slot * ROWS + at_four * 512, 512, 512)
        other_ref[at, :] = times(table, other_sel).astype(BF16)
        chunk_ref[rows_at(slot * (ROWS // CHUNK) + at_four * 16, 16, 16), :] = times(member, table)
        if slot == 1:
            own_ref[rows_at(at_four * 512, 512, 512), :] = times(table, own_sel).astype(BF16)
        return carry

    lax.fori_loop(0, ROWS // 512, blocks, 0)


def chunk_lists(chunk_ref, adjacent, list_ref, plan_ref):
    named = hot(chunk_ref[...] > 0.5)
    per = BLOCK // CHUNK
    own = ROWS // CHUNK
    member = hot(iota((32, own), 1) // per == iota((32, own), 0))
    of_block = hot(times(member, named[own : 2 * own]) > 0.5)
    wanted = hot(times(of_block, adjacent) > 0.5)
    needed = hot(times(named, wanted, ((1,), (1,))) > 0.5)
    below = hot(iota((CHUNKS, CHUNKS), 1) <= iota((CHUNKS, CHUNKS), 0))
    upto = times(below, needed)
    spot = fiota((CHUNKS, LIST), 1)
    for b in range(BLOCKS):
        column = upto[:, b : b + 1]
        found = jnp.sum(jnp.where(column <= spot, 1.0, 0.0), axis=0, keepdims=True)
        list_ref[b : b + 1, :] = found.astype(jnp.int32)
    list_ref[BLOCKS : BLOCKS + 8, :] = jnp.full((8, LIST), CHUNKS, jnp.int32)
    spot = fiota((1, PLAN), 1)
    block, begun, end = (jnp.zeros((1, PLAN), F32) for _ in range(3))
    for b in range(BLOCKS):
        count = upto[CHUNKS - 1 : CHUNKS, b : b + 1]
        steps = jnp.floor((count + (STEP - 1)) / STEP)
        end = end + steps
        passed = end <= spot
        block = block + jnp.where(passed, 1.0, 0.0)
        begun = begun + jnp.where(passed, steps, 0.0)
    within = jnp.where(block < BLOCKS, (spot - begun) * STEP, 0.0)
    plan_ref[0:1, :] = block.astype(jnp.int32)
    plan_ref[1:2, :] = within.astype(jnp.int32)
    plan_ref[2:3, :] = end.astype(jnp.int32)


def arrive_kernel(
    dens_ref,
    geometry_ref,
    leaf_ref,
    from_ref,
    to_ref,
    near_ref,
    far_ref,
    offset_ref,
    table_ref,
    translation_ref,
    own_sel_ref,
    other_sel_ref,
    win_out,
    other_out,
    own_out,
    local_ref,
    list_ref,
    plan_ref,
    mate_to_ref,
    mate_ref,
    x2_ref,
    col_ref,
    wide_ref,
    send_ref,
    land_ref,
    moment_ref,
    sel_ref,
    adj_ref,
    chunk_ref,
    multi_ref,
    padded_ref,
    info_ref,
    infos_ref,
    mid_ref,
    spare_ref,
    other_ref,
    own_ref,
    trans_ref,
    wide_trans_ref,
    trans_part_ref,
    trans_sem,
    out_sem,
    info_send,
    info_recv,
    mate_send,
    mate_recv,
    plane_sem,
    cube_sem,
    pack_send,
    pack_recv,
    halo_send,
    halo_recv,
    multi_send,
    multi_recv,
):
    me, my, core = place()
    left, right = (me + DEVS - 1) % DEVS, (me + 1) % DEVS
    mate = me + 1 - 2 * core
    turn = turns(my)
    all_here = greet(core, (left, right))

    info_ref[...] = jnp.zeros(info_ref.shape, F32)
    info_ref[0:4, :] = geometry_ref[...]
    info_ref[4:5, :] = leaf_ref[...].astype(F32)
    info_ref[5:6, :] = from_ref[...].astype(F32)
    info_ref[6:7, :] = to_ref[...].astype(F32)
    infos_ref[1] = info_ref[...]
    to_columns(lambda at: info_ref[5:6, at], col_ref)
    side_by_side(dens_ref, x2_ref)

    all_here()
    to_mate = remote(dens_ref, mate_ref, mate_send, mate_recv, device_of(mate))
    to_mate.start()
    info_copies = []
    for at, (device, slot) in enumerate(((right, 0), (left, 2))):
        copy = remote(
            info_ref, infos_ref.at[slot], info_send.at[at], info_recv.at[at], device_of(device)
        )
        copy.start()
        info_copies.append(copy)

    def gather_half(side, after):
        def one(step, carry):
            pair = (step + my // 8) % PAIRS
            chips = [CHIPS // 2 * upper + 8 * pair + j for upper in range(2) for j in range(8)]
            idx = jnp.concatenate(
                [col_ref[rows_at(PACK * chip + QUOTA * core, QUOTA, 8), :] for chip in chips],
                axis=0,
            )
            got = taken(idx, x2_ref)
            for at, chip in enumerate(chips):
                wide_ref[rows_at(PACK * chip + QUOTA * side, QUOTA, 8), :] = got[
                    QUOTA * at : QUOTA * (at + 1)
                ]
            after(step, pair)
            return carry

        lax.fori_loop(0, PAIRS, one, 0)

    def ship(step, pair):
        for upper in range(2):
            at = rows_at(8 * PACK * pair + HALF * upper, 8 * PACK, 128)
            send_ref[at, :] = wide_ref[at, :].astype(BF16)
        send_packs(step, pair, turn, my, core, send_ref, land_ref, pack_send, pack_recv)

    spread("y", core, plane_sem)
    gather_half(core, lambda step, pair: None)
    pl.semaphore_wait(plane_sem, 3)
    spread("z", core, cube_sem)
    for copy in info_copies:
        copy.wait_recv()
    to_columns(lambda at: infos_ref[2 - 2 * core, 5:6, at], col_ref)
    to_mate.wait_recv()
    side_by_side(mate_ref, x2_ref)
    pl.semaphore_wait(cube_sem, 3)
    gather_half(1 - core, ship)
    mine = rows_at(PACK * my, PACK, 16)
    land_ref[mine, :] = send_ref[mine, :]

    offsets = trans_ref.shape[0]
    fetched = [
        pltpu.make_async_copy(translation_ref.at[:, o], trans_ref.at[o], trans_sem.at[o])
        for o in range(offsets)
    ]
    for copy in fetched:
        copy.start()
    mate_to_ref[...] = infos_ref[2 - 2 * core, 6:7, :]
    lane = iota((LEAVES, 128), 1)
    nears, fars = near_ref.shape[0], far_ref.shape[0]
    padded_ref[...] = jnp.zeros((128, 128), F32)
    padded_ref[0:nears, 0:LEAVES] = near_ref[...].astype(F32)
    base = ((me - 1) * LEAVES).astype(F32)
    code = offset_ref[...].astype(F32) * 128.0 + far_ref[...].astype(F32) - base
    padded_ref[16 : 16 + fars, 0:LEAVES] = code
    listed = padded_ref[...].T[:LEAVES].astype(jnp.int32)
    adjacent = jnp.zeros((LEAVES, 128), F32)
    for j in range(nears):
        adjacent = jnp.maximum(
            adjacent, jnp.where(listed[:, j : j + 1] + HOT == lane, 1.0, 0.0)
        )
    first = jnp.where(me == 0, OWN, HOT)
    end = jnp.where(me == DEVS - 1, OWN + LEAVES, HOT + 3 * LEAVES)
    adjacent = jnp.where((lane >= first) & (lane < end), adjacent, 0.0)
    adj_ref[...] = jnp.zeros((128, 128), F32)
    adj_ref[OWN : OWN + LEAVES, :] = adjacent
    sel_ref[...] = own_sel_ref[...]
    sel_ref[OWN : OWN + LEAVES, :] = jnp.where(
        (lane >= HOT) & (lane < HOT + 3 * LEAVES), (1.0 - adjacent) * FAR_AWAY, 0.0
    )
    own_sel, other_sel = sel_ref[...].astype(BF16), other_sel_ref[...].astype(BF16)
    member = hot(iota((16, 512), 1) // CHUNK == iota((16, 512), 0))
    for slot in range(3):
        features(
            slot, infos_ref, own_sel, other_sel, member, own_ref, other_ref, chunk_ref
        )
    spare = pl.ds(3 * ROWS, CHUNK)
    other_ref[spare, :] = hot(iota((CHUNK, 128), 1) == 120)
    spare_ref[...] = jnp.zeros((CHUNK, WIDTH), BF16)
    stored = [
        pltpu.make_async_copy(src, dst, out_sem.at[at])
        for at, (src, dst) in enumerate(
            ((other_ref, other_out), (own_ref, own_out), (spare_ref, win_out.at[spare]))
        )
    ]
    for copy in stored:
        copy.start()
    chunk_lists(chunk_ref, adj_ref[...].astype(BF16), list_ref, plan_ref)
    moment_ref[...] = jnp.zeros((128, 128), F32)
    moment_ref[:, : table_ref.shape[1]] = table_ref[...].astype(F32)
    moment = moment_ref[...].astype(BF16)
    to_columns(lambda at: info_ref[6:7, at], col_ref)
    in_leaf = jnp.concatenate(
        [
            hot(fiota((LEAVES, 128), 0) == info_ref[4:5, 128 * b : 128 * (b + 1)])
            for b in range(ROWS // 128)
        ],
        axis=1,
    )
    counted = []
    for o in range(offsets):
        count = jnp.zeros((LEAVES, 128), F32)
        for j in range(16, 16 + fars):
            count = count + jnp.where(listed[:, j : j + 1] == lane + o * 128, 1.0, 0.0)
        counted.append(count.astype(BF16))
    counted = jnp.concatenate(counted, axis=0)
    nm = trans_ref.shape[1]
    wide_trans_ref[...] = jnp.zeros(wide_trans_ref.shape, F32)
    for o in range(offsets):
        fetched[o].wait()
        wide_trans_ref[:nm, 128 * o : 128 * o + nm] = trans_ref[o]
    for o in range(offsets):
        at = slice(128 * o, 128 * (o + 1))
        for p, part in enumerate(parts(wide_trans_ref[:, at])):
            trans_part_ref[p, :, at] = part

    all_received(land_ref, pack_recv, pack_send, device_of(right))
    side_by_side(land_ref, x2_ref)

    def halo(start, count):
        src = mid_ref.at[rows_at(start, count, 512)]
        return [
            remote(
                src,
                win_out.at[rows_at(base + start, count, 512)],
                halo_send.at[at],
                halo_recv.at[at],
                device_of(device),
            )
            for at, (device, base) in enumerate(((right, 0), (left, 2 * ROWS)))
        ]

    def leaf_rows(b, carry):
        at = rows_at(b * 512, 512, 512)
        mid_ref[at, :] = taken(col_ref[at, :], x2_ref).astype(BF16)
        for copy in halo(b * 512, 512):
            copy.start()
        return carry

    lax.fori_loop(0, ROWS // 512, leaf_rows, 0)
    kept = pltpu.make_async_copy(mid_ref, win_out.at[pl.ds(ROWS, ROWS)], out_sem.at[3])
    kept.start()

    leaf_sum = times(in_leaf, mid_ref[...])
    multi = sum(times(p, moment) for p in parts(leaf_sum))
    multi_ref[1] = multi
    multi_ref[3] = jnp.zeros((LEAVES, 128), F32)
    multi_copies = []
    for at, (device, slot) in enumerate(((right, 0), (left, 2))):
        copy = remote(
            multi_ref.at[1],
            multi_ref.at[slot],
            multi_send.at[at],
            multi_recv.at[at],
            device_of(device),
        )
        copy.start()
        multi_copies.append(copy)
    for copy in multi_copies:
        copy.wait_recv()
    nearby = multi_ref[...].reshape(128, 128)
    grouped = sum(times(counted, p) for p in parts(nearby))
    grouped = jnp.concatenate(
        [grouped[LEAVES * o : LEAVES * (o + 1)] for o in range(offsets)], axis=1
    )
    grouped = jnp.concatenate(parts(grouped), axis=0)
    local = jnp.zeros((LEAVES, 128), F32)
    for p in range(3):
        kept_parts = (3 - p) * LEAVES
        got = times(grouped[:kept_parts], trans_part_ref[p], ((1,), (1,)))
        for at in range(0, kept_parts, LEAVES):
            local = local + got[at : at + LEAVES]
    far = sum(times(p, moment, ((1,), (1,))) for p in parts(local))
    for at, part in enumerate(parts(far / NAMED)):
        padded_ref[...] = jnp.zeros((128, 128), F32)
        padded_ref[OWN : OWN + LEAVES, :] = part.astype(F32)
        local_ref[at] = padded_ref[...].astype(BF16)

    all_sent(send_ref, land_ref, pack_send, pack_recv, device_of(right))
    for copy in halo(0, ROWS):
        copy.wait()
    for copy in multi_copies + info_copies + [to_mate]:
        copy.wait_send()
    for copy in stored + [kept]:
        copy.wait()


def near_kernel(
    list_ref, plan_ref, own_ref, other_ref, win_ref, local_ref, block_ref, out_ref, sum_ref
):
    sum_ref[...] = jnp.zeros((ROWS, WIDTH), F32)

    def rows_of(at):
        return rows_at(jnp.minimum(plan_ref[0, at], BLOCKS - 1) * BLOCK, BLOCK, BLOCK)

    def potential(at):
        own = own_ref[rows_of(at), :]
        row, first = plan_ref[0, at], plan_ref[1, at]
        starts = [rows_at(list_ref[row, first + j] * CHUNK, CHUNK, CHUNK) for j in range(STEP)]
        other = jnp.concatenate([other_ref[start, :] for start in starts], axis=0)
        weight = lax.rsqrt(times(own, other, ((1,), (1,)))).astype(BF16)
        dens = jnp.concatenate([win_ref[start, :] for start in starts], axis=0)
        return times(weight, dens)

    def together(i, carry):
        found = [potential(i * ABREAST + j) for j in range(ABREAST)]
        for j in range(ABREAST):
            at = rows_of(i * ABREAST + j)
            sum_ref[at, :] = sum_ref[at, :] + found[j]
        return carry

    steps = plan_ref[2, 0]
    lax.fori_loop(0, (steps + ABREAST - 1) // ABREAST, together, 0)

    near_first = jnp.concatenate([block_ref[...], local_ref[0]], axis=0)
    rest = jnp.concatenate([local_ref[1], local_ref[2]], axis=0)

    def finish(b, carry):
        at = rows_at(b * 1024, 1024, 1024)
        near = sum_ref[at, :].astype(BF16)
        leaf = other_ref[rows_at(ROWS + b * 1024, 1024, 1024), :]
        total = times(jnp.concatenate([near, leaf], axis=1), near_first)
        total = total + times(jnp.concatenate([leaf, leaf], axis=1), rest)
        out_ref[at, :] = total.astype(BF16)
        return carry

    lax.fori_loop(0, ROWS // 1024, finish, 0)


def return_kernel(
    total_ref,
    from_ref,
    to_ref,
    mate_to_ref,
    out_ref,
    mate_ref,
    x2_ref,
    col_ref,
    mate_col_ref,
    wide_ref,
    send_ref,
    land_ref,
    mate_send,
    mate_recv,
    plane_sem,
    cube_sem,
    pack_send,
    pack_recv,
):
    me, my, core = place()
    mate = me + 1 - 2 * core
    turn = turns(my)
    all_here = greet(core, (mate,))
    to_columns(lambda at: to_ref[0:1, at].astype(F32), col_ref)
    to_columns(lambda at: mate_to_ref[0:1, at], mate_col_ref)
    split_by_target(total_ref, col_ref, x2_ref)
    all_here()
    to_mate = remote(total_ref, mate_ref, mate_send, mate_recv, device_of(mate))
    to_mate.start()
    sub = jnp.concatenate([iota((QUOTA, 128), 0) + PACK * j for j in range(8)], axis=0)

    def scattered(row, order_of):
        pieces = []
        for b in range(ROWS // 128):
            order = order_of(pl.ds(128 * b, 128)).astype(F32)
            order = jnp.where(order >= HALF, order - HALF, order)
            pieces.append(hot(row == order))
        return times(jnp.concatenate(pieces, axis=1), x2_ref[...])

    def scatter_half(order_ref, side, after):
        def one(step, carry):
            pair = (step + my // 8) % PAIRS
            row = (sub + (8 * PACK * pair + QUOTA * core)).astype(F32)
            both = scattered(row, lambda at: order_ref[0:1, at])
            for upper in range(2):
                for j in range(8):
                    chip = CHIPS // 2 * upper + 8 * pair + j
                    wide_ref[rows_at(PACK * chip + QUOTA * side, QUOTA, 8), :] = both[
                        QUOTA * j : QUOTA * (j + 1), WIDTH * upper : WIDTH * (upper + 1)
                    ]
            after(step, pair)
            return carry

        lax.fori_loop(0, PAIRS, one, 0)

    def ship(step, pair):
        for upper in range(2):
            at = rows_at(8 * PACK * pair + HALF * upper, 8 * PACK, 128)
            send_ref[at, :] = wide_ref[at, :].astype(BF16)
        send_packs(step, pair, turn, my, core, send_ref, land_ref, pack_send, pack_recv)

    spread("y", core, plane_sem)
    scatter_half(to_ref, core, lambda step, pair: None)
    pl.semaphore_wait(plane_sem, 3)
    spread("z", core, cube_sem)
    to_mate.wait_recv()
    split_by_target(mate_ref, mate_col_ref, x2_ref)
    pl.semaphore_wait(cube_sem, 3)
    scatter_half(mate_to_ref, 1 - core, ship)
    mine = rows_at(PACK * my, PACK, 16)
    land_ref[mine, :] = send_ref[mine, :]
    to_columns(lambda at: from_ref[0:1, at].astype(F32), col_ref)
    some = HALF // PAIRS
    for step in range(PAIRS):
        received(15 if step == 0 else 16, land_ref, pack_recv.at[step], pack_send, device_of(mate))
        pair = (my // 8 + PAIRS - step) % PAIRS
        spans = [rows_at(HALF * upper + some * pair, some, 128) for upper in range(2)]
        for at in spans:
            split_rows(land_ref[at, :], col_ref[at, :], x2_ref, at)
        x2 = jnp.concatenate([x2_ref[at, :] for at in spans], axis=0)
        orders = []
        for upper in range(2):
            for b in range(0, some, 128):
                at = rows_at(HALF * upper + some * pair + b, 128, 128)
                order = from_ref[0:1, at].astype(F32)
                orders.append(jnp.where(order >= HALF, order - HALF, order))

        def ordered(b, carry):
            row = fiota((256, 128), 0) + (b * 256).astype(F32)
            pick = jnp.concatenate([hot(row == order) for order in orders], axis=1)
            both = times(pick, x2)
            low, high = rows_at(b * 256, 256, 256), rows_at(HALF + b * 256, 256, 256)
            left, right = both[:, :WIDTH], both[:, WIDTH:]
            if step > 0:
                left, right = wide_ref[low, :] + left, wide_ref[high, :] + right
            if step < PAIRS - 1:
                wide_ref[low, :] = left
                wide_ref[high, :] = right
            else:
                out_ref[low, :] = left.astype(BF16)
                out_ref[high, :] = right.astype(BF16)
            return carry

        lax.fori_loop(0, HALF // 256, ordered, 0, unroll=2)
    all_sent(send_ref, land_ref, pack_send, pack_recv, device_of(mate))
    to_mate.wait_send()


def call(kernel, outs, scratch, inputs, smem=(), hbm=(), hbm_outs=(), collective=None):
    spaces = [
        pltpu.SMEM if at in smem else pl.ANY if at in hbm else pltpu.VMEM
        for at in range(len(inputs))
    ]
    params = dict(vmem_limit_bytes=VMEM)
    if collective is not None:
        params.update(collective_id=collective, has_side_effects=True)
    return pl.pallas_call(
        kernel,
        out_shape=outs,
        in_specs=[pl.BlockSpec(memory_space=space) for space in spaces],
        out_specs=[
            pl.BlockSpec(memory_space=pl.ANY if at in hbm_outs else pltpu.VMEM)
            for at in range(len(outs))
        ],
        scratch_shapes=scratch,
        compiler_params=pltpu.CompilerParams(**params),
    )(*inputs)


def shaped(*shape, dtype=BF16):
    return jax.ShapeDtypeStruct(shape, dtype)


def on_device(
    density,
    send_order,
    recv_order,
    geometry,
    pair_leaf,
    near_list,
    far_list,
    far_offset,
    moment_table,
    coulomb_block,
    translation,
):
    dma = pltpu.SemaphoreType.DMA
    vmem = lambda *shape, dtype=BF16: pltpu.VMEM(shape, dtype)
    offsets, nm = translation.shape[:2]
    own_sel, other_sel = (jnp.asarray(s) for s in selections())
    win, other, own, local, lists, plan, mate_to = call(
        arrive_kernel,
        (
            shaped(WINDOW, WIDTH),
            shaped(WINDOW, 128),
            shaped(ROWS, 128),
            shaped(3, 128, 128),
            shaped(BLOCKS + 8, LIST, dtype=jnp.int32),
            shaped(8, PLAN, dtype=jnp.int32),
            shaped(1, ROWS, dtype=F32),
        ),
        [
            vmem(ROWS, WIDTH),
            vmem(HALF, 2 * WIDTH),
            vmem(ROWS, 128, dtype=F32),
            vmem(ROWS, WIDTH, dtype=F32),
            vmem(ROWS, WIDTH),
            vmem(ROWS, WIDTH),
            vmem(128, 128, dtype=F32),
            vmem(128, 128, dtype=F32),
            vmem(128, 128, dtype=F32),
            vmem(CHUNKS, 128, dtype=F32),
            vmem(4, LEAVES, 128, dtype=F32),
            vmem(128, 128, dtype=F32),
            vmem(8, ROWS, dtype=F32),
            vmem(3, 8, ROWS, dtype=F32),
            vmem(ROWS, WIDTH),
            vmem(CHUNK, WIDTH),
            vmem(WINDOW, 128),
            vmem(ROWS, 128),
            vmem(offsets, nm, nm, dtype=F32),
            vmem(128, 128 * offsets, dtype=F32),
            vmem(3, 128, 128 * offsets),
            dma((offsets,)),
            dma((4,)),
            dma((2,)),
            dma((2,)),
            dma,
            dma,
            pltpu.SemaphoreType.REGULAR,
            pltpu.SemaphoreType.REGULAR,
            dma,
            dma((PAIRS,)),
            dma((2,)),
            dma((2,)),
            dma((2,)),
            dma((2,)),
        ],
        (
            density,
            geometry,
            pair_leaf,
            send_order,
            recv_order,
            near_list.T,
            far_list.T,
            far_offset.T,
            moment_table,
            translation.transpose(1, 0, 2),
            own_sel,
            other_sel,
        ),
        hbm=(9,),
        hbm_outs=(0, 1, 2),
        collective=0,
    )
    (total,) = call(
        near_kernel,
        (shaped(ROWS, WIDTH),),
        [vmem(ROWS, WIDTH, dtype=F32)],
        (lists, plan, own, other, win, local, coulomb_block),
        smem=(0, 1),
    )
    (coulomb,) = call(
        return_kernel,
        (shaped(ROWS, WIDTH),),
        [
            vmem(ROWS, WIDTH),
            vmem(ROWS, 2 * WIDTH),
            vmem(ROWS, 128, dtype=F32),
            vmem(ROWS, 128, dtype=F32),
            vmem(ROWS, WIDTH, dtype=F32),
            vmem(ROWS, WIDTH),
            vmem(ROWS, WIDTH),
            dma,
            dma,
            pltpu.SemaphoreType.REGULAR,
            pltpu.SemaphoreType.REGULAR,
            dma,
            dma((PAIRS,)),
        ],
        (total, send_order, recv_order, mate_to),
        collective=1,
    )
    return coulomb.astype(F32)


def solution(mesh):
    rows = P(("gx", "gy"), None)
    placed = (rows, rows, rows, P(None, ("gx", "gy")), rows, rows, rows, rows, P(), P(), P())
    return jax.shard_map(
        on_device, mesh=mesh, in_specs=placed, out_specs=rows, check_vma=False
    )
```

```python
import functools

import jax
import jax.numpy as jnp
import numpy as np
from jax import lax
from jax.experimental import pallas as pl
from jax.experimental.pallas import tpu as pltpu
from jax.sharding import PartitionSpec as P

MESH = pl.DeviceIdType.MESH
F32, BF16 = jnp.float32, jnp.bfloat16
FAR_AWAY = 3e38
NAMED = 4.0
ROWS = 3072
WIDTH = 128
HALF = ROWS // 2
DEVS, CHIPS = 128, 64
QUOTA = 24
PAIRS = 4
PACK = 2 * QUOTA
LEAVES = 32
HOT = 24
OWN = HOT + LEAVES
CHUNK = 32
CHUNKS = 3 * ROWS // CHUNK
BLOCK = 128
BLOCKS = ROWS // BLOCK
STEP = 8
ABREAST = 32
LIST = 384
PLAN = 896
WINDOW = 3 * ROWS + CHUNK
VMEM = 56 * 1024 * 1024


def selections():
    own, other = np.zeros((128, 128), np.float32), np.zeros((128, 128), np.float32)
    for axis in range(3):
        for at, (a, b) in enumerate(((0, 0), (0, 8), (8, 0), (0, 16), (16, 0), (8, 8))):
            own[a + axis, 6 * axis + at] = 1.0
            other[b + axis, 6 * axis + at] = -2.0
    for at in range(3):
        own[8 * at + 3, 18 + at] = 1.0
        other[4, 18 + at] = 1.0
        own[4, 21 + at] = 1.0
        other[8 * at + 3, 21 + at] = 1.0
    own[4, 120] = FAR_AWAY
    for at in range(HOT, HOT + 3 * LEAVES):
        other[at, at] = NAMED
    return own, other


def iota(shape, axis):
    return lax.broadcasted_iota(jnp.int32, shape, axis)


def fiota(shape, axis):
    return iota(shape, axis).astype(F32)


def hot(condition):
    return jnp.where(condition, 1.0, 0.0).astype(BF16)


def times(a, b, dims=((1,), (0,))):
    return lax.dot_general(a, b, (dims, ((), ())), preferred_element_type=F32)


def parts(x):
    high = x.astype(BF16)
    rest = x - high.astype(F32)
    middle = rest.astype(BF16)
    low = (rest - middle.astype(F32)).astype(BF16)
    return high, middle, low


def remote(src, dst, send, recv, device):
    return pltpu.make_async_remote_copy(
        src_ref=src,
        dst_ref=dst,
        send_sem=send,
        recv_sem=recv,
        device_id=device,
        device_id_type=MESH,
    )


def place():
    gx, gy = lax.axis_index("gx"), lax.axis_index("gy")
    me = gx * 8 + gy
    return me, me // 2, gy % 2


def device_of(d):
    return (d // 8, d % 8)


def of_chip(chip, core):
    return (chip // 4, (chip % 4) * 2 + core)


def rows_at(start, count, step):
    return pl.ds(pl.multiple_of(start, step), count)


def to_columns(row_of, col_ref):
    def block(b, carry):
        at = rows_at(b * 128, 128, 128)
        col_ref[at, :] = jnp.broadcast_to(row_of(at), (128, 128)).T
        return carry

    lax.fori_loop(0, ROWS // 128, block, 0, unroll=8)


def side_by_side(x_ref, x2_ref):
    x2_ref[:, :WIDTH] = x_ref[:HALF]
    x2_ref[:, WIDTH:] = x_ref[HALF:]


def taken(idx, x2_ref):
    upper = idx >= HALF
    low = jnp.where(upper, idx - HALF, idx)
    lane = fiota(idx.shape, 1)
    pick = jnp.concatenate([hot(low == lane + 128.0 * b) for b in range(HALF // 128)], axis=1)
    both = times(pick, x2_ref[...])
    return jnp.where(upper, both[:, WIDTH:], both[:, :WIDTH])


def split_rows(x, target, x2_ref, at):
    x, upper = x.astype(F32), target >= HALF
    x2_ref[at, :WIDTH] = jnp.where(upper, 0.0, x).astype(BF16)
    x2_ref[at, WIDTH:] = jnp.where(upper, x, 0.0).astype(BF16)


def split_by_target(x_ref, col_ref, x2_ref):
    def block(b, carry):
        at = rows_at(b * 256, 256, 256)
        split_rows(x_ref[at, :], col_ref[at, :], x2_ref, at)
        return carry

    lax.fori_loop(0, ROWS // 256, block, 0)


def turns(my):
    order = [(my + j) % 8 for j in range(8)]
    return [(m, m // 4, (m % 4) * 2) for m in order]


def send_packs(step, pair, turn, my, core, send_ref, land_ref, send_sem, recv_sem):
    for upper in range(2):
        for m, along, across in turn:
            chip = CHIPS // 2 * upper + 8 * pair + m

            @pl.when(chip != my)
            def _():
                remote(
                    send_ref.at[rows_at(PACK * chip, PACK, 16)],
                    land_ref.at[rows_at(PACK * my, PACK, 16)],
                    send_sem,
                    recv_sem.at[step],
                    (8 * upper + 2 * pair + along, across + core),
                ).start()


def received(packs, land_ref, recv_sem, send_sem, device):
    got = pl.ds(0, PACK * packs)
    remote(land_ref.at[got], land_ref.at[got], send_sem, recv_sem, device).wait_recv()


def all_received(land_ref, recv_sem, send_sem, device):
    for step in range(PAIRS):
        packs = 15 if step == 0 else 16
        received(packs, land_ref, recv_sem.at[step], send_sem, device)


def all_sent(send_ref, land_ref, send_sem, recv_sem, device):
    got = pl.ds(0, PACK * (CHIPS - 1))
    remote(send_ref.at[got], land_ref.at[got], send_sem, recv_sem.at[0], device).wait_send()


def lines(axis, core):
    gx, gy = lax.axis_index("gx"), lax.axis_index("gy")
    x, z, y = gx // 4, gx % 4, gy // 2
    if axis == "x":
        return [(((x + o) % 4) * 4 + z, gy) for o in (1, 2, 3)]
    if axis == "z":
        return [(x * 4 + (z + o) % 4, gy) for o in (1, 2, 3)]
    return [(gx, ((y + o) % 4) * 2 + core) for o in (1, 2, 3)]


def greet(core, others):
    barrier = pltpu.get_barrier_semaphore()
    devices = lines("x", core) + lines("y", core) + lines("z", core)
    devices = [device_of(other) for other in others] + devices
    for device in devices:
        pl.semaphore_signal(barrier, inc=1, device_id=device, device_id_type=MESH)
    return lambda: pl.semaphore_wait(barrier, len(devices))


def spread(axis, core, sem):
    for device in lines(axis, core):
        pl.semaphore_signal(sem, inc=1, device_id=device, device_id_type=MESH)


def features(slot, info_ref, own_sel, other_sel, member, own_ref, other_ref, chunk_ref):
    def blocks(at_four, carry):
        got = []
        for part in range(4):
            at = rows_at(at_four * 512 + part * 128, 128, 128)
            geo = info_ref[slot, :, at]
            sub = iota((8, 128), 0)
            norm = geo[0:1] ** 2 + geo[1:2] ** 2 + geo[2:3] ** 2 + geo[3:4]
            base = jnp.where(
                sub < 3, geo, jnp.where(sub == 3, norm, jnp.where(sub == 4, 1.0, 0.0))
            )
            high, middle, low = (p.astype(F32) for p in parts(base))
            leaf = geo[4:5] + float(LEAVES * slot)
            named = jnp.where(fiota((104, 128), 0) == leaf, 1.0, 0.0)
            got.append(jnp.concatenate([high, middle, low, named], axis=0).T.astype(BF16))
        table = jnp.concatenate(got, axis=0)
        at = rows_at(slot * ROWS + at_four * 512, 512, 512)
        other_ref[at, :] = times(table, other_sel).astype(BF16)
        chunk_ref[rows_at(slot * (ROWS // CHUNK) + at_four * 16, 16, 16), :] = times(member, table)
        if slot == 1:
            own_ref[rows_at(at_four * 512, 512, 512), :] = times(table, own_sel).astype(BF16)
        return carry

    lax.fori_loop(0, ROWS // 512, blocks, 0)


def chunk_lists(chunk_ref, adjacent, list_ref, plan_ref):
    named = hot(chunk_ref[...] > 0.5)
    per = BLOCK // CHUNK
    own = ROWS // CHUNK
    member = hot(iota((32, own), 1) // per == iota((32, own), 0))
    of_block = hot(times(member, named[own : 2 * own]) > 0.5)
    wanted = hot(times(of_block, adjacent) > 0.5)
    needed = hot(times(named, wanted, ((1,), (1,))) > 0.5)
    below = hot(iota((CHUNKS, CHUNKS), 1) <= iota((CHUNKS, CHUNKS), 0))
    upto = times(below, needed)
    spot = fiota((CHUNKS, LIST), 1)
    for b in range(BLOCKS):
        column = upto[:, b : b + 1]
        found = jnp.sum(jnp.where(column <= spot, 1.0, 0.0), axis=0, keepdims=True)
        list_ref[b : b + 1, :] = found.astype(jnp.int32)
    list_ref[BLOCKS : BLOCKS + 8, :] = jnp.full((8, LIST), CHUNKS, jnp.int32)
    spot = fiota((1, PLAN), 1)
    block, begun, end = (jnp.zeros((1, PLAN), F32) for _ in range(3))
    for b in range(BLOCKS):
        count = upto[CHUNKS - 1 : CHUNKS, b : b + 1]
        steps = jnp.floor((count + (STEP - 1)) / STEP)
        end = end + steps
        passed = end <= spot
        block = block + jnp.where(passed, 1.0, 0.0)
        begun = begun + jnp.where(passed, steps, 0.0)
    within = jnp.where(block < BLOCKS, (spot - begun) * STEP, 0.0)
    plan_ref[0:1, :] = block.astype(jnp.int32)
    plan_ref[1:2, :] = within.astype(jnp.int32)
    plan_ref[2:3, :] = end.astype(jnp.int32)


def arrive_kernel(
    dens_ref,
    geometry_ref,
    leaf_ref,
    from_ref,
    to_ref,
    near_ref,
    far_ref,
    offset_ref,
    table_ref,
    translation_ref,
    own_sel_ref,
    other_sel_ref,
    win_out,
    other_out,
    own_out,
    local_ref,
    list_ref,
    plan_ref,
    mate_to_ref,
    mate_ref,
    mate_from_ref,
    x2_ref,
    col_ref,
    wide_ref,
    send_ref,
    land_ref,
    moment_ref,
    sel_ref,
    adj_ref,
    chunk_ref,
    multi_ref,
    padded_ref,
    info_ref,
    infos_ref,
    mid_ref,
    spare_ref,
    other_ref,
    own_ref,
    trans_ref,
    wide_trans_ref,
    trans_part_ref,
    trans_sem,
    out_sem,
    order_send,
    order_recv,
    info_send,
    info_recv,
    mate_send,
    mate_recv,
    plane_sem,
    cube_sem,
    pack_send,
    pack_recv,
    halo_send,
    halo_recv,
    multi_send,
    multi_recv,
):
    me, my, core = place()
    left, right = (me + DEVS - 1) % DEVS, (me + 1) % DEVS
    mate = me + 1 - 2 * core
    turn = turns(my)
    all_here = greet(core, (left, right))

    info_ref[...] = jnp.zeros(info_ref.shape, F32)
    info_ref[0:4, :] = geometry_ref[...]
    info_ref[4:5, :] = leaf_ref[...].astype(F32)
    info_ref[5:6, :] = from_ref[...].astype(F32)
    info_ref[6:7, :] = to_ref[...].astype(F32)
    all_here()
    to_mate = remote(dens_ref, mate_ref, mate_send, mate_recv, device_of(mate))
    orders = [
        remote(src, dst, order_send.at[at], order_recv.at[at], device_of(mate))
        for at, (src, dst) in enumerate(((from_ref, mate_from_ref), (to_ref, mate_to_ref)))
    ]
    for copy in orders + [to_mate]:
        copy.start()
    infos_ref[1] = info_ref[...]
    info_copies = []
    for at, (device, slot) in enumerate(((right, 0), (left, 2))):
        copy = remote(
            info_ref, infos_ref.at[slot], info_send.at[at], info_recv.at[at], device_of(device)
        )
        copy.start()
        info_copies.append(copy)

    def gather_half(side, after):
        def one(step, carry):
            pair = (step + my // 8) % PAIRS
            chips = [CHIPS // 2 * upper + 8 * pair + j for upper in range(2) for j in range(8)]
            idx = jnp.concatenate(
                [col_ref[rows_at(PACK * chip + QUOTA * core, QUOTA, 8), :] for chip in chips],
                axis=0,
            )
            got = taken(idx, x2_ref)
            for at, chip in enumerate(chips):
                wide_ref[rows_at(PACK * chip + QUOTA * side, QUOTA, 8), :] = got[
                    QUOTA * at : QUOTA * (at + 1)
                ]
            after(step, pair)
            return carry

        lax.fori_loop(0, PAIRS, one, 0)

    def ship(step, pair):
        for upper in range(2):
            at = rows_at(8 * PACK * pair + HALF * upper, 8 * PACK, 128)
            send_ref[at, :] = wide_ref[at, :].astype(BF16)
        send_packs(step, pair, turn, my, core, send_ref, land_ref, pack_send, pack_recv)

    spread("y", core, plane_sem)
    to_columns(lambda at: info_ref[5:6, at], col_ref)
    side_by_side(dens_ref, x2_ref)
    gather_half(core, lambda step, pair: None)
    pl.semaphore_wait(plane_sem, 3)
    spread("z", core, cube_sem)
    for copy in orders:
        copy.wait_recv()
    to_columns(lambda at: mate_from_ref[0:1, at].astype(F32), col_ref)
    to_mate.wait_recv()
    side_by_side(mate_ref, x2_ref)
    pl.semaphore_wait(cube_sem, 3)
    gather_half(1 - core, ship)
    mine = rows_at(PACK * my, PACK, 16)
    land_ref[mine, :] = send_ref[mine, :]

    offsets = trans_ref.shape[0]
    fetched = [
        pltpu.make_async_copy(translation_ref.at[:, o], trans_ref.at[o], trans_sem.at[o])
        for o in range(offsets)
    ]
    for copy in fetched:
        copy.start()
    lane = iota((LEAVES, 128), 1)
    nears, fars = near_ref.shape[0], far_ref.shape[0]
    padded_ref[...] = jnp.zeros((128, 128), F32)
    padded_ref[0:nears, 0:LEAVES] = near_ref[...].astype(F32)
    base = ((me - 1) * LEAVES).astype(F32)
    code = offset_ref[...].astype(F32) * 128.0 + far_ref[...].astype(F32) - base
    padded_ref[16 : 16 + fars, 0:LEAVES] = code
    listed = padded_ref[...].T[:LEAVES].astype(jnp.int32)
    adjacent = jnp.zeros((LEAVES, 128), F32)
    for j in range(nears):
        adjacent = jnp.maximum(
            adjacent, jnp.where(listed[:, j : j + 1] + HOT == lane, 1.0, 0.0)
        )
    first = jnp.where(me == 0, OWN, HOT)
    end = jnp.where(me == DEVS - 1, OWN + LEAVES, HOT + 3 * LEAVES)
    adjacent = jnp.where((lane >= first) & (lane < end), adjacent, 0.0)
    adj_ref[...] = jnp.zeros((128, 128), F32)
    adj_ref[OWN : OWN + LEAVES, :] = adjacent
    sel_ref[...] = own_sel_ref[...]
    sel_ref[OWN : OWN + LEAVES, :] = jnp.where(
        (lane >= HOT) & (lane < HOT + 3 * LEAVES), (1.0 - adjacent) * FAR_AWAY, 0.0
    )
    own_sel, other_sel = sel_ref[...].astype(BF16), other_sel_ref[...].astype(BF16)
    member = hot(iota((16, 512), 1) // CHUNK == iota((16, 512), 0))
    for copy in info_copies:
        copy.wait_recv()
    for slot in range(3):
        features(
            slot, infos_ref, own_sel, other_sel, member, own_ref, other_ref, chunk_ref
        )
    spare = pl.ds(3 * ROWS, CHUNK)
    other_ref[spare, :] = hot(iota((CHUNK, 128), 1) == 120)
    spare_ref[...] = jnp.zeros((CHUNK, WIDTH), BF16)
    stored = [
        pltpu.make_async_copy(src, dst, out_sem.at[at])
        for at, (src, dst) in enumerate(
            ((other_ref, other_out), (own_ref, own_out), (spare_ref, win_out.at[spare]))
        )
    ]
    for copy in stored:
        copy.start()
    chunk_lists(chunk_ref, adj_ref[...].astype(BF16), list_ref, plan_ref)
    moment_ref[...] = jnp.zeros((128, 128), F32)
    moment_ref[:, : table_ref.shape[1]] = table_ref[...].astype(F32)
    moment = moment_ref[...].astype(BF16)
    to_columns(lambda at: info_ref[6:7, at], col_ref)
    in_leaf = jnp.concatenate(
        [
            hot(fiota((LEAVES, 128), 0) == info_ref[4:5, 128 * b : 128 * (b + 1)])
            for b in range(ROWS // 128)
        ],
        axis=1,
    )
    counted = []
    for o in range(offsets):
        count = jnp.zeros((LEAVES, 128), F32)
        for j in range(16, 16 + fars):
            count = count + jnp.where(listed[:, j : j + 1] == lane + o * 128, 1.0, 0.0)
        counted.append(count.astype(BF16))
    counted = jnp.concatenate(counted, axis=0)
    nm = trans_ref.shape[1]
    wide_trans_ref[...] = jnp.zeros(wide_trans_ref.shape, F32)
    for o in range(offsets):
        fetched[o].wait()
        wide_trans_ref[:nm, 128 * o : 128 * o + nm] = trans_ref[o]
    for o in range(offsets):
        at = slice(128 * o, 128 * (o + 1))
        for p, part in enumerate(parts(wide_trans_ref[:, at])):
            trans_part_ref[p, :, at] = part

    all_received(land_ref, pack_recv, pack_send, device_of(right))
    side_by_side(land_ref, x2_ref)

    def halo(start, count):
        src = mid_ref.at[rows_at(start, count, 512)]
        return [
            remote(
                src,
                win_out.at[rows_at(base + start, count, 512)],
                halo_send.at[at],
                halo_recv.at[at],
                device_of(device),
            )
            for at, (device, base) in enumerate(((right, 0), (left, 2 * ROWS)))
        ]

    def leaf_rows(b, carry):
        at = rows_at(b * 512, 512, 512)
        mid_ref[at, :] = taken(col_ref[at, :], x2_ref).astype(BF16)
        for copy in halo(b * 512, 512):
            copy.start()
        return carry

    lax.fori_loop(0, ROWS // 512, leaf_rows, 0)
    kept = pltpu.make_async_copy(mid_ref, win_out.at[pl.ds(ROWS, ROWS)], out_sem.at[3])
    kept.start()

    leaf_sum = times(in_leaf, mid_ref[...])
    multi = sum(times(p, moment) for p in parts(leaf_sum))
    multi_ref[1] = multi
    multi_ref[3] = jnp.zeros((LEAVES, 128), F32)
    multi_copies = []
    for at, (device, slot) in enumerate(((right, 0), (left, 2))):
        copy = remote(
            multi_ref.at[1],
            multi_ref.at[slot],
            multi_send.at[at],
            multi_recv.at[at],
            device_of(device),
        )
        copy.start()
        multi_copies.append(copy)
    for copy in multi_copies:
        copy.wait_recv()
    nearby = multi_ref[...].reshape(128, 128)
    grouped = sum(times(counted, p) for p in parts(nearby))
    grouped = jnp.concatenate(
        [grouped[LEAVES * o : LEAVES * (o + 1)] for o in range(offsets)], axis=1
    )
    grouped = jnp.concatenate(parts(grouped), axis=0)
    local = jnp.zeros((LEAVES, 128), F32)
    for p in range(3):
        kept_parts = (3 - p) * LEAVES
        got = times(grouped[:kept_parts], trans_part_ref[p], ((1,), (1,)))
        for at in range(0, kept_parts, LEAVES):
            local = local + got[at : at + LEAVES]
    far = sum(times(p, moment, ((1,), (1,))) for p in parts(local))
    for at, part in enumerate(parts(far / NAMED)):
        padded_ref[...] = jnp.zeros((128, 128), F32)
        padded_ref[OWN : OWN + LEAVES, :] = part.astype(F32)
        local_ref[at] = padded_ref[...].astype(BF16)

    all_sent(send_ref, land_ref, pack_send, pack_recv, device_of(right))
    for copy in halo(0, ROWS):
        copy.wait()
    for copy in multi_copies + info_copies + orders + [to_mate]:
        copy.wait_send()
    for copy in stored + [kept]:
        copy.wait()


def near_kernel(
    list_ref, plan_ref, own_ref, other_ref, win_ref, local_ref, block_ref, out_ref, sum_ref
):
    sum_ref[...] = jnp.zeros((ROWS, WIDTH), F32)

    def rows_of(at):
        return rows_at(jnp.minimum(plan_ref[0, at], BLOCKS - 1) * BLOCK, BLOCK, BLOCK)

    def potential(at):
        own = own_ref[rows_of(at), :]
        row, first = plan_ref[0, at], plan_ref[1, at]
        starts = [rows_at(list_ref[row, first + j] * CHUNK, CHUNK, CHUNK) for j in range(STEP)]
        other = jnp.concatenate([other_ref[start, :] for start in starts], axis=0)
        weight = lax.rsqrt(times(own, other, ((1,), (1,)))).astype(BF16)
        dens = jnp.concatenate([win_ref[start, :] for start in starts], axis=0)
        return times(weight, dens)

    def together(i, carry):
        found = [potential(i * ABREAST + j) for j in range(ABREAST)]
        for j in range(ABREAST):
            at = rows_of(i * ABREAST + j)
            sum_ref[at, :] = sum_ref[at, :] + found[j]
        return carry

    steps = plan_ref[2, 0]
    lax.fori_loop(0, (steps + ABREAST - 1) // ABREAST, together, 0)

    near_first = jnp.concatenate([block_ref[...], local_ref[0]], axis=0)
    rest = jnp.concatenate([local_ref[1], local_ref[2]], axis=0)

    def finish(b, carry):
        at = rows_at(b * 1024, 1024, 1024)
        near = sum_ref[at, :].astype(BF16)
        leaf = other_ref[rows_at(ROWS + b * 1024, 1024, 1024), :]
        total = times(jnp.concatenate([near, leaf], axis=1), near_first)
        total = total + times(jnp.concatenate([leaf, leaf], axis=1), rest)
        out_ref[at, :] = total.astype(BF16)
        return carry

    lax.fori_loop(0, ROWS // 1024, finish, 0)


def return_kernel(
    total_ref,
    from_ref,
    to_ref,
    mate_to_ref,
    out_ref,
    mate_ref,
    x2_ref,
    col_ref,
    mate_col_ref,
    wide_ref,
    send_ref,
    land_ref,
    mate_send,
    mate_recv,
    plane_sem,
    cube_sem,
    pack_send,
    pack_recv,
):
    me, my, core = place()
    mate = me + 1 - 2 * core
    turn = turns(my)
    all_here = greet(core, (mate,))
    all_here()
    to_mate = remote(total_ref, mate_ref, mate_send, mate_recv, device_of(mate))
    to_mate.start()
    spread("y", core, plane_sem)
    to_columns(lambda at: to_ref[0:1, at].astype(F32), col_ref)
    split_by_target(total_ref, col_ref, x2_ref)
    sub = jnp.concatenate([iota((QUOTA, 128), 0) + PACK * j for j in range(8)], axis=0)

    def scattered(row, order_of):
        pieces = []
        for b in range(ROWS // 128):
            order = order_of(pl.ds(128 * b, 128)).astype(F32)
            order = jnp.where(order >= HALF, order - HALF, order)
            pieces.append(hot(row == order))
        return times(jnp.concatenate(pieces, axis=1), x2_ref[...])

    def scatter_half(order_ref, side, after):
        def one(step, carry):
            pair = (step + my // 8) % PAIRS
            row = (sub + (8 * PACK * pair + QUOTA * core)).astype(F32)
            both = scattered(row, lambda at: order_ref[0:1, at])
            for upper in range(2):
                for j in range(8):
                    chip = CHIPS // 2 * upper + 8 * pair + j
                    wide_ref[rows_at(PACK * chip + QUOTA * side, QUOTA, 8), :] = both[
                        QUOTA * j : QUOTA * (j + 1), WIDTH * upper : WIDTH * (upper + 1)
                    ]
            after(step, pair)
            return carry

        lax.fori_loop(0, PAIRS, one, 0)

    def ship(step, pair):
        for upper in range(2):
            at = rows_at(8 * PACK * pair + HALF * upper, 8 * PACK, 128)
            send_ref[at, :] = wide_ref[at, :].astype(BF16)
        send_packs(step, pair, turn, my, core, send_ref, land_ref, pack_send, pack_recv)

    scatter_half(to_ref, core, lambda step, pair: None)
    to_columns(lambda at: mate_to_ref[0:1, at].astype(F32), mate_col_ref)
    pl.semaphore_wait(plane_sem, 3)
    spread("z", core, cube_sem)
    to_mate.wait_recv()
    split_by_target(mate_ref, mate_col_ref, x2_ref)
    pl.semaphore_wait(cube_sem, 3)
    scatter_half(mate_to_ref, 1 - core, ship)
    mine = rows_at(PACK * my, PACK, 16)
    land_ref[mine, :] = send_ref[mine, :]
    to_columns(lambda at: from_ref[0:1, at].astype(F32), col_ref)
    some = HALF // PAIRS
    for step in range(PAIRS):
        received(15 if step == 0 else 16, land_ref, pack_recv.at[step], pack_send, device_of(mate))
        pair = (my // 8 + PAIRS - step) % PAIRS
        spans = [rows_at(HALF * upper + some * pair, some, 128) for upper in range(2)]
        for at in spans:
            split_rows(land_ref[at, :], col_ref[at, :], x2_ref, at)
        x2 = jnp.concatenate([x2_ref[at, :] for at in spans], axis=0)
        orders = []
        for upper in range(2):
            for b in range(0, some, 128):
                at = rows_at(HALF * upper + some * pair + b, 128, 128)
                order = from_ref[0:1, at].astype(F32)
                orders.append(jnp.where(order >= HALF, order - HALF, order))

        def ordered(b, carry):
            row = fiota((256, 128), 0) + (b * 256).astype(F32)
            pick = jnp.concatenate([hot(row == order) for order in orders], axis=1)
            both = times(pick, x2)
            low, high = rows_at(b * 256, 256, 256), rows_at(HALF + b * 256, 256, 256)
            left, right = both[:, :WIDTH], both[:, WIDTH:]
            if step > 0:
                left, right = wide_ref[low, :] + left, wide_ref[high, :] + right
            if step < PAIRS - 1:
                wide_ref[low, :] = left
                wide_ref[high, :] = right
            else:
                out_ref[low, :] = left.astype(BF16)
                out_ref[high, :] = right.astype(BF16)
            return carry

        lax.fori_loop(0, HALF // 256, ordered, 0, unroll=2)
    all_sent(send_ref, land_ref, pack_send, pack_recv, device_of(mate))
    to_mate.wait_send()


def widen_kernel(x_ref, out_ref):
    out_ref[...] = x_ref[...].astype(F32)


def widened(x):
    blocks = 4
    spec = pl.BlockSpec((ROWS // blocks, WIDTH), lambda b: (b, 0))
    return pl.pallas_call(
        widen_kernel,
        grid=(blocks,),
        out_shape=shaped(ROWS, WIDTH, dtype=F32),
        in_specs=[spec],
        out_specs=spec,
    )(x)


def call(kernel, outs, scratch, inputs, smem=(), hbm=(), hbm_outs=(), collective=None):
    spaces = [
        pltpu.SMEM if at in smem else pl.ANY if at in hbm else pltpu.VMEM
        for at in range(len(inputs))
    ]
    params = dict(vmem_limit_bytes=VMEM)
    if collective is not None:
        params.update(collective_id=collective, has_side_effects=True)
    return pl.pallas_call(
        kernel,
        out_shape=outs,
        in_specs=[pl.BlockSpec(memory_space=space) for space in spaces],
        out_specs=[
            pl.BlockSpec(memory_space=pl.ANY if at in hbm_outs else pltpu.VMEM)
            for at in range(len(outs))
        ],
        scratch_shapes=scratch,
        compiler_params=pltpu.CompilerParams(**params),
    )(*inputs)


def shaped(*shape, dtype=BF16):
    return jax.ShapeDtypeStruct(shape, dtype)


def on_device(
    density,
    send_order,
    recv_order,
    geometry,
    pair_leaf,
    near_list,
    far_list,
    far_offset,
    moment_table,
    coulomb_block,
    translation,
):
    dma = pltpu.SemaphoreType.DMA
    vmem = lambda *shape, dtype=BF16: pltpu.VMEM(shape, dtype)
    offsets, nm = translation.shape[:2]
    own_sel, other_sel = (jnp.asarray(s) for s in selections())
    win, other, own, local, lists, plan, mate_to = call(
        arrive_kernel,
        (
            shaped(WINDOW, WIDTH),
            shaped(WINDOW, 128),
            shaped(ROWS, 128),
            shaped(3, 128, 128),
            shaped(BLOCKS + 8, LIST, dtype=jnp.int32),
            shaped(8, PLAN, dtype=jnp.int32),
            shaped(1, ROWS, dtype=jnp.int32),
        ),
        [
            vmem(ROWS, WIDTH),
            vmem(1, ROWS, dtype=jnp.int32),
            vmem(HALF, 2 * WIDTH),
            vmem(ROWS, 128, dtype=F32),
            vmem(ROWS, WIDTH, dtype=F32),
            vmem(ROWS, WIDTH),
            vmem(ROWS, WIDTH),
            vmem(128, 128, dtype=F32),
            vmem(128, 128, dtype=F32),
            vmem(128, 128, dtype=F32),
            vmem(CHUNKS, 128, dtype=F32),
            vmem(4, LEAVES, 128, dtype=F32),
            vmem(128, 128, dtype=F32),
            vmem(8, ROWS, dtype=F32),
            vmem(3, 8, ROWS, dtype=F32),
            vmem(ROWS, WIDTH),
            vmem(CHUNK, WIDTH),
            vmem(WINDOW, 128),
            vmem(ROWS, 128),
            vmem(offsets, nm, nm, dtype=F32),
            vmem(128, 128 * offsets, dtype=F32),
            vmem(3, 128, 128 * offsets),
            dma((offsets,)),
            dma((4,)),
            dma((2,)),
            dma((2,)),
            dma((2,)),
            dma((2,)),
            dma,
            dma,
            pltpu.SemaphoreType.REGULAR,
            pltpu.SemaphoreType.REGULAR,
            dma,
            dma((PAIRS,)),
            dma((2,)),
            dma((2,)),
            dma((2,)),
            dma((2,)),
        ],
        (
            density,
            geometry,
            pair_leaf,
            send_order,
            recv_order,
            near_list.T,
            far_list.T,
            far_offset.T,
            moment_table,
            translation.transpose(1, 0, 2),
            own_sel,
            other_sel,
        ),
        hbm=(9,),
        hbm_outs=(0, 1, 2),
        collective=0,
    )
    (total,) = call(
        near_kernel,
        (shaped(ROWS, WIDTH),),
        [vmem(ROWS, WIDTH, dtype=F32)],
        (lists, plan, own, other, win, local, coulomb_block),
        smem=(0, 1),
    )
    (coulomb,) = call(
        return_kernel,
        (shaped(ROWS, WIDTH),),
        [
            vmem(ROWS, WIDTH),
            vmem(ROWS, 2 * WIDTH),
            vmem(ROWS, 128, dtype=F32),
            vmem(ROWS, 128, dtype=F32),
            vmem(ROWS, WIDTH, dtype=F32),
            vmem(ROWS, WIDTH),
            vmem(ROWS, WIDTH),
            dma,
            dma,
            pltpu.SemaphoreType.REGULAR,
            pltpu.SemaphoreType.REGULAR,
            dma,
            dma((PAIRS,)),
        ],
        (total, send_order, recv_order, mate_to),
        collective=1,
    )
    return widened(coulomb)


def solution(mesh):
    rows = P(("gx", "gy"), None)
    placed = (rows, rows, rows, P(None, ("gx", "gy")), rows, rows, rows, rows, P(), P(), P())
    return jax.shard_map(
        on_device, mesh=mesh, in_specs=placed, out_specs=rows, check_vma=False
    )
```

```python
import functools

import jax
import jax.numpy as jnp
import numpy as np
from jax import lax
from jax.experimental import pallas as pl
from jax.experimental.pallas import tpu as pltpu
from jax.sharding import PartitionSpec as P

MESH = pl.DeviceIdType.MESH
F32, BF16 = jnp.float32, jnp.bfloat16
FAR_AWAY = 3e38
NAMED = 4.0
ROWS = 3072
WIDTH = 128
HALF = ROWS // 2
DEVS, CHIPS = 128, 64
QUOTA = 24
PAIRS = 4
PACK = 2 * QUOTA
LEAVES = 32
HOT = 24
OWN = HOT + LEAVES
CHUNK = 32
CHUNKS = 3 * ROWS // CHUNK
BLOCK = 128
BLOCKS = ROWS // BLOCK
STEP = 8
ABREAST = 32
LIST = 384
PLAN = 896
WINDOW = 3 * ROWS + CHUNK
VMEM = 26 * 1024 * 1024


def selections():
    own, other = np.zeros((128, 128), np.float32), np.zeros((128, 128), np.float32)
    for axis in range(3):
        for at, (a, b) in enumerate(((0, 0), (0, 8), (8, 0), (0, 16), (16, 0), (8, 8))):
            own[a + axis, 6 * axis + at] = 1.0
            other[b + axis, 6 * axis + at] = -2.0
    for at in range(3):
        own[8 * at + 3, 18 + at] = 1.0
        other[4, 18 + at] = 1.0
        own[4, 21 + at] = 1.0
        other[8 * at + 3, 21 + at] = 1.0
    own[4, 120] = FAR_AWAY
    for at in range(HOT, HOT + 3 * LEAVES):
        other[at, at] = NAMED
    return own, other


def iota(shape, axis):
    return lax.broadcasted_iota(jnp.int32, shape, axis)


def fiota(shape, axis):
    return iota(shape, axis).astype(F32)


def hot(condition):
    return jnp.where(condition, 1.0, 0.0).astype(BF16)


def times(a, b, dims=((1,), (0,))):
    return lax.dot_general(a, b, (dims, ((), ())), preferred_element_type=F32)


def parts(x):
    high = x.astype(BF16)
    rest = x - high.astype(F32)
    middle = rest.astype(BF16)
    low = (rest - middle.astype(F32)).astype(BF16)
    return high, middle, low


def remote(src, dst, send, recv, device):
    return pltpu.make_async_remote_copy(
        src_ref=src,
        dst_ref=dst,
        send_sem=send,
        recv_sem=recv,
        device_id=device,
        device_id_type=MESH,
    )


def place():
    gx, gy = lax.axis_index("gx"), lax.axis_index("gy")
    me = gx * 8 + gy
    return me, me // 2, gy % 2


def device_of(d):
    return (d // 8, d % 8)


def of_chip(chip, core):
    return (chip // 4, (chip % 4) * 2 + core)


def rows_at(start, count, step):
    return pl.ds(pl.multiple_of(start, step), count)


def to_columns(row_of, col_ref):
    def block(b, carry):
        at = rows_at(b * 128, 128, 128)
        col_ref[at, :] = jnp.broadcast_to(row_of(at), (128, 128)).T
        return carry

    lax.fori_loop(0, ROWS // 128, block, 0, unroll=8)


def side_by_side(x_ref, x2_ref):
    x2_ref[:, :WIDTH] = x_ref[:HALF]
    x2_ref[:, WIDTH:] = x_ref[HALF:]


def taken(idx, x2_ref):
    upper = idx >= HALF
    low = jnp.where(upper, idx - HALF, idx)
    lane = fiota(idx.shape, 1)
    pick = jnp.concatenate([hot(low == lane + 128.0 * b) for b in range(HALF // 128)], axis=1)
    both = times(pick, x2_ref[...])
    return jnp.where(upper, both[:, WIDTH:], both[:, :WIDTH])


def split_rows(x, target, x2_ref, at):
    x, upper = x.astype(F32), target >= HALF
    x2_ref[at, :WIDTH] = jnp.where(upper, 0.0, x).astype(BF16)
    x2_ref[at, WIDTH:] = jnp.where(upper, x, 0.0).astype(BF16)


def split_by_target(x_ref, col_ref, x2_ref):
    def block(b, carry):
        at = rows_at(b * 256, 256, 256)
        split_rows(x_ref[at, :], col_ref[at, :], x2_ref, at)
        return carry

    lax.fori_loop(0, ROWS // 256, block, 0)


def turns(my):
    order = [(my + j) % 8 for j in range(8)]
    return [(m, m // 4, (m % 4) * 2) for m in order]


def send_packs(step, pair, turn, my, core, send_ref, land_ref, send_sem, recv_sem):
    for upper in range(2):
        for m, along, across in turn:
            chip = CHIPS // 2 * upper + 8 * pair + m

            @pl.when(chip != my)
            def _():
                remote(
                    send_ref.at[rows_at(PACK * chip, PACK, 16)],
                    land_ref.at[rows_at(PACK * my, PACK, 16)],
                    send_sem,
                    recv_sem.at[step],
                    (8 * upper + 2 * pair + along, across + core),
                ).start()


def received(packs, land_ref, recv_sem, send_sem, device):
    got = pl.ds(0, PACK * packs)
    remote(land_ref.at[got], land_ref.at[got], send_sem, recv_sem, device).wait_recv()


def all_received(land_ref, recv_sem, send_sem, device):
    for step in range(PAIRS):
        packs = 15 if step == 0 else 16
        received(packs, land_ref, recv_sem.at[step], send_sem, device)


def all_sent(send_ref, land_ref, send_sem, recv_sem, device):
    got = pl.ds(0, PACK * (CHIPS - 1))
    remote(send_ref.at[got], land_ref.at[got], send_sem, recv_sem.at[0], device).wait_send()


def lines(axis, core):
    gx, gy = lax.axis_index("gx"), lax.axis_index("gy")
    x, z, y = gx // 4, gx % 4, gy // 2
    if axis == "x":
        return [(((x + o) % 4) * 4 + z, gy) for o in (1, 2, 3)]
    if axis == "z":
        return [(x * 4 + (z + o) % 4, gy) for o in (1, 2, 3)]
    return [(gx, ((y + o) % 4) * 2 + core) for o in (1, 2, 3)]


def greet(core, others):
    barrier = pltpu.get_barrier_semaphore()
    devices = lines("x", core) + lines("y", core) + lines("z", core)
    devices = [device_of(other) for other in others] + devices
    for device in devices:
        pl.semaphore_signal(barrier, inc=1, device_id=device, device_id_type=MESH)
    return lambda: pl.semaphore_wait(barrier, len(devices))


def spread(axis, core, sem):
    for device in lines(axis, core):
        pl.semaphore_signal(sem, inc=1, device_id=device, device_id_type=MESH)


def features(slot, info_ref, own_sel, other_sel, member, own_ref, other_ref, chunk_ref):
    def blocks(at_four, carry):
        got = []
        for part in range(4):
            at = rows_at(at_four * 512 + part * 128, 128, 128)
            geo = info_ref[slot, :, at]
            sub = iota((8, 128), 0)
            norm = geo[0:1] ** 2 + geo[1:2] ** 2 + geo[2:3] ** 2 + geo[3:4]
            base = jnp.where(
                sub < 3, geo, jnp.where(sub == 3, norm, jnp.where(sub == 4, 1.0, 0.0))
            )
            high, middle, low = (p.astype(F32) for p in parts(base))
            leaf = geo[4:5] + float(LEAVES * slot)
            named = jnp.where(fiota((104, 128), 0) == leaf, 1.0, 0.0)
            got.append(jnp.concatenate([high, middle, low, named], axis=0).T.astype(BF16))
        table = jnp.concatenate(got, axis=0)
        at = rows_at(slot * ROWS + at_four * 512, 512, 512)
        other_ref[at, :] = times(table, other_sel).astype(BF16)
        chunk_ref[rows_at(slot * (ROWS // CHUNK) + at_four * 16, 16, 16), :] = times(member, table)
        if slot == 1:
            own_ref[rows_at(at_four * 512, 512, 512), :] = times(table, own_sel).astype(BF16)
        return carry

    lax.fori_loop(0, ROWS // 512, blocks, 0)


def chunk_lists(chunk_ref, adjacent, list_ref, plan_ref):
    named = hot(chunk_ref[...] > 0.5)
    per = BLOCK // CHUNK
    own = ROWS // CHUNK
    member = hot(iota((32, own), 1) // per == iota((32, own), 0))
    of_block = hot(times(member, named[own : 2 * own]) > 0.5)
    wanted = hot(times(of_block, adjacent) > 0.5)
    needed = hot(times(named, wanted, ((1,), (1,))) > 0.5)
    below = hot(iota((CHUNKS, CHUNKS), 1) <= iota((CHUNKS, CHUNKS), 0))
    upto = times(below, needed)
    spot = fiota((CHUNKS, LIST), 1)
    for b in range(BLOCKS):
        column = upto[:, b : b + 1]
        found = jnp.sum(jnp.where(column <= spot, 1.0, 0.0), axis=0, keepdims=True)
        list_ref[b : b + 1, :] = found.astype(jnp.int32)
    list_ref[BLOCKS : BLOCKS + 8, :] = jnp.full((8, LIST), CHUNKS, jnp.int32)
    spot = fiota((1, PLAN), 1)
    block, begun, end = (jnp.zeros((1, PLAN), F32) for _ in range(3))
    for b in range(BLOCKS):
        count = upto[CHUNKS - 1 : CHUNKS, b : b + 1]
        steps = jnp.floor((count + (STEP - 1)) / STEP)
        end = end + steps
        passed = end <= spot
        block = block + jnp.where(passed, 1.0, 0.0)
        begun = begun + jnp.where(passed, steps, 0.0)
    within = jnp.where(block < BLOCKS, (spot - begun) * STEP, 0.0)
    plan_ref[0:1, :] = block.astype(jnp.int32)
    plan_ref[1:2, :] = within.astype(jnp.int32)
    plan_ref[2:3, :] = end.astype(jnp.int32)


def arrive_kernel(
    dens_ref,
    geometry_ref,
    leaf_ref,
    from_ref,
    to_ref,
    near_ref,
    far_ref,
    offset_ref,
    table_ref,
    translation_ref,
    own_sel_ref,
    other_sel_ref,
    win_out,
    other_out,
    own_out,
    local_ref,
    list_ref,
    plan_ref,
    mate_to_ref,
    mate_ref,
    mate_from_ref,
    x2_ref,
    col_ref,
    wide_ref,
    send_ref,
    land_ref,
    moment_ref,
    sel_ref,
    adj_ref,
    chunk_ref,
    multi_ref,
    padded_ref,
    info_ref,
    infos_ref,
    mid_ref,
    spare_ref,
    other_ref,
    own_ref,
    trans_ref,
    wide_trans_ref,
    trans_part_ref,
    trans_sem,
    out_sem,
    order_send,
    order_recv,
    info_send,
    info_recv,
    mate_send,
    mate_recv,
    plane_sem,
    cube_sem,
    pack_send,
    pack_recv,
    halo_send,
    halo_recv,
    multi_send,
    multi_recv,
):
    me, my, core = place()
    left, right = (me + DEVS - 1) % DEVS, (me + 1) % DEVS
    mate = me + 1 - 2 * core
    turn = turns(my)
    all_here = greet(core, (left, right))

    info_ref[...] = jnp.zeros(info_ref.shape, F32)
    info_ref[0:4, :] = geometry_ref[...]
    info_ref[4:5, :] = leaf_ref[...].astype(F32)
    info_ref[5:6, :] = from_ref[...].astype(F32)
    info_ref[6:7, :] = to_ref[...].astype(F32)
    all_here()
    to_mate = remote(dens_ref, mate_ref, mate_send, mate_recv, device_of(mate))
    orders = [
        remote(src, dst, order_send.at[at], order_recv.at[at], device_of(mate))
        for at, (src, dst) in enumerate(((from_ref, mate_from_ref), (to_ref, mate_to_ref)))
    ]
    for copy in orders + [to_mate]:
        copy.start()
    infos_ref[1] = info_ref[...]
    info_copies = []
    for at, (device, slot) in enumerate(((right, 0), (left, 2))):
        copy = remote(
            info_ref, infos_ref.at[slot], info_send.at[at], info_recv.at[at], device_of(device)
        )
        copy.start()
        info_copies.append(copy)

    def gather_half(side, after):
        def one(step, carry):
            pair = (step + my // 8) % PAIRS
            chips = [CHIPS // 2 * upper + 8 * pair + j for upper in range(2) for j in range(8)]
            idx = jnp.concatenate(
                [col_ref[rows_at(PACK * chip + QUOTA * core, QUOTA, 8), :] for chip in chips],
                axis=0,
            )
            got = taken(idx, x2_ref)
            for at, chip in enumerate(chips):
                wide_ref[rows_at(PACK * chip + QUOTA * side, QUOTA, 8), :] = got[
                    QUOTA * at : QUOTA * (at + 1)
                ]
            after(step, pair)
            return carry

        lax.fori_loop(0, PAIRS, one, 0)

    def ship(step, pair):
        for upper in range(2):
            at = rows_at(8 * PACK * pair + HALF * upper, 8 * PACK, 128)
            send_ref[at, :] = wide_ref[at, :].astype(BF16)
        send_packs(step, pair, turn, my, core, send_ref, land_ref, pack_send, pack_recv)

    spread("y", core, plane_sem)
    to_columns(lambda at: info_ref[5:6, at], col_ref)
    side_by_side(dens_ref, x2_ref)
    gather_half(core, lambda step, pair: None)
    pl.semaphore_wait(plane_sem, 3)
    spread("z", core, cube_sem)
    for copy in orders:
        copy.wait_recv()
    to_columns(lambda at: mate_from_ref[0:1, at].astype(F32), col_ref)
    to_mate.wait_recv()
    side_by_side(mate_ref, x2_ref)

    def ship_later(step, pair):
        @pl.when(step == 0)
        def _():
            pl.semaphore_wait(cube_sem, 3)

        ship(step, pair)

    gather_half(1 - core, ship_later)
    mine = rows_at(PACK * my, PACK, 16)
    land_ref[mine, :] = send_ref[mine, :]

    offsets = trans_ref.shape[0]
    fetched = [
        pltpu.make_async_copy(translation_ref.at[:, o], trans_ref.at[o], trans_sem.at[o])
        for o in range(offsets)
    ]
    for copy in fetched:
        copy.start()
    lane = iota((LEAVES, 128), 1)
    nears, fars = near_ref.shape[0], far_ref.shape[0]
    padded_ref[...] = jnp.zeros((128, 128), F32)
    padded_ref[0:nears, 0:LEAVES] = near_ref[...].astype(F32)
    base = ((me - 1) * LEAVES).astype(F32)
    code = offset_ref[...].astype(F32) * 128.0 + far_ref[...].astype(F32) - base
    padded_ref[16 : 16 + fars, 0:LEAVES] = code
    listed = padded_ref[...].T[:LEAVES].astype(jnp.int32)
    adjacent = jnp.zeros((LEAVES, 128), F32)
    for j in range(nears):
        adjacent = jnp.maximum(
            adjacent, jnp.where(listed[:, j : j + 1] + HOT == lane, 1.0, 0.0)
        )
    first = jnp.where(me == 0, OWN, HOT)
    end = jnp.where(me == DEVS - 1, OWN + LEAVES, HOT + 3 * LEAVES)
    adjacent = jnp.where((lane >= first) & (lane < end), adjacent, 0.0)
    adj_ref[...] = jnp.zeros((128, 128), F32)
    adj_ref[OWN : OWN + LEAVES, :] = adjacent
    sel_ref[...] = own_sel_ref[...]
    sel_ref[OWN : OWN + LEAVES, :] = jnp.where(
        (lane >= HOT) & (lane < HOT + 3 * LEAVES), (1.0 - adjacent) * FAR_AWAY, 0.0
    )
    own_sel, other_sel = sel_ref[...].astype(BF16), other_sel_ref[...].astype(BF16)
    member = hot(iota((16, 512), 1) // CHUNK == iota((16, 512), 0))
    for copy in info_copies:
        copy.wait_recv()
    for slot in range(3):
        features(
            slot, infos_ref, own_sel, other_sel, member, own_ref, other_ref, chunk_ref
        )
    spare = pl.ds(3 * ROWS, CHUNK)
    other_ref[spare, :] = hot(iota((CHUNK, 128), 1) == 120)
    spare_ref[...] = jnp.zeros((CHUNK, WIDTH), BF16)
    stored = [
        pltpu.make_async_copy(src, dst, out_sem.at[at])
        for at, (src, dst) in enumerate(
            ((other_ref, other_out), (own_ref, own_out), (spare_ref, win_out.at[spare]))
        )
    ]
    for copy in stored:
        copy.start()
    chunk_lists(chunk_ref, adj_ref[...].astype(BF16), list_ref, plan_ref)
    moment_ref[...] = jnp.zeros((128, 128), F32)
    moment_ref[:, : table_ref.shape[1]] = table_ref[...].astype(F32)
    moment = moment_ref[...].astype(BF16)
    to_columns(lambda at: info_ref[6:7, at], col_ref)
    in_leaf = jnp.concatenate(
        [
            hot(fiota((LEAVES, 128), 0) == info_ref[4:5, 128 * b : 128 * (b + 1)])
            for b in range(ROWS // 128)
        ],
        axis=1,
    )
    counted = []
    for o in range(offsets):
        count = jnp.zeros((LEAVES, 128), F32)
        for j in range(16, 16 + fars):
            count = count + jnp.where(listed[:, j : j + 1] == lane + o * 128, 1.0, 0.0)
        counted.append(count.astype(BF16))
    counted = jnp.concatenate(counted, axis=0)
    nm = trans_ref.shape[1]
    wide_trans_ref[...] = jnp.zeros(wide_trans_ref.shape, F32)
    for o in range(offsets):
        fetched[o].wait()
        wide_trans_ref[:nm, 128 * o : 128 * o + nm] = trans_ref[o]
    for o in range(offsets):
        at = slice(128 * o, 128 * (o + 1))
        for p, part in enumerate(parts(wide_trans_ref[:, at])):
            trans_part_ref[p, :, at] = part

    all_received(land_ref, pack_recv, pack_send, device_of(right))
    side_by_side(land_ref, x2_ref)

    def halo(start, count):
        src = mid_ref.at[rows_at(start, count, 512)]
        return [
            remote(
                src,
                win_out.at[rows_at(base + start, count, 512)],
                halo_send.at[at],
                halo_recv.at[at],
                device_of(device),
            )
            for at, (device, base) in enumerate(((right, 0), (left, 2 * ROWS)))
        ]

    def leaf_rows(b, carry):
        at = rows_at(b * 512, 512, 512)
        mid_ref[at, :] = taken(col_ref[at, :], x2_ref).astype(BF16)
        for copy in halo(b * 512, 512):
            copy.start()
        return carry

    lax.fori_loop(0, ROWS // 512, leaf_rows, 0)
    kept = pltpu.make_async_copy(mid_ref, win_out.at[pl.ds(ROWS, ROWS)], out_sem.at[3])
    kept.start()

    leaf_sum = times(in_leaf, mid_ref[...])
    multi = sum(times(p, moment) for p in parts(leaf_sum))
    multi_ref[1] = multi
    multi_ref[3] = jnp.zeros((LEAVES, 128), F32)
    multi_copies = []
    for at, (device, slot) in enumerate(((right, 0), (left, 2))):
        copy = remote(
            multi_ref.at[1],
            multi_ref.at[slot],
            multi_send.at[at],
            multi_recv.at[at],
            device_of(device),
        )
        copy.start()
        multi_copies.append(copy)
    for copy in multi_copies:
        copy.wait_recv()
    nearby = multi_ref[...].reshape(128, 128)
    grouped = sum(times(counted, p) for p in parts(nearby))
    grouped = jnp.concatenate(
        [grouped[LEAVES * o : LEAVES * (o + 1)] for o in range(offsets)], axis=1
    )
    grouped = jnp.concatenate(parts(grouped), axis=0)
    local = jnp.zeros((LEAVES, 128), F32)
    for p in range(3):
        kept_parts = (3 - p) * LEAVES
        got = times(grouped[:kept_parts], trans_part_ref[p], ((1,), (1,)))
        for at in range(0, kept_parts, LEAVES):
            local = local + got[at : at + LEAVES]
    far = sum(times(p, moment, ((1,), (1,))) for p in parts(local))
    for at, part in enumerate(parts(far / NAMED)):
        padded_ref[...] = jnp.zeros((128, 128), F32)
        padded_ref[OWN : OWN + LEAVES, :] = part.astype(F32)
        local_ref[at] = padded_ref[...].astype(BF16)

    all_sent(send_ref, land_ref, pack_send, pack_recv, device_of(right))
    for copy in halo(0, ROWS):
        copy.wait()
    for copy in multi_copies + info_copies + orders + [to_mate]:
        copy.wait_send()
    for copy in stored + [kept]:
        copy.wait()


def near_kernel(
    list_ref, plan_ref, own_ref, other_ref, win_ref, local_ref, block_ref, out_ref, sum_ref
):
    sum_ref[...] = jnp.zeros((ROWS, WIDTH), F32)

    def rows_of(at):
        return rows_at(jnp.minimum(plan_ref[0, at], BLOCKS - 1) * BLOCK, BLOCK, BLOCK)

    def potential(at):
        own = own_ref[rows_of(at), :]
        row, first = plan_ref[0, at], plan_ref[1, at]
        starts = [rows_at(list_ref[row, first + j] * CHUNK, CHUNK, CHUNK) for j in range(STEP)]
        other = jnp.concatenate([other_ref[start, :] for start in starts], axis=0)
        weight = lax.rsqrt(times(own, other, ((1,), (1,)))).astype(BF16)
        dens = jnp.concatenate([win_ref[start, :] for start in starts], axis=0)
        return times(weight, dens)

    def together(i, carry):
        found = [potential(i * ABREAST + j) for j in range(ABREAST)]
        for j in range(ABREAST):
            at = rows_of(i * ABREAST + j)
            sum_ref[at, :] = sum_ref[at, :] + found[j]
        return carry

    steps = plan_ref[2, 0]
    lax.fori_loop(0, (steps + ABREAST - 1) // ABREAST, together, 0)

    near_first = jnp.concatenate([block_ref[...], local_ref[0]], axis=0)
    rest = jnp.concatenate([local_ref[1], local_ref[2]], axis=0)

    def finish(b, carry):
        at = rows_at(b * 1024, 1024, 1024)
        near = sum_ref[at, :].astype(BF16)
        leaf = other_ref[rows_at(ROWS + b * 1024, 1024, 1024), :]
        total = times(jnp.concatenate([near, leaf], axis=1), near_first)
        total = total + times(jnp.concatenate([leaf, leaf], axis=1), rest)
        out_ref[at, :] = total.astype(BF16)
        return carry

    lax.fori_loop(0, ROWS // 1024, finish, 0)


def return_kernel(
    total_ref,
    from_ref,
    to_ref,
    mate_to_ref,
    out_ref,
    mate_ref,
    x2_ref,
    col_ref,
    mate_col_ref,
    wide_ref,
    send_ref,
    land_ref,
    mate_send,
    mate_recv,
    plane_sem,
    cube_sem,
    pack_send,
    pack_recv,
):
    me, my, core = place()
    mate = me + 1 - 2 * core
    turn = turns(my)
    all_here = greet(core, (mate,))
    to_columns(lambda at: to_ref[0:1, at].astype(F32), col_ref)
    to_columns(lambda at: mate_to_ref[0:1, at].astype(F32), mate_col_ref)
    split_by_target(total_ref, col_ref, x2_ref)
    all_here()
    to_mate = remote(total_ref, mate_ref, mate_send, mate_recv, device_of(mate))
    to_mate.start()
    spread("y", core, plane_sem)
    sub = jnp.concatenate([iota((QUOTA, 128), 0) + PACK * j for j in range(8)], axis=0)

    def scattered(row, order_of):
        pieces = []
        for b in range(ROWS // 128):
            order = order_of(pl.ds(128 * b, 128)).astype(F32)
            order = jnp.where(order >= HALF, order - HALF, order)
            pieces.append(hot(row == order))
        return times(jnp.concatenate(pieces, axis=1), x2_ref[...])

    def scatter_half(order_ref, side, after):
        def one(step, carry):
            pair = (step + my // 8) % PAIRS
            row = (sub + (8 * PACK * pair + QUOTA * core)).astype(F32)
            both = scattered(row, lambda at: order_ref[0:1, at])
            for upper in range(2):
                for j in range(8):
                    chip = CHIPS // 2 * upper + 8 * pair + j
                    wide_ref[rows_at(PACK * chip + QUOTA * side, QUOTA, 8), :] = both[
                        QUOTA * j : QUOTA * (j + 1), WIDTH * upper : WIDTH * (upper + 1)
                    ]
            after(step, pair)
            return carry

        lax.fori_loop(0, PAIRS, one, 0)

    def ship(step, pair):
        for upper in range(2):
            at = rows_at(8 * PACK * pair + HALF * upper, 8 * PACK, 128)
            send_ref[at, :] = wide_ref[at, :].astype(BF16)
        send_packs(step, pair, turn, my, core, send_ref, land_ref, pack_send, pack_recv)

    scatter_half(to_ref, core, lambda step, pair: None)
    pl.semaphore_wait(plane_sem, 3)
    spread("z", core, cube_sem)
    to_mate.wait_recv()
    split_by_target(mate_ref, mate_col_ref, x2_ref)

    def ship_later(step, pair):
        @pl.when(step == 0)
        def _():
            pl.semaphore_wait(cube_sem, 3)

        ship(step, pair)

    scatter_half(mate_to_ref, 1 - core, ship_later)
    mine = rows_at(PACK * my, PACK, 16)
    land_ref[mine, :] = send_ref[mine, :]
    to_columns(lambda at: from_ref[0:1, at].astype(F32), col_ref)
    some = HALF // PAIRS
    for step in range(PAIRS):
        received(15 if step == 0 else 16, land_ref, pack_recv.at[step], pack_send, device_of(mate))
        pair = (my // 8 + PAIRS - step) % PAIRS
        spans = [rows_at(HALF * upper + some * pair, some, 128) for upper in range(2)]
        for at in spans:
            split_rows(land_ref[at, :], col_ref[at, :], x2_ref, at)
        x2 = jnp.concatenate([x2_ref[at, :] for at in spans], axis=0)
        orders = []
        for upper in range(2):
            for b in range(0, some, 128):
                at = rows_at(HALF * upper + some * pair + b, 128, 128)
                order = from_ref[0:1, at].astype(F32)
                orders.append(jnp.where(order >= HALF, order - HALF, order))

        def ordered(b, carry):
            row = fiota((256, 128), 0) + (b * 256).astype(F32)
            pick = jnp.concatenate([hot(row == order) for order in orders], axis=1)
            both = times(pick, x2)
            low, high = rows_at(b * 256, 256, 256), rows_at(HALF + b * 256, 256, 256)
            left, right = both[:, :WIDTH], both[:, WIDTH:]
            if step > 0:
                left, right = wide_ref[low, :] + left, wide_ref[high, :] + right
            if step < PAIRS - 1:
                wide_ref[low, :] = left
                wide_ref[high, :] = right
            else:
                out_ref[low, :] = left.astype(BF16)
                out_ref[high, :] = right.astype(BF16)
            return carry

        lax.fori_loop(0, HALF // 256, ordered, 0, unroll=2)
    all_sent(send_ref, land_ref, pack_send, pack_recv, device_of(mate))
    to_mate.wait_send()


def call(kernel, outs, scratch, inputs, smem=(), hbm=(), hbm_outs=(), collective=None, limit=VMEM):
    spaces = [
        pltpu.SMEM if at in smem else pl.ANY if at in hbm else pltpu.VMEM
        for at in range(len(inputs))
    ]
    params = dict(vmem_limit_bytes=limit)
    if collective is not None:
        params.update(collective_id=collective, has_side_effects=True)
    return pl.pallas_call(
        kernel,
        out_shape=outs,
        in_specs=[pl.BlockSpec(memory_space=space) for space in spaces],
        out_specs=[
            pl.BlockSpec(memory_space=pl.ANY if at in hbm_outs else pltpu.VMEM)
            for at in range(len(outs))
        ],
        scratch_shapes=scratch,
        compiler_params=pltpu.CompilerParams(**params),
    )(*inputs)


def shaped(*shape, dtype=BF16):
    return jax.ShapeDtypeStruct(shape, dtype)


def on_device(
    density,
    send_order,
    recv_order,
    geometry,
    pair_leaf,
    near_list,
    far_list,
    far_offset,
    moment_table,
    coulomb_block,
    translation,
):
    dma = pltpu.SemaphoreType.DMA
    vmem = lambda *shape, dtype=BF16: pltpu.VMEM(shape, dtype)
    offsets, nm = translation.shape[:2]
    own_sel, other_sel = (jnp.asarray(s) for s in selections())
    win, other, own, local, lists, plan, mate_to = call(
        arrive_kernel,
        (
            shaped(WINDOW, WIDTH),
            shaped(WINDOW, 128),
            shaped(ROWS, 128),
            shaped(3, 128, 128),
            shaped(BLOCKS + 8, LIST, dtype=jnp.int32),
            shaped(8, PLAN, dtype=jnp.int32),
            shaped(1, ROWS, dtype=jnp.int32),
        ),
        [
            vmem(ROWS, WIDTH),
            vmem(1, ROWS, dtype=jnp.int32),
            vmem(HALF, 2 * WIDTH),
            vmem(ROWS, 128, dtype=F32),
            vmem(ROWS, WIDTH, dtype=F32),
            vmem(ROWS, WIDTH),
            vmem(ROWS, WIDTH),
            vmem(128, 128, dtype=F32),
            vmem(128, 128, dtype=F32),
            vmem(128, 128, dtype=F32),
            vmem(CHUNKS, 128, dtype=F32),
            vmem(4, LEAVES, 128, dtype=F32),
            vmem(128, 128, dtype=F32),
            vmem(8, ROWS, dtype=F32),
            vmem(3, 8, ROWS, dtype=F32),
            vmem(ROWS, WIDTH),
            vmem(CHUNK, WIDTH),
            vmem(WINDOW, 128),
            vmem(ROWS, 128),
            vmem(offsets, nm, nm, dtype=F32),
            vmem(128, 128 * offsets, dtype=F32),
            vmem(3, 128, 128 * offsets),
            dma((offsets,)),
            dma((4,)),
            dma((2,)),
            dma((2,)),
            dma((2,)),
            dma((2,)),
            dma,
            dma,
            pltpu.SemaphoreType.REGULAR,
            pltpu.SemaphoreType.REGULAR,
            dma,
            dma((PAIRS,)),
            dma((2,)),
            dma((2,)),
            dma((2,)),
            dma((2,)),
        ],
        (
            density,
            geometry,
            pair_leaf,
            send_order,
            recv_order,
            near_list.T,
            far_list.T,
            far_offset.T,
            moment_table,
            translation.transpose(1, 0, 2),
            own_sel,
            other_sel,
        ),
        hbm=(9,),
        hbm_outs=(0, 1, 2),
        collective=0,
        limit=60 * 1024 * 1024,
    )
    (total,) = call(
        near_kernel,
        (shaped(ROWS, WIDTH),),
        [vmem(ROWS, WIDTH, dtype=F32)],
        (lists, plan, own, other, win, local, coulomb_block),
        smem=(0, 1),
        limit=60 * 1024 * 1024,
    )
    (coulomb,) = call(
        return_kernel,
        (shaped(ROWS, WIDTH),),
        [
            vmem(ROWS, WIDTH),
            vmem(ROWS, 2 * WIDTH),
            vmem(ROWS, 128, dtype=F32),
            vmem(ROWS, 128, dtype=F32),
            vmem(ROWS, WIDTH, dtype=F32),
            vmem(ROWS, WIDTH),
            vmem(ROWS, WIDTH),
            dma,
            dma,
            pltpu.SemaphoreType.REGULAR,
            pltpu.SemaphoreType.REGULAR,
            dma,
            dma((PAIRS,)),
        ],
        (total, send_order, recv_order, mate_to),
        collective=1,
        limit=26 * 1024 * 1024,
    )
    return coulomb.astype(F32)


def solution(mesh):
    rows = P(("gx", "gy"), None)
    placed = (rows, rows, rows, P(None, ("gx", "gy")), rows, rows, rows, rows, P(), P(), P())
    return jax.shard_map(
        on_device, mesh=mesh, in_specs=placed, out_specs=rows, check_vma=False
    )
```
